128 devices in a mesh: dp: 128 (over x, z, y, core).
Axes of the slice: x: 4, y: 4, z: 4, core: 2. Of those that a mesh axis runs over, the one named last changes fastest.
Arguments:
- queries: bfloat16 [16384, 768], P('dp'), may hold values from -2 to 2
- documents: bfloat16 [16384, 768], P('dp'), may hold values from -2 to 2
- positives: int32 [16384], P('dp'), may hold values from 0 to 16383, each once
Outputs:
- loss: float32 [], replicated
- grad_queries: float32 [16384, 768], P('dp')
- grad_documents: float32 [16384, 768], P('dp')
The draws below stay inside these ranges and needn't reach their ends.
Inputs may be any that keep to these rules, and one draw needn't show every extreme that they name: `positives`: every document is the positive of exactly one query.
All inputs are finite; a program needn't handle non-finite values.
Results may differ from the reference program's by a relative error of at most 0.0004.
The reference program's roundings to bfloat16 on the way (of `qb` and `weights`) count: a program that leaves them out, or rounds other values in their place, can miss the bound.
Values may be sent and summed in bfloat16 or wider, within the bound.
No kernel may reach another device: no remote copies, remote signals or barrier semaphores. Data moves between devices by JAX's collectives and lax.ppermute only.
A program may use at most 192 MiB of HBM per device.

```python
import math
import jax
import jax.numpy as jnp
from jax import lax

D = 768
QUERIES = 16384
DOCS = 16384


def row_scales(key, count):
    return jnp.exp(jax.random.uniform(key, (count, 1), jnp.float32, math.log(0.3), math.log(3.0)))


def draw_queries(key, part):
    key = jax.random.fold_in(key, 11)
    key_scale, key_body = jax.random.split(key)
    scales = row_scales(key_scale, QUERIES)
    values = jnp.clip(jax.random.normal(key_body, (QUERIES, D), jnp.float32), -4.0, 4.0)
    return (scales * values / math.sqrt(D)).astype(jnp.bfloat16)


def draw_documents(key, part):
    key = jax.random.fold_in(key, 23)
    key_scale, key_body = jax.random.split(key)
    scales = row_scales(key_scale, DOCS)
    values = jnp.clip(jax.random.normal(key_body, (DOCS, D), jnp.float32), -4.0, 4.0)
    return (scales * values / math.sqrt(D)).astype(jnp.bfloat16)


def setup_inputs(seed: int = 0) -> dict:
    key_of = jax.random.split(jax.random.key(seed), 4)
    queries = draw_queries(jax.random.fold_in(key_of[3], 71), 0)
    documents = draw_documents(jax.random.fold_in(key_of[3], 71), 0)
    positives = jax.random.permutation(key_of[2], QUERIES).astype(jnp.int32)
    return {"queries": queries, "documents": documents, "positives": positives}


def normalize(values):
    wide = values.astype(jnp.float32)
    length = jnp.sqrt(lax.optimization_barrier(jnp.sum(wide * wide, axis=1, keepdims=True)) + 1e-06)
    return (wide / length, length)

def reference(queries, documents, positives):
    qn, qnorm = normalize(queries)
    dn, dnorm = normalize(documents)
    qb = qn.astype(jnp.bfloat16)
    db = dn.astype(jnp.bfloat16)
    block = math.gcd(QUERIES, 512)
    qblocks = qb.reshape(QUERIES // block, block, D)
    pblocks = positives.reshape(QUERIES // block, block)
    columns = jnp.arange(DOCS, dtype=jnp.int32)

    def per_block(carry, item):
        loss_sum, grad_docs = carry
        rows, picks = item
        scores = 20.0 * jnp.dot(rows, db.T, preferred_element_type=jnp.float32)
        lse = 20.0 + jnp.log(lax.optimization_barrier(jnp.sum(jnp.exp(scores - 20.0), axis=1)))
        hit = picks[:, None] == columns[None, :]
        positive_score = lax.optimization_barrier(jnp.sum(jnp.where(hit, scores, jnp.float32(0.0)), axis=1))
        weights = (jnp.exp(scores - lse[:, None]) - hit.astype(jnp.float32)).astype(jnp.bfloat16)
        grad_rows = 20.0 * jnp.dot(weights, db, preferred_element_type=jnp.float32)
        grad_docs = grad_docs + 20.0 * jnp.dot(weights.T, rows, preferred_element_type=jnp.float32)
        return ((loss_sum + jnp.sum(lse - positive_score), grad_docs), grad_rows)
    start = (jnp.zeros((), jnp.float32), jnp.zeros((DOCS, D), jnp.float32))
    (loss_sum, gd), stacked = lax.scan(per_block, start, (qblocks, pblocks))
    gq = stacked.reshape(QUERIES, D)
    grad_queries = (gq - lax.optimization_barrier(jnp.sum(gq * qn, axis=1, keepdims=True)) * qn) / qnorm
    grad_documents = (gd - lax.optimization_barrier(jnp.sum(gd * dn, axis=1, keepdims=True)) * dn) / dnorm
    return (loss_sum / QUERIES, grad_queries, grad_documents)
```

```python
import functools

import jax
import jax.numpy as jnp
from jax import lax
from jax.experimental import pallas as pl
from jax.experimental.pallas import tpu as pltpu
from jax.sharding import PartitionSpec as P

PAIRS_A = ((0, 1), (2, 3))
PAIRS_B = ((0, 3), (1, 2))
CUBE = 8
CORES = 2
PAD = 16
LOG2E = 1.4426950408889634


def device_index(x, z, y, core):
    return ((x * 4 + z) * 4 + y) * CORES + core


def cubes(pairs, core):
    return [
        [device_index(x, z, y, core) for x in px for z in pz for y in py]
        for px in pairs
        for pz in pairs
        for py in pairs
    ]


GROUPS_OWN = cubes(PAIRS_A, 0) + cubes(PAIRS_B, 1)
GROUPS_SUMS = cubes(PAIRS_A, 0) + cubes(PAIRS_A, 1)
SWAP = [(i, i ^ 1) for i in range(128)]


def normalize(values):
    wide = values.astype(jnp.float32)
    length = jnp.sqrt(jnp.sum(wide * wide, axis=1, keepdims=True) + 1e-06)
    return (wide / length, length)


def row_ids(block):
    rows = block.shape[0] - PAD
    tail = block[rows:, :rows].astype(jnp.float32)
    return tail[0:1, :] * 128.0 + tail[1:2, :]


def down_rows(row):
    return jnp.transpose(jnp.broadcast_to(row, (128, row.shape[1])))


def tile_kernel(role_ref, x_ref, y_ref, e_ref, stats_ref, cols_ref):
    step = pl.program_id(0)
    role = role_ref[0]
    block = e_ref.shape[0]
    x = x_ref[0, :block, :]

    @pl.when(step == 0)
    def _():
        cols_ref[...] = jnp.zeros_like(cols_ref)

    ids = down_rows(row_ids(x_ref[0]))
    partial = jnp.zeros((block, 128), jnp.float32)
    for k in range(CUBE):
        dots = lax.dot_general(
            x, y_ref[k, :block, :], (((1,), (1,)), ((), ())), preferred_element_type=jnp.float32
        )
        e = jnp.exp2(dots * (20.0 * LOG2E) - 20.0 * LOG2E)
        e_ref[:, k * block : (k + 1) * block] = e
        for h in range(block // 128):
            partial = partial + e[:, h * 128 : (h + 1) * 128]
        yids = row_ids(y_ref[k])
        columns = slice(k * block, (k + 1) * block)
        cols_ref[0:8, columns] += jnp.sum(e.reshape(block // 8, 8, block), axis=0)
        hit = jnp.where(jnp.concatenate([ids] * (block // 128), axis=1) == yids, dots, 0.0)
        cols_ref[8:16, columns] += jnp.sum(hit.reshape(block // 8, 8, block), axis=0)

    per = block // 128

    @pl.when(role == 0)
    def _():
        row = jnp.sum(jnp.transpose(partial), axis=0, keepdims=True)
        for h in range(per):
            piece = row[:, h * 128 : (h + 1) * 128]
            for g in range(CUBE):
                stats_ref[g, pl.ds(step * per + h, 1), :] = piece
                stats_ref[g, pl.ds(CUBE * per + step * per + h, 1), :] = jnp.zeros_like(piece)

    @pl.when((role == 1) & (step == CUBE - 1))
    def _():
        for part in range(2):
            col = jnp.sum(cols_ref[part * 8 : part * 8 + 8, :], axis=0, keepdims=True)
            for i in range(CUBE * per):
                for g in range(CUBE):
                    stats_ref[g, pl.ds(part * CUBE * per + i, 1), :] = col[:, i * 128 : (i + 1) * 128]


def grad_kernel(role_ref, e_ref, x_ref, y_ref, stats_ref, out_ref, y_all, scale_ref):
    step = pl.program_id(0)
    role = role_ref[0]
    block = e_ref.shape[0]
    per = block // 128
    half = CUBE * per

    @pl.when(step == 0)
    def _():
        for k in range(CUBE):
            y_all[k * block : (k + 1) * block, :] = y_ref[k, :block, :]
        total = jnp.sum(stats_ref[:, :half, :], axis=0)
        scale_ref[0:half, :] = 1.0 / total
        lse = 20.0 + jnp.log(total)
        picked = 20.0 * jnp.sum(stats_ref[:, half:, :], axis=0)
        scale_ref[half : half + 1, :] = jnp.broadcast_to(jnp.sum(lse - picked), (1, 128))

    ids = row_ids(x_ref[0])
    scale = [jnp.where(role == 0, scale_ref[pl.ds(step * per + h, 1), :], 1.0) for h in range(per)]
    scale = down_rows(jnp.concatenate(scale, axis=1))
    ids = down_rows(ids)
    ids = jnp.concatenate([ids] * per, axis=1)
    scale = jnp.concatenate([scale] * per, axis=1)
    weights = []
    for k in range(CUBE):
        col = [jnp.where(role == 1, scale_ref[k * per + h : k * per + h + 1, :], 1.0) for h in range(per)]
        col = jnp.concatenate(col, axis=1)
        hit = jnp.where(ids == row_ids(y_ref[k]), 1.0, 0.0)
        p = e_ref[:, k * block : (k + 1) * block] * scale * col
        weights.append((p - hit).astype(jnp.bfloat16))
    weights = jnp.concatenate(weights, axis=1)
    out_ref[0, :block, :] = 20.0 * jnp.dot(weights, y_all[...], preferred_element_type=jnp.float32)
    out_ref[0, block:, :] = jnp.broadcast_to(scale_ref[half : half + 1, 0:1], (8, out_ref.shape[2]))


def local(queries, documents, positives):
    me = lax.axis_index("dp")
    role = lax.rem(me, CORES)
    rows, width = queries.shape
    block = CORES * rows
    qn, qnorm = normalize(queries)
    dn, dnorm = normalize(documents)
    qb = qn.astype(jnp.bfloat16)
    db = dn.astype(jnp.bfloat16)
    first = role == 0

    def with_ids(values, ids):
        tail = jnp.stack([ids // 128, ids % 128]).astype(jnp.bfloat16)
        tail = jnp.pad(tail, ((0, PAD // 2 - 2), (0, width - rows)))
        return jnp.concatenate([values, tail], axis=0)

    mine = me * rows + lax.iota(jnp.int32, rows)
    qside = with_ids(qb, positives)
    dside = with_ids(db, mine)
    keep = jnp.where(first, qside, dside)
    come = lax.ppermute(jnp.where(first, dside, qside), "dp", SWAP)
    low = jnp.where(first, keep, come)
    high = jnp.where(first, come, keep)
    ids = jnp.concatenate([low[rows : rows + 2, :rows], high[rows : rows + 2, :rows]], axis=1)
    ids = jnp.pad(ids, ((0, PAD - 2), (0, width - block)))
    own = jnp.concatenate([low[:rows], high[:rows], ids], axis=0)
    sent = jnp.broadcast_to(own[None], (CUBE, block + PAD, width))
    x = lax.all_to_all(sent, "dp", 0, 0, axis_index_groups=GROUPS_OWN, tiled=True)
    y = lax.ppermute(x, "dp", SWAP)

    side = CUBE * block
    roles = role.reshape((1,)).astype(jnp.int32)
    per_block = pl.BlockSpec((1, block + PAD, width), lambda i: (i, 0, 0))
    whole = pl.BlockSpec((CUBE, block + PAD, width), lambda i: (0, 0, 0))
    tile_rows = pl.BlockSpec((block, side), lambda i: (i, 0))
    nstats = 2 * side // 128
    stats_spec = pl.BlockSpec((CUBE, nstats, 128), lambda i: (0, 0, 0))
    params = pltpu.CompilerParams(
        dimension_semantics=("arbitrary",), vmem_limit_bytes=56 * 1024 * 1024
    )
    e, stats = pl.pallas_call(
        tile_kernel,
        grid=(CUBE,),
        in_specs=[pl.BlockSpec(memory_space=pltpu.SMEM), per_block, whole],
        out_specs=[tile_rows, stats_spec],
        out_shape=[
            jax.ShapeDtypeStruct((side, side), jnp.float32),
            jax.ShapeDtypeStruct((CUBE, nstats, 128), jnp.float32),
        ],
        scratch_shapes=[pltpu.VMEM((16, side), jnp.float32)],
        compiler_params=params,
        name="tile",
    )(roles, x, y)
    stats = lax.all_to_all(stats, "dp", 0, 0, axis_index_groups=GROUPS_SUMS, tiled=True)
    parts = pl.pallas_call(
        grad_kernel,
        grid=(CUBE,),
        in_specs=[pl.BlockSpec(memory_space=pltpu.SMEM), tile_rows, per_block, whole, stats_spec],
        out_specs=pl.BlockSpec((1, block + 8, width), lambda i: (i, 0, 0)),
        out_shape=jax.ShapeDtypeStruct((CUBE, block + 8, width), jnp.float32),
        scratch_shapes=[
            pltpu.VMEM((side, width), jnp.bfloat16),
            pltpu.VMEM((side // 128 + 8, 128), jnp.float32),
        ],
        compiler_params=params,
        name="grad",
    )(roles, e, x, y, stats)
    parts = lax.all_to_all(parts, "dp", 0, 0, axis_index_groups=GROUPS_OWN, tiled=True)
    total = jnp.sum(parts, axis=0)
    low, high, tail = total[:rows], total[rows:block], total[block:]
    come = lax.ppermute(jnp.concatenate([jnp.where(first, high, low), tail], axis=0), "dp", SWAP)
    kept = jnp.where(first, low, high)
    gq = jnp.where(first, kept, come[:rows])
    gd = jnp.where(first, come[:rows], kept)
    loss = jnp.where(first, come[rows, 0], tail[0, 0]) / (rows * lax.axis_size("dp"))
    grad_queries = (gq - jnp.sum(gq * qn, axis=1, keepdims=True) * qn) / qnorm
    grad_documents = (gd - jnp.sum(gd * dn, axis=1, keepdims=True) * dn) / dnorm
    return (loss, grad_queries, grad_documents)


def solution(mesh):
    placed = (P("dp", None), P("dp", None), P("dp"))
    return jax.shard_map(
        local,
        mesh=mesh,
        in_specs=placed,
        out_specs=(P(), P("dp", None), P("dp", None)),
        check_vma=False,
    )
```

```python
import functools

import jax
import jax.numpy as jnp
from jax import lax
from jax.experimental import pallas as pl
from jax.experimental.pallas import tpu as pltpu
from jax.sharding import PartitionSpec as P

PAIRS_A = ((0, 1), (2, 3))
PAIRS_B = ((0, 3), (1, 2))
CUBE = 8
CORES = 2
ROWS = 128
BLOCK = CORES * ROWS
SIDE = CUBE * BLOCK
WIDTH = 768
PAD = 16
LOSS = 8
PER = BLOCK // 128
HALF = CUBE * PER
LOG2E = 1.4426950408889634
F32 = jnp.float32
BF16 = jnp.bfloat16


def device_index(x, z, y, core):
    return ((x * 4 + z) * 4 + y) * CORES + core


def partners(bits):
    moves = []
    for x in range(4):
        for z in range(4):
            for y in range(4):
                for core in range(CORES):
                    flip = (lambda v: v ^ 1) if core == 0 else (lambda v: 3 - v)
                    to = [flip(v) if bits & bit else v for v, bit in ((x, 4), (z, 2), (y, 1))]
                    moves.append((device_index(x, z, y, core), device_index(*to, core)))
    return moves


def a_cubes():
    return [
        [device_index(x, z, y, core) for x in px for z in pz for y in py]
        for core in range(CORES)
        for px in PAIRS_A
        for pz in PAIRS_A
        for py in PAIRS_A
    ]


SWAP = [(i, i ^ 1) for i in range(128)]
SUM_GROUPS = a_cubes()


def send(value, bits):
    return lax.ppermute(value, "dp", partners(bits))


def swap(value):
    return lax.ppermute(value, "dp", SWAP)


def near(value):
    return pltpu.with_memory_space_constraint(value, pltpu.VMEM)


def call(kernel, name, out_shape, *args, scratch=(), limit=8):
    return pl.pallas_call(
        kernel,
        name=name,
        out_shape=out_shape,
        scratch_shapes=scratch,
        compiler_params=pltpu.CompilerParams(vmem_limit_bytes=limit * 1024 * 1024),
    )(*args)


def role_of():
    return lax.axis_index("dp") & 1


def unit_rows(values):
    wide = values.astype(F32)
    length = jnp.sqrt(jnp.sum(wide * wide, axis=1, keepdims=True) + 1e-06)
    return wide / length, length


def row_ids(block_ref):
    tail = block_ref[BLOCK:, :BLOCK].astype(F32)
    return tail[0:1, :] * 128.0 + tail[1:2, :]


def down_rows(row, width):
    wide = jnp.transpose(jnp.broadcast_to(row, (128, row.shape[1])))
    return jnp.concatenate([wide] * (width // 128), axis=1)


def pre_kernel(q_ref, d_ref, p_ref, keep_ref, send_ref):
    me = lax.axis_index("dp")
    role = role_of()

    def fill(ref, values, ids):
        ref[:ROWS, :] = unit_rows(values)[0].astype(BF16)
        high = ids >> 7
        rows = lax.broadcasted_iota(jnp.int32, (PAD, ROWS), 0)
        tail = jnp.where(rows == 0, high, jnp.where(rows == 1, ids - high * 128, 0))
        ref[ROWS:, :] = jnp.zeros((PAD, WIDTH), BF16)
        ref[ROWS:, :ROWS] = tail.astype(F32).astype(BF16)

    mine = me * ROWS + lax.broadcasted_iota(jnp.int32, (1, ROWS), 1)

    @pl.when(role == 0)
    def _():
        fill(keep_ref, q_ref[...], p_ref[...])
        fill(send_ref, d_ref[...], mine)

    @pl.when(role == 1)
    def _():
        fill(keep_ref, d_ref[...], mine)
        fill(send_ref, q_ref[...], p_ref[...])


def join_kernel(keep_ref, come_ref, own_ref):
    def fill(low, high):
        own_ref[:ROWS, :] = low[:ROWS, :]
        own_ref[ROWS:BLOCK, :] = high[:ROWS, :]
        own_ref[BLOCK:, :] = jnp.zeros((PAD, WIDTH), BF16)
        own_ref[BLOCK:, :ROWS] = low[ROWS:, :ROWS]
        own_ref[BLOCK:, ROWS:BLOCK] = high[ROWS:, :ROWS]

    role = role_of()

    @pl.when(role == 0)
    def _():
        fill(keep_ref, come_ref)

    @pl.when(role == 1)
    def _():
        fill(come_ref, keep_ref)


def place_in_cube():
    me = lax.axis_index("dp")
    return ((me >> 5) & 1) * 4 + ((me >> 3) & 1) * 2 + ((me >> 1) & 1)


def tile_kernel(*refs):
    x, y, (e_ref, stats_ref, cols_ref) = refs[:CUBE], refs[CUBE : 2 * CUBE], refs[2 * CUBE :]
    place = place_in_cube()

    def block_of(i, k):
        dots = lax.dot_general(
            x[i][:BLOCK, :], y[k][:BLOCK, :], (((1,), (1,)), ((), ())), preferred_element_type=F32
        )
        e = jnp.exp2(dots * (20.0 * LOG2E) - 20.0 * LOG2E)
        e_ref[i * BLOCK : (i + 1) * BLOCK, k * BLOCK : (k + 1) * BLOCK] = e
        return dots, e

    def put(part, k, row):
        at = (place ^ k) * PER + part * HALF
        for h in range(PER):
            for g in range(CUBE):
                stats_ref[g, pl.ds(at + h, 1), :] = row[:, h * 128 : (h + 1) * 128]

    @pl.when(role_of() == 0)
    def _():
        for i in range(CUBE):
            partial = None
            for k in range(CUBE):
                _, e = block_of(i, k)
                for h in range(PER):
                    piece = e[:, h * 128 : (h + 1) * 128]
                    partial = piece if partial is None else partial + piece
            put(0, i, jnp.sum(jnp.transpose(partial), axis=0, keepdims=True))
            put(1, i, jnp.zeros((1, BLOCK), F32))

    @pl.when(role_of() == 1)
    def _():
        for i in range(CUBE):
            ids = down_rows(row_ids(x[i]), BLOCK)
            for k in range(CUBE):
                dots, e = block_of(i, k)
                hit = jnp.where(ids == row_ids(y[k]), dots, 0.0)
                columns = slice(k * BLOCK, (k + 1) * BLOCK)
                for part, value in enumerate((e, hit)):
                    value = jnp.sum(value.reshape(BLOCK // 8, 8, BLOCK), axis=0)
                    at = slice(part * 8, part * 8 + 8)
                    cols_ref[at, columns] = value if i == 0 else cols_ref[at, columns] + value
        for k in range(CUBE):
            for part in range(2):
                column = cols_ref[part * 8 : part * 8 + 8, k * BLOCK : (k + 1) * BLOCK]
                put(part, k, jnp.sum(column, axis=0, keepdims=True))


def grad_kernel(chosen, *refs):
    e_ref, stats_ref = refs[:2]
    y = refs[2 : 2 + CUBE]
    xs = refs[2 + CUBE : 2 + CUBE + len(chosen)]
    outs = refs[2 + CUBE + len(chosen) : -1]
    scale_ref = refs[-1]
    place = place_in_cube()
    total = jnp.sum(stats_ref[:, :HALF, :], axis=0)
    scale_ref[0:HALF, :] = 1.0 / total
    lse = 20.0 + jnp.log(total)
    picked = 20.0 * jnp.sum(stats_ref[:, HALF:, :], axis=0)
    loss = jnp.sum(lse - picked)

    def scale_of(k):
        at = (place ^ k) * PER
        return jnp.concatenate([scale_ref[pl.ds(at + h, 1), :] for h in range(PER)], axis=1)

    def body(role):
        for n, i in enumerate(chosen):
            ids = down_rows(row_ids(xs[n]), BLOCK)
            scale = down_rows(scale_of(i), BLOCK) if role == 0 else None
            acc = None
            for k in range(CUBE):
                if role == 1:
                    scale = scale_of(k)
                e = e_ref[i * BLOCK : (i + 1) * BLOCK, k * BLOCK : (k + 1) * BLOCK]
                weights = (e * scale - jnp.where(ids == row_ids(y[k]), 1.0, 0.0)).astype(BF16)
                part = jnp.dot(weights, y[k][:BLOCK, :], preferred_element_type=F32)
                acc = part if acc is None else acc + part
            outs[n][:BLOCK, :] = 20.0 * acc
            outs[n][BLOCK:, :] = jnp.full((LOSS, WIDTH), loss, F32)

    pl.when(role_of() == 0)(functools.partial(body, 0))
    pl.when(role_of() == 1)(functools.partial(body, 1))


def split_kernel(a_ref, b_ref, c_ref, d_ref, e_ref, keep_ref, send_ref):
    def total(at):
        return a_ref[at, :] + b_ref[at, :] + c_ref[at, :] + d_ref[at, :] + e_ref[at, :]

    low, high, tail = slice(0, ROWS), slice(ROWS, BLOCK), slice(BLOCK, BLOCK + LOSS)
    role = role_of()
    keep_ref[ROWS:, :] = total(tail)
    send_ref[ROWS:, :] = total(tail)

    @pl.when(role == 0)
    def _():
        keep_ref[:ROWS, :] = total(low)
        send_ref[:ROWS, :] = total(high)

    @pl.when(role == 1)
    def _():
        keep_ref[:ROWS, :] = total(high)
        send_ref[:ROWS, :] = total(low)


def post_kernel(q_ref, d_ref, keep_ref, come_ref, loss_ref, gq_ref, gd_ref):
    def project(out_ref, grad, values):
        unit, length = unit_rows(values)
        out_ref[...] = (grad - jnp.sum(grad * unit, axis=1, keepdims=True) * unit) / length

    def fill(gq, gd):
        project(gq_ref, gq[:ROWS, :], q_ref[...])
        project(gd_ref, gd[:ROWS, :], d_ref[...])
        loss_ref[...] = gd[ROWS : ROWS + 1, 0:1] * (1.0 / 16384)

    role = role_of()

    @pl.when(role == 0)
    def _():
        fill(keep_ref, come_ref)

    @pl.when(role == 1)
    def _():
        fill(come_ref, keep_ref)


def local(queries, documents, positives):
    piece = pltpu.VMEM((ROWS + PAD, WIDTH), BF16)
    keep, give = call(
        pre_kernel, "pre", [piece, piece], queries, documents, positives.reshape(1, ROWS)
    )
    come = swap(give)
    own = call(join_kernel, "join", pltpu.VMEM((BLOCK + PAD, WIDTH), BF16), near(keep), near(come))
    x = [own] + [None] * 7
    for bits in (4, 2, 1, 7):
        x[bits] = send(own, bits)
    y = [None] * 8
    for bits in (0, 4, 2, 1):
        y[bits] = swap(x[bits])
    x[6] = send(x[2], 4)
    x[3] = send(x[1], 2)
    x[5] = send(x[4], 1)
    for bits in (7, 6, 3, 5):
        y[bits] = swap(x[bits])
    x = [near(v) for v in x]
    y = [near(v) for v in y]

    e, stats = call(
        tile_kernel,
        "tile",
        [pltpu.VMEM((SIDE, SIDE), F32), pltpu.VMEM((CUBE, 2 * HALF, 128), F32)],
        *x,
        *y,
        scratch=[pltpu.VMEM((16, SIDE), F32)],
    )
    stats = lax.all_to_all(stats, "dp", 0, 0, axis_index_groups=SUM_GROUPS, tiled=True)

    def grads(chosen, name):
        return call(
            functools.partial(grad_kernel, chosen),
            name,
            [pltpu.VMEM((BLOCK + LOSS, WIDTH), F32)] * len(chosen),
            near(e),
            near(stats),
            *y,
            *[x[i] for i in chosen],
            scratch=[pltpu.VMEM((HALF, 128), F32)],
        )

    g6, g3, g5, g7 = grads((6, 3, 5, 7), "grad_far")
    r6, r3, r5, r7 = send(g6, 4), send(g3, 2), send(g5, 1), send(g7, 7)
    g4, g2, g1, g0 = grads((4, 2, 1, 0), "grad_near")
    r4 = send(g4 + r5, 4)
    r2 = send(g2 + r6, 2)
    r1 = send(g1 + r3, 1)
    part = pltpu.VMEM((ROWS + LOSS, WIDTH), F32)
    keep, give = call(
        split_kernel, "split", [part, part], *[near(v) for v in (g0, r4, r2, r1, r7)]
    )
    come = swap(give)
    loss, gq, gd = call(
        post_kernel,
        "post",
        [
            jax.ShapeDtypeStruct((1, 1), F32),
            jax.ShapeDtypeStruct((ROWS, WIDTH), F32),
            jax.ShapeDtypeStruct((ROWS, WIDTH), F32),
        ],
        queries,
        documents,
        near(keep),
        near(come),
    )
    return (loss.reshape(()), gq, gd)


def solution(mesh):
    placed = (P("dp", None), P("dp", None), P("dp"))
    return jax.shard_map(
        local,
        mesh=mesh,
        in_specs=placed,
        out_specs=(P(), P("dp", None), P("dp", None)),
        check_vma=False,
    )
```

```python
import functools

import jax
import jax.numpy as jnp
from jax import lax
from jax.experimental import pallas as pl
from jax.experimental.pallas import tpu as pltpu
from jax.sharding import PartitionSpec as P

PAIRS_A = ((0, 1), (2, 3))
PAIRS_B = ((0, 3), (1, 2))
CUBE = 8
CORES = 2
ROWS = 128
BLOCK = CORES * ROWS
SIDE = CUBE * BLOCK
WIDTH = 768
PAD = 16
LOSS = 8
PER = BLOCK // 128
HALF = CUBE * PER
LOG2E = 1.4426950408889634
FULL = 32760.0
NEAR = (0, 4, 2, 1)
FAR = (6, 3, 5, 7)
F32 = jnp.float32
BF16 = jnp.bfloat16


def device_index(x, z, y, core):
    return ((x * 4 + z) * 4 + y) * CORES + core


def partners(bits):
    moves = []
    for x in range(4):
        for z in range(4):
            for y in range(4):
                for core in range(CORES):
                    flip = (lambda v: v ^ 1) if core == 0 else (lambda v: 3 - v)
                    to = [flip(v) if bits & bit else v for v, bit in ((x, 4), (z, 2), (y, 1))]
                    moves.append((device_index(x, z, y, core), device_index(*to, core)))
    return moves


def a_cubes():
    return [
        [device_index(x, z, y, core) for x in px for z in pz for y in py]
        for core in range(CORES)
        for px in PAIRS_A
        for pz in PAIRS_A
        for py in PAIRS_A
    ]


SWAP = [(i, i ^ 1) for i in range(128)]
SUM_GROUPS = a_cubes()


def send(value, bits):
    return lax.ppermute(value, "dp", partners(bits))


def swap(value):
    return lax.ppermute(value, "dp", SWAP)


def near(value):
    return pltpu.with_memory_space_constraint(value, pltpu.VMEM)


def call(kernel, name, out_shape, *args, scratch=(), limit=8):
    return pl.pallas_call(
        kernel,
        name=name,
        out_shape=out_shape,
        scratch_shapes=scratch,
        compiler_params=pltpu.CompilerParams(vmem_limit_bytes=limit * 1024 * 1024),
    )(*args)


def role_of():
    return lax.axis_index("dp") & 1


def unit_rows(values):
    wide = values.astype(F32)
    length = jnp.sqrt(jnp.sum(wide * wide, axis=1, keepdims=True) + 1e-06)
    return wide / length, length


def row_ids(block_ref):
    tail = block_ref[BLOCK:, :BLOCK].astype(F32)
    return tail[0:1, :] * 128.0 + tail[1:2, :]


def down_rows(row, width):
    wide = jnp.transpose(jnp.broadcast_to(row, (128, row.shape[1])))
    return jnp.concatenate([wide] * (width // 128), axis=1)


def pre_kernel(q_hbm, d_hbm, p_hbm, keep_ref, send_ref, q_ref, d_ref, p_ref, sems):
    copies = [
        pltpu.make_async_copy(src, dst, sems.at[n])
        for n, (src, dst) in enumerate(((q_hbm, q_ref), (d_hbm, d_ref), (p_hbm, p_ref)))
    ]
    for copy in copies:
        copy.start()
    me = lax.axis_index("dp")
    role = role_of()
    for copy in copies:
        copy.wait()

    def fill(ref, values, ids):
        ref[:ROWS, :] = unit_rows(values)[0].astype(BF16)
        high = ids >> 7
        rows = lax.broadcasted_iota(jnp.int32, (PAD, ROWS), 0)
        tail = jnp.where(rows == 0, high, jnp.where(rows == 1, ids - high * 128, 0))
        ref[ROWS:, :] = jnp.zeros((PAD, WIDTH), BF16)
        ref[ROWS:, :ROWS] = tail.astype(F32).astype(BF16)

    mine = me * ROWS + lax.broadcasted_iota(jnp.int32, (1, ROWS), 1)

    @pl.when(role == 0)
    def _():
        fill(keep_ref, q_ref[...], p_ref[...])
        fill(send_ref, d_ref[...], mine)

    @pl.when(role == 1)
    def _():
        fill(keep_ref, d_ref[...], mine)
        fill(send_ref, q_ref[...], p_ref[...])


def join_kernel(keep_ref, come_ref, own_ref):
    def fill(low, high):
        own_ref[:ROWS, :] = low[:ROWS, :]
        own_ref[ROWS:BLOCK, :] = high[:ROWS, :]
        own_ref[BLOCK:, :] = jnp.zeros((PAD, WIDTH), BF16)
        own_ref[BLOCK:, :ROWS] = low[ROWS:, :ROWS]
        own_ref[BLOCK:, ROWS:BLOCK] = high[ROWS:, :ROWS]

    role = role_of()

    @pl.when(role == 0)
    def _():
        fill(keep_ref, come_ref)

    @pl.when(role == 1)
    def _():
        fill(come_ref, keep_ref)


def place_in_cube():
    me = lax.axis_index("dp")
    return ((me >> 5) & 1) * 4 + ((me >> 3) & 1) * 2 + ((me >> 1) & 1)


def tile_kernel(rows, columns, last, *refs):
    x, refs = refs[: len(rows)], refs[len(rows) :]
    y, refs = refs[: len(columns)], refs[len(columns) :]
    if last:
        before, (e_ref, stats_ref, rowsum_ref, colsum_ref) = refs[:4], refs[4:]
    else:
        e_ref, rowsum_ref, colsum_ref = refs
    place = place_in_cube()

    def block_of(i, k):
        dots = lax.dot_general(
            x[i][:BLOCK, :], y[k][:BLOCK, :], (((1,), (1,)), ((), ())), preferred_element_type=F32
        )
        e = jnp.exp2(dots * (20.0 * LOG2E) - 20.0 * LOG2E)
        e_ref[i * BLOCK : (i + 1) * BLOCK, k * BLOCK : (k + 1) * BLOCK] = e
        return dots, e

    def put(part, number, row):
        at = (place ^ number) * PER + part * HALF
        for h in range(PER):
            for g in range(CUBE):
                stats_ref[g, pl.ds(at + h, 1), :] = row[:, h * 128 : (h + 1) * 128]

    @pl.when(role_of() == 0)
    def _():
        for i, number in enumerate(rows):
            partial = None
            for k in range(len(columns)):
                _, e = block_of(i, k)
                for h in range(PER):
                    piece = e[:, h * 128 : (h + 1) * 128]
                    partial = piece if partial is None else partial + piece
            if last:
                at = i % len(NEAR) * BLOCK
                partial = partial + before[i // len(NEAR)][at : at + BLOCK, :]
                put(0, number, jnp.sum(jnp.transpose(partial), axis=0, keepdims=True))
                put(1, number, jnp.zeros((1, BLOCK), F32))
            else:
                rowsum_ref[i * BLOCK : (i + 1) * BLOCK, :] = partial

    @pl.when(role_of() == 1)
    def _():
        for i in range(len(rows)):
            ids = down_rows(row_ids(x[i]), BLOCK)
            for k in range(len(columns)):
                dots, e = block_of(i, k)
                hit = jnp.where(ids == row_ids(y[k]), dots, 0.0)
                at = slice(k * BLOCK, (k + 1) * BLOCK)
                for part, value in enumerate((e, hit)):
                    value = jnp.sum(value.reshape(BLOCK // 8, 8, BLOCK), axis=0)
                    to = slice(part * 8, part * 8 + 8)
                    colsum_ref[to, at] = value if i == 0 else colsum_ref[to, at] + value
        if last:
            for k in range(len(columns)):
                at = slice(k * BLOCK, (k + 1) * BLOCK)
                for part in range(2):
                    to = slice(part * 8, part * 8 + 8)
                    put(part, columns[k], jnp.sum(colsum_ref[to, at], axis=0, keepdims=True))
                    earlier = before[2][to, at] + before[3][to, at]
                    put(part, NEAR[k], jnp.sum(earlier, axis=0, keepdims=True))


def encode(out_ref, value, digits):
    largest = None
    for h in range(WIDTH // 128):
        piece = jnp.abs(value[:, h * 128 : (h + 1) * 128])
        largest = piece if largest is None else jnp.maximum(largest, piece)
    largest = jnp.max(jnp.transpose(largest), axis=0, keepdims=True)
    power = jnp.ceil(jnp.log2(jnp.maximum(largest, 1e-35)) * 128.0)
    steps = value * down_rows(FULL * jnp.exp2(power * (-1.0 / 128.0)), WIDTH)
    out_ref[:BLOCK, :] = jnp.floor(steps + 0.5).astype(jnp.int32).astype(jnp.int16)
    at = lax.broadcasted_iota(jnp.int32, (PAD, BLOCK), 0)
    lane = lax.broadcasted_iota(jnp.int32, (PAD, BLOCK), 1)
    tail = jnp.where(at == 0, jnp.broadcast_to(power, (PAD, BLOCK)), 0.0)
    for n, digit in enumerate(digits):
        tail = jnp.where((at == 1) & (lane == n), digit, tail)
    out_ref[BLOCK:, :] = jnp.zeros((PAD, WIDTH), jnp.int16)
    out_ref[BLOCK:, :BLOCK] = tail.astype(jnp.int32).astype(jnp.int16)


def decode(ref):
    tail = ref[BLOCK:, :BLOCK].astype(jnp.int32).astype(F32)
    scale = down_rows(jnp.exp2(tail[0:1, :] * (1.0 / 128.0)) * (1.0 / FULL), WIDTH)
    return ref[:BLOCK, :].astype(jnp.int32).astype(F32) * scale


def digits_of(loss):
    high = jnp.floor(loss * (1.0 / 16.0))
    rest = (loss - high * 16.0) * 1024.0
    middle = jnp.floor(rest)
    low = jnp.floor((rest - middle) * 16384.0)
    return high, middle, low


def loss_of(ref):
    tail = ref[BLOCK:, :BLOCK].astype(jnp.int32).astype(F32)[1:2, :]
    lane = lax.broadcasted_iota(jnp.int32, (1, BLOCK), 1)
    unit = jnp.where(lane == 0, 16.0, jnp.where(lane == 1, 1.0 / 1024.0, 1.0 / (1024.0 * 16384.0)))
    return jnp.sum(jnp.where(lane < 3, tail * unit, 0.0))


def grad_kernel(chosen, coded, *refs):
    e_near, e_far, e_rest, stats_ref = refs[:4]
    y = refs[4 : 4 + CUBE]
    xs = refs[4 + CUBE : 4 + CUBE + len(chosen)]
    outs = refs[4 + CUBE + len(chosen) : -1]
    scale_ref = refs[-1]
    place = place_in_cube()
    total = jnp.sum(stats_ref[:, :HALF, :], axis=0)
    scale_ref[...] = 1.0 / total
    lse = 20.0 + jnp.log(total)
    picked = 20.0 * jnp.sum(stats_ref[:, HALF:, :], axis=0)
    loss = jnp.sum(lse - picked)

    def scale_of(number):
        at = (place ^ number) * PER
        return jnp.concatenate([scale_ref[pl.ds(at + h, 1), :] for h in range(PER)], axis=1)

    def exps(number, k):
        if k < len(NEAR):
            ref = e_near if number in NEAR else e_far
            i = (NEAR if number in NEAR else FAR).index(number)
        else:
            ref, i, k = e_rest, (NEAR + FAR).index(number), k - len(NEAR)
        return ref[i * BLOCK : (i + 1) * BLOCK, k * BLOCK : (k + 1) * BLOCK]

    def body(role):
        for n, number in enumerate(chosen):
            ids = down_rows(row_ids(xs[n]), BLOCK)
            scale = down_rows(scale_of(number), BLOCK) if role == 0 else None
            acc = None
            for k, column in enumerate(NEAR + FAR):
                if role == 1:
                    scale = scale_of(column)
                hit = jnp.where(ids == row_ids(y[k]), 1.0, 0.0)
                weights = (exps(number, k) * scale - hit).astype(BF16)
                part = jnp.dot(weights, y[k][:BLOCK, :], preferred_element_type=F32)
                acc = part if acc is None else acc + part
            if coded:
                encode(outs[n], 20.0 * acc, digits_of(loss))
            else:
                outs[n][:BLOCK, :] = 20.0 * acc
                outs[n][BLOCK:, :] = jnp.full((LOSS, WIDTH), loss, F32)

    pl.when(role_of() == 0)(functools.partial(body, 0))
    pl.when(role_of() == 1)(functools.partial(body, 1))


def merge_kernel(own_ref, *refs):
    come, out_ref = refs[:-1], refs[-1]
    value, loss = own_ref[:BLOCK, :], own_ref[BLOCK, 0]
    for ref in come:
        value = value + decode(ref)
        loss = loss + loss_of(ref)
    encode(out_ref, value, digits_of(loss))


def split_kernel(own_ref, a_ref, b_ref, c_ref, keep_ref, send_ref):
    value, loss = own_ref[:BLOCK, :], own_ref[BLOCK, 0]
    for ref in (a_ref, b_ref, c_ref):
        value = value + decode(ref)
        loss = loss + loss_of(ref)
    role = role_of()
    keep_ref[ROWS:, :] = jnp.full((LOSS, WIDTH), loss, F32)
    send_ref[ROWS:, :] = jnp.full((LOSS, WIDTH), loss, F32)

    @pl.when(role == 0)
    def _():
        keep_ref[:ROWS, :] = value[:ROWS, :]
        send_ref[:ROWS, :] = value[ROWS:, :]

    @pl.when(role == 1)
    def _():
        keep_ref[:ROWS, :] = value[ROWS:, :]
        send_ref[:ROWS, :] = value[:ROWS, :]


def post_kernel(q_ref, d_ref, keep_ref, come_ref, loss_ref, gq_ref, gd_ref):
    def project(out_ref, grad, values):
        unit, length = unit_rows(values)
        out_ref[...] = (grad - jnp.sum(grad * unit, axis=1, keepdims=True) * unit) / length

    def fill(gq, gd):
        project(gq_ref, gq[:ROWS, :], q_ref[...])
        project(gd_ref, gd[:ROWS, :], d_ref[...])
        loss_ref[...] = gd[ROWS : ROWS + 1, 0:1] * (1.0 / 16384)

    role = role_of()

    @pl.when(role == 0)
    def _():
        fill(keep_ref, come_ref)

    @pl.when(role == 1)
    def _():
        fill(come_ref, keep_ref)


def local(queries, documents, positives):
    piece = pltpu.VMEM((ROWS + PAD, WIDTH), BF16)
    raw = pl.BlockSpec(memory_space=pl.ANY)
    keep, give = pl.pallas_call(
        pre_kernel,
        name="pre",
        in_specs=[raw, raw, raw],
        out_shape=[piece, piece],
        scratch_shapes=[
            pltpu.VMEM((ROWS, WIDTH), BF16),
            pltpu.VMEM((ROWS, WIDTH), BF16),
            pltpu.VMEM((1, ROWS), jnp.int32),
            pltpu.SemaphoreType.DMA((3,)),
        ],
        compiler_params=pltpu.CompilerParams(vmem_limit_bytes=8 * 1024 * 1024),
    )(queries, documents, positives.reshape(1, ROWS))
    come = swap(give)
    own = call(join_kernel, "join", pltpu.VMEM((BLOCK + PAD, WIDTH), BF16), near(keep), near(come))
    x = {0: own}
    for bits in (4, 2, 1):
        x[bits] = send(own, bits)
    y = {0: swap(own)}
    x[5] = send(x[4], 1)
    x[7] = send(x[4], 3)
    x[6] = send(x[2], 4)
    x[3] = send(x[1], 2)
    for bits in NEAR[1:] + FAR:
        y[bits] = swap(x[bits])
    x = {bits: near(v) for bits, v in x.items()}
    y = {bits: near(v) for bits, v in y.items()}

    def tile(rows, columns, name, *before):
        shape = (len(rows) * BLOCK, len(columns) * BLOCK)
        sums = [pltpu.VMEM((shape[0], 128), F32), pltpu.VMEM((16, shape[1]), F32)]
        outs = [pltpu.VMEM(shape, F32)]
        return call(
            functools.partial(tile_kernel, rows, columns, bool(before)),
            name,
            outs + ([pltpu.VMEM((CUBE, 2 * HALF, 128), F32)] if before else sums),
            *[x[i] for i in rows],
            *[y[k] for k in columns],
            *before,
            scratch=sums if before else [],
        )

    e_near, rows_near, cols_near = tile(NEAR, NEAR, "tile_near")
    e_far, rows_far, cols_far = tile(FAR, NEAR, "tile_far")
    e_rest, stats = tile(
        NEAR + FAR, FAR, "tile_rest", *[near(v) for v in (rows_near, rows_far, cols_near, cols_far)]
    )
    stats = lax.all_to_all(stats, "dp", 0, 0, axis_index_groups=SUM_GROUPS, tiled=True)

    coded = pltpu.VMEM((BLOCK + PAD, WIDTH), jnp.int16)
    plain = pltpu.VMEM((BLOCK + LOSS, WIDTH), F32)

    def grads(chosen, name, shape):
        return call(
            functools.partial(grad_kernel, chosen, shape is coded),
            name,
            [shape] * len(chosen),
            *[near(v) for v in (e_near, e_far, e_rest, stats)],
            *[y[k] for k in NEAR + FAR],
            *[x[i] for i in chosen],
            scratch=[pltpu.VMEM((HALF, 128), F32)],
        )

    def merge(own, name, *come):
        return call(merge_kernel, name, coded, near(own), *[near(v) for v in come])

    (g7,) = grads((7,), "grad_7", coded)
    r7 = send(g7, 3)
    (g5,) = grads((5,), "grad_5", coded)
    r5 = send(g5, 1)
    (g6,) = grads((6,), "grad_6", coded)
    r6 = send(g6, 4)
    (g3,) = grads((3,), "grad_3", coded)
    r3 = send(g3, 2)
    g2, g1 = grads((2, 1), "grad_21", plain)
    g4, g0 = grads((4, 0), "grad_40", plain)
    r2 = send(merge(g2, "merge_2", r6), 2)
    r1 = send(merge(g1, "merge_1", r3), 1)
    r4 = send(merge(g4, "merge_4", r5, r7), 4)
    part = pltpu.VMEM((ROWS + LOSS, WIDTH), F32)
    keep, give = call(split_kernel, "split", [part, part], *[near(v) for v in (g0, r4, r2, r1)])
    come = swap(give)
    loss, gq, gd = call(
        post_kernel,
        "post",
        [
            jax.ShapeDtypeStruct((1, 1), F32),
            jax.ShapeDtypeStruct((ROWS, WIDTH), F32),
            jax.ShapeDtypeStruct((ROWS, WIDTH), F32),
        ],
        queries,
        documents,
        near(keep),
        near(come),
    )
    return (loss.reshape(()), gq, gd)


def solution(mesh):
    placed = (P("dp", None), P("dp", None), P("dp"))
    return jax.shard_map(
        local,
        mesh=mesh,
        in_specs=placed,
        out_specs=(P(), P("dp", None), P("dp", None)),
        check_vma=False,
    )
```

```python
import functools

import jax
import jax.numpy as jnp
from jax import lax
from jax.experimental import pallas as pl
from jax.experimental.pallas import tpu as pltpu
from jax.sharding import PartitionSpec as P

PAIRS_A = ((0, 1), (2, 3))
PAIRS_B = ((0, 3), (1, 2))
CUBE = 8
CORES = 2
ROWS = 128
BLOCK = CORES * ROWS
SIDE = CUBE * BLOCK
WIDTH = 768
PAD = 16
LOSS = 8
PER = BLOCK // 128
HALF = CUBE * PER
LOG2E = 1.4426950408889634
FULL = 32760.0
NEAR = (0, 4, 2, 1)
SIDES = (6, 3)
ENDS = (5, 7)
PACKS = (NEAR, SIDES, ENDS)
ALL = NEAR + SIDES + ENDS
PARTS = (
    (NEAR, NEAR),
    (SIDES, NEAR),
    (NEAR + SIDES, SIDES),
    (ENDS, NEAR + SIDES),
    (ALL, ENDS),
)
SPAN = BLOCK + PAD
F32 = jnp.float32
BF16 = jnp.bfloat16


def device_index(x, z, y, core):
    return ((x * 4 + z) * 4 + y) * CORES + core


def partners(bits):
    moves = []
    for x in range(4):
        for z in range(4):
            for y in range(4):
                for core in range(CORES):
                    flip = (lambda v: v ^ 1) if core == 0 else (lambda v: 3 - v)
                    to = [flip(v) if bits & bit else v for v, bit in ((x, 4), (z, 2), (y, 1))]
                    moves.append((device_index(x, z, y, core), device_index(*to, core)))
    return moves


def a_cubes():
    return [
        [device_index(x, z, y, core) for x in px for z in pz for y in py]
        for core in range(CORES)
        for px in PAIRS_A
        for pz in PAIRS_A
        for py in PAIRS_A
    ]


SWAP = [(i, i ^ 1) for i in range(128)]
SUM_GROUPS = a_cubes()


def send(value, bits):
    return lax.ppermute(value, "dp", partners(bits))


def swap(value):
    return lax.ppermute(value, "dp", SWAP)


def near(value):
    return pltpu.with_memory_space_constraint(value, pltpu.VMEM)


def call(kernel, name, out_shape, *args, scratch=(), after=()):
    n = len(args)

    def body(*refs):
        kernel(*refs[:n], *refs[n + len(after) :])

    return pl.pallas_call(
        body,
        name=name,
        out_shape=out_shape,
        scratch_shapes=scratch,
        compiler_params=pltpu.CompilerParams(vmem_limit_bytes=8 * 1024 * 1024),
    )(*args, *[near(v) for v in after])


def role_of():
    return lax.axis_index("dp") & 1


def unit_rows(values):
    wide = values.astype(F32)
    length = jnp.sqrt(jnp.sum(wide * wide, axis=1, keepdims=True) + 1e-06)
    return wide / length, length


def row_ids(ref, at=0):
    tail = ref[at + BLOCK : at + SPAN, :BLOCK].astype(F32)
    return tail[0:1, :] * 128.0 + tail[1:2, :]


def down_rows(row, width):
    wide = jnp.transpose(jnp.broadcast_to(row, (128, row.shape[1])))
    return jnp.concatenate([wide] * (width // 128), axis=1)


def pre_kernel(q_hbm, d_hbm, p_hbm, keep_ref, send_ref, q_ref, d_ref, p_ref, sems):
    copies = [
        pltpu.make_async_copy(src, dst, sems.at[n])
        for n, (src, dst) in enumerate(((q_hbm, q_ref), (d_hbm, d_ref), (p_hbm, p_ref)))
    ]
    for copy in copies:
        copy.start()
    me = lax.axis_index("dp")
    role = role_of()
    for copy in copies:
        copy.wait()

    def fill(ref, values, ids):
        ref[:ROWS, :] = unit_rows(values)[0].astype(BF16)
        high = ids >> 7
        rows = lax.broadcasted_iota(jnp.int32, (PAD, ROWS), 0)
        tail = jnp.where(rows == 0, high, jnp.where(rows == 1, ids - high * 128, 0))
        ref[ROWS:, :] = jnp.zeros((PAD, WIDTH), BF16)
        ref[ROWS:, :ROWS] = tail.astype(F32).astype(BF16)

    mine = me * ROWS + lax.broadcasted_iota(jnp.int32, (1, ROWS), 1)

    @pl.when(role == 0)
    def _():
        fill(keep_ref, q_ref[...], p_ref[...])
        fill(send_ref, d_ref[...], mine)

    @pl.when(role == 1)
    def _():
        fill(keep_ref, d_ref[...], mine)
        fill(send_ref, q_ref[...], p_ref[...])


def join_kernel(keep_ref, come_ref, own_ref):
    def fill(low, high):
        own_ref[:ROWS, :] = low[:ROWS, :]
        own_ref[ROWS:BLOCK, :] = high[:ROWS, :]
        own_ref[BLOCK:, :] = jnp.zeros((PAD, WIDTH), BF16)
        own_ref[BLOCK:, :ROWS] = low[ROWS:, :ROWS]
        own_ref[BLOCK:, ROWS:BLOCK] = high[ROWS:, :ROWS]

    role = role_of()

    @pl.when(role == 0)
    def _():
        fill(keep_ref, come_ref)

    @pl.when(role == 1)
    def _():
        fill(come_ref, keep_ref)


def place_in_cube():
    me = lax.axis_index("dp")
    return ((me >> 5) & 1) * 4 + ((me >> 3) & 1) * 2 + ((me >> 1) & 1)


def pack_kernel(*refs):
    for n, ref in enumerate(refs[:-1]):
        refs[-1][n * SPAN : (n + 1) * SPAN, :] = ref[...]


def packs_of(columns):
    used = [pack for pack in PACKS if set(pack) & set(columns)]
    return used, [
        (p, pack.index(number) * SPAN) for number in columns for p, pack in enumerate(used) if number in pack
    ]


def tile_kernel(part, *refs):
    rows, columns = PARTS[part]
    last = part == len(PARTS) - 1
    used, where = packs_of(columns)
    x, refs = refs[: len(rows)], refs[len(rows) :]
    y, refs = refs[: len(used)], refs[len(used) :]
    if last:
        before, (e_ref, stats_ref, rowsum_ref, colsum_ref) = refs[: 2 * part], refs[2 * part :]
        before = [(before[2 * n], before[2 * n + 1]) for n in range(part)]
    else:
        e_ref, rowsum_ref, colsum_ref = refs
    ids_of_columns = [row_ids(y[p], at) for p, at in where]
    for i in range(len(rows)):
        ids = down_rows(row_ids(x[i]), BLOCK)
        partial = None
        for k, (p, start) in enumerate(where):
            dots = lax.dot_general(
                x[i][:BLOCK, :],
                y[p][start : start + BLOCK, :],
                (((1,), (1,)), ((), ())),
                preferred_element_type=F32,
            )
            e = jnp.exp2(dots * (20.0 * LOG2E) - 20.0 * LOG2E)
            at = slice(k * BLOCK, (k + 1) * BLOCK)
            e_ref[i * BLOCK : (i + 1) * BLOCK, at] = e
            for h in range(PER):
                piece = e[:, h * 128 : (h + 1) * 128]
                partial = piece if partial is None else partial + piece
            hit = jnp.where(ids == ids_of_columns[k], dots, 0.0)
            for n, value in enumerate((e, hit)):
                value = jnp.sum(value.reshape(BLOCK // 8, 8, BLOCK), axis=0)
                to = slice(n * 8, n * 8 + 8)
                colsum_ref[to, at] = value if i == 0 else colsum_ref[to, at] + value
        rowsum_ref[i * BLOCK : (i + 1) * BLOCK, :] = partial

    if last:
        place = place_in_cube()
        sums = before + [(rowsum_ref, colsum_ref)]

        def put(n, number, row):
            at = (place ^ number) * PER + n * HALF
            for h in range(PER):
                for g in range(CUBE):
                    stats_ref[g, pl.ds(at + h, 1), :] = row[:, h * 128 : (h + 1) * 128]

        @pl.when(role_of() == 0)
        def _():
            for number in ALL:
                total = None
                for (these, _), (ref, _) in zip(PARTS, sums):
                    if number in these:
                        at = these.index(number) * BLOCK
                        piece = ref[at : at + BLOCK, :]
                        total = piece if total is None else total + piece
                put(0, number, jnp.sum(jnp.transpose(total), axis=0, keepdims=True))
                put(1, number, jnp.zeros((1, BLOCK), F32))

        @pl.when(role_of() == 1)
        def _():
            for number in ALL:
                for n in range(2):
                    total = None
                    for (_, these), (_, ref) in zip(PARTS, sums):
                        if number in these:
                            at = these.index(number) * BLOCK
                            piece = ref[n * 8 : n * 8 + 8, at : at + BLOCK]
                            total = piece if total is None else total + piece
                    put(n, number, jnp.sum(total, axis=0, keepdims=True))


def encode(out_ref, value, digits):
    largest = None
    for h in range(WIDTH // 128):
        piece = jnp.abs(value[:, h * 128 : (h + 1) * 128])
        largest = piece if largest is None else jnp.maximum(largest, piece)
    largest = jnp.max(jnp.transpose(largest), axis=0, keepdims=True)
    power = jnp.ceil(jnp.log2(jnp.maximum(largest, 1e-35)) * 128.0)
    steps = value * down_rows(FULL * jnp.exp2(power * (-1.0 / 128.0)), WIDTH)
    out_ref[:BLOCK, :] = jnp.floor(steps + 0.5).astype(jnp.int32).astype(jnp.int16)
    at = lax.broadcasted_iota(jnp.int32, (PAD, BLOCK), 0)
    lane = lax.broadcasted_iota(jnp.int32, (PAD, BLOCK), 1)
    tail = jnp.where(at == 0, jnp.broadcast_to(power, (PAD, BLOCK)), 0.0)
    for n, digit in enumerate(digits):
        tail = jnp.where((at == 1) & (lane == n), digit, tail)
    out_ref[BLOCK:, :] = jnp.zeros((PAD, WIDTH), jnp.int16)
    out_ref[BLOCK:, :BLOCK] = tail.astype(jnp.int32).astype(jnp.int16)


def decode(ref):
    tail = ref[BLOCK:, :BLOCK].astype(jnp.int32).astype(F32)
    scale = down_rows(jnp.exp2(tail[0:1, :] * (1.0 / 128.0)) * (1.0 / FULL), WIDTH)
    return ref[:BLOCK, :].astype(jnp.int32).astype(F32) * scale


def digits_of(loss):
    high = jnp.floor(loss * (1.0 / 16.0))
    rest = (loss - high * 16.0) * 1024.0
    middle = jnp.floor(rest)
    low = jnp.floor((rest - middle) * 16384.0)
    return high, middle, low


def loss_of(ref):
    tail = ref[BLOCK:, :BLOCK].astype(jnp.int32).astype(F32)[1:2, :]
    lane = lax.broadcasted_iota(jnp.int32, (1, BLOCK), 1)
    unit = jnp.where(lane == 0, 16.0, jnp.where(lane == 1, 1.0 / 1024.0, 1.0 / (1024.0 * 16384.0)))
    return jnp.sum(jnp.where(lane < 3, tail * unit, 0.0))


def scale_kernel(stats_ref, out_ref):
    total = jnp.sum(stats_ref[:, :HALF, :], axis=0)
    out_ref[:HALF, :] = 1.0 / total
    lse = 20.0 + jnp.log(total)
    picked = 20.0 * jnp.sum(stats_ref[:, HALF:, :], axis=0)
    out_ref[HALF:, :] = jnp.full((8, 128), jnp.sum(lse - picked), F32)


def grad_kernel(number, coded, *refs):
    exps, refs = refs[: len(PARTS)], refs[len(PARTS) :]
    y, refs = refs[: len(PACKS)], refs[len(PACKS) :]
    scale_ref, x_ref, come, out_ref = refs[0], refs[1], refs[2:-1], refs[-1]
    place = place_in_cube()
    role = role_of()
    loss = scale_ref[HALF, 0]
    _, where = packs_of(ALL)

    def scale_of(block):
        at = (place ^ block) * PER
        return jnp.concatenate([scale_ref[pl.ds(at + h, 1), :] for h in range(PER)], axis=1)

    ids = down_rows(row_ids(x_ref), BLOCK)
    down = down_rows(jnp.where(role == 0, scale_of(number), 1.0), BLOCK)
    acc = None
    for column, (p, start) in zip(ALL, where):
        (e,) = [
            ref[
                rows.index(number) * BLOCK : (rows.index(number) + 1) * BLOCK,
                columns.index(column) * BLOCK : (columns.index(column) + 1) * BLOCK,
            ]
            for (rows, columns), ref in zip(PARTS, exps)
            if number in rows and column in columns
        ]
        along = jnp.where(role == 1, scale_of(column), 1.0)
        hit = jnp.where(ids == row_ids(y[p], start), 1.0, 0.0)
        weights = (e * down * along - hit).astype(BF16)
        part = jnp.dot(weights, y[p][start : start + BLOCK, :], preferred_element_type=F32)
        acc = part if acc is None else acc + part
    value = 20.0 * acc
    for ref in come:
        value = value + decode(ref)
        loss = loss + loss_of(ref)
    if coded:
        encode(out_ref, value, digits_of(loss))
    else:
        out_ref[:BLOCK, :] = value
        out_ref[BLOCK:, :] = jnp.full((LOSS, WIDTH), loss, F32)


def split_kernel(own_ref, a_ref, b_ref, c_ref, keep_ref, send_ref):
    value, loss = own_ref[:BLOCK, :], own_ref[BLOCK, 0]
    for ref in (a_ref, b_ref, c_ref):
        value = value + decode(ref)
        loss = loss + loss_of(ref)
    role = role_of()
    keep_ref[ROWS:, :] = jnp.full((LOSS, WIDTH), loss, F32)
    send_ref[ROWS:, :] = jnp.full((LOSS, WIDTH), loss, F32)

    @pl.when(role == 0)
    def _():
        keep_ref[:ROWS, :] = value[:ROWS, :]
        send_ref[:ROWS, :] = value[ROWS:, :]

    @pl.when(role == 1)
    def _():
        keep_ref[:ROWS, :] = value[ROWS:, :]
        send_ref[:ROWS, :] = value[:ROWS, :]


def post_kernel(q_ref, d_ref, keep_ref, come_ref, loss_ref, gq_ref, gd_ref):
    def project(out_ref, grad, values):
        unit, length = unit_rows(values)
        out_ref[...] = (grad - jnp.sum(grad * unit, axis=1, keepdims=True) * unit) / length

    def fill(gq, gd):
        project(gq_ref, gq[:ROWS, :], q_ref[...])
        project(gd_ref, gd[:ROWS, :], d_ref[...])
        loss_ref[...] = gd[ROWS : ROWS + 1, 0:1] * (1.0 / 16384)

    role = role_of()

    @pl.when(role == 0)
    def _():
        fill(keep_ref, come_ref)

    @pl.when(role == 1)
    def _():
        fill(come_ref, keep_ref)


def local(queries, documents, positives):
    piece = pltpu.VMEM((ROWS + PAD, WIDTH), BF16)
    raw = [queries, documents, positives.reshape(1, ROWS)]
    keep, give = pl.pallas_call(
        pre_kernel,
        name="pre",
        in_specs=[pl.BlockSpec(memory_space=pltpu.HBM)] * 3,
        out_shape=[piece, piece],
        scratch_shapes=[
            pltpu.VMEM((ROWS, WIDTH), BF16),
            pltpu.VMEM((ROWS, WIDTH), BF16),
            pltpu.VMEM((1, ROWS), jnp.int32),
            pltpu.SemaphoreType.DMA((3,)),
        ],
        compiler_params=pltpu.CompilerParams(vmem_limit_bytes=8 * 1024 * 1024),
    )(*[pltpu.with_memory_space_constraint(v, pltpu.HBM) for v in raw])
    come = swap(give)
    own = call(join_kernel, "join", pltpu.VMEM((SPAN, WIDTH), BF16), near(keep), near(come))

    def pack(blocks, name, after=()):
        shape = pltpu.VMEM((len(blocks) * SPAN, WIDTH), BF16)
        return call(pack_kernel, name, shape, *[near(x[n]) for n in blocks], after=after)

    x = {0: own}
    for bits in (4, 2, 1):
        x[bits] = send(own, bits)
    x[7] = send(x[4], 3)
    x[6] = send(x[2], 4)
    x[3] = send(x[1], 2)
    x[5] = send(x[1], 4)
    y = [swap(pack(NEAR, "pack_near"))]
    parts = []

    def tile(part, name):
        rows, columns = PARTS[part]
        used, _ = packs_of(columns)
        last = part == len(PARTS) - 1
        e = pltpu.VMEM((len(rows) * BLOCK, len(columns) * BLOCK), F32)
        sums = [pltpu.VMEM((len(rows) * BLOCK, 128), F32), pltpu.VMEM((16, len(columns) * BLOCK), F32)]
        before = [near(v) for done in parts for v in done[1:]] if last else []
        parts.append(
            call(
                functools.partial(tile_kernel, part),
                name,
                [e, pltpu.VMEM((CUBE, 2 * HALF, 128), F32)] if last else [e, *sums],
                *[near(x[n]) for n in rows],
                *[near(y[PACKS.index(pack)]) for pack in used],
                *before,
                scratch=sums if last else [],
            )
        )

    tile(0, "tile_0")
    y.append(swap(pack(SIDES, "pack_sides", after=[parts[0][1]])))
    tile(1, "tile_1")
    y.append(swap(pack(ENDS, "pack_ends", after=[parts[1][1]])))
    tile(2, "tile_2")
    tile(3, "tile_3")
    tile(4, "tile_4")
    stats = lax.all_to_all(parts[-1][1], "dp", 0, 0, axis_index_groups=SUM_GROUPS, tiled=True)
    scales = call(scale_kernel, "scales", pltpu.VMEM((HALF + 8, 128), F32), near(stats))

    coded = pltpu.VMEM((SPAN, WIDTH), jnp.int16)
    plain = pltpu.VMEM((BLOCK + LOSS, WIDTH), F32)

    def grad(number, *come, after, shape=coded):
        return call(
            functools.partial(grad_kernel, number, shape is coded),
            f"grad_{number}",
            shape,
            *[near(v[0]) for v in parts],
            *[near(v) for v in y],
            near(scales),
            near(x[number]),
            *[near(v) for v in come],
            after=after,
        )

    g7 = grad(7, after=[])
    r7 = send(g7, 3)
    g3 = grad(3, after=[])
    r3 = send(g3, 2)
    g5 = grad(5, after=[])
    r5 = send(g5, 1)
    g6 = grad(6, after=[])
    r6 = send(g6, 4)
    g1 = grad(1, r3, after=[])
    r1 = send(g1, 1)
    g2 = grad(2, r6, after=[])
    r2 = send(g2, 2)
    g4 = grad(4, r5, r7, after=[])
    r4 = send(g4, 4)
    g0 = grad(0, after=[], shape=plain)
    part = pltpu.VMEM((ROWS + LOSS, WIDTH), F32)
    keep, give = call(split_kernel, "split", [part, part], *[near(v) for v in (g0, r1, r2, r4)])
    come = swap(give)
    loss, gq, gd = call(
        post_kernel,
        "post",
        [
            jax.ShapeDtypeStruct((1, 1), F32),
            jax.ShapeDtypeStruct((ROWS, WIDTH), F32),
            jax.ShapeDtypeStruct((ROWS, WIDTH), F32),
        ],
        queries,
        documents,
        near(keep),
        near(come),
    )
    return (loss.reshape(()), gq, gd)


def solution(mesh):
    placed = (P("dp", None), P("dp", None), P("dp"))
    return jax.shard_map(
        local,
        mesh=mesh,
        in_specs=placed,
        out_specs=(P(), P("dp", None), P("dp", None)),
        check_vma=False,
    )
```

```python
import functools

import jax
import jax.numpy as jnp
from jax import lax
from jax.experimental import pallas as pl
from jax.experimental.pallas import tpu as pltpu
from jax.sharding import PartitionSpec as P

PAIRS_A = ((0, 1), (2, 3))
PAIRS_B = ((0, 3), (1, 2))
CUBE = 8
CORES = 2
ROWS = 128
BLOCK = CORES * ROWS
SIDE = CUBE * BLOCK
WIDTH = 768
PAD = 16
LOSS = 8
PER = BLOCK // 128
HALF = CUBE * PER
LOG2E = 1.4426950408889634
FULL = 32760.0
NEAR = (0, 4, 2, 1)
SIDES = (3, 6, 5)
CORNER = (7,)
PACKS = (NEAR, SIDES, CORNER)
ALL = NEAR + SIDES + CORNER
PARTS = (
    (NEAR, NEAR),
    (SIDES, NEAR),
    (NEAR + SIDES, SIDES),
    (CORNER, NEAR + SIDES),
    (ALL, CORNER),
)
SPAN = BLOCK + PAD
F32 = jnp.float32
BF16 = jnp.bfloat16


def device_index(x, z, y, core):
    return ((x * 4 + z) * 4 + y) * CORES + core


def partners(bits):
    moves = []
    for x in range(4):
        for z in range(4):
            for y in range(4):
                for core in range(CORES):
                    flip = (lambda v: v ^ 1) if core == 0 else (lambda v: 3 - v)
                    to = [flip(v) if bits & bit else v for v, bit in ((x, 4), (z, 2), (y, 1))]
                    moves.append((device_index(x, z, y, core), device_index(*to, core)))
    return moves


def a_cubes():
    return [
        [device_index(x, z, y, core) for x in px for z in pz for y in py]
        for core in range(CORES)
        for px in PAIRS_A
        for pz in PAIRS_A
        for py in PAIRS_A
    ]


SWAP = [(i, i ^ 1) for i in range(128)]
SUM_GROUPS = a_cubes()


def send(value, bits):
    return lax.ppermute(value, "dp", partners(bits))


def swap(value):
    return lax.ppermute(value, "dp", SWAP)


def near(value):
    return pltpu.with_memory_space_constraint(value, pltpu.VMEM)


def call(kernel, name, out_shape, *args, scratch=(), after=()):
    n = len(args)

    def body(*refs):
        kernel(*refs[:n], *refs[n + len(after) :])

    return pl.pallas_call(
        body,
        name=name,
        out_shape=out_shape,
        scratch_shapes=scratch,
        compiler_params=pltpu.CompilerParams(vmem_limit_bytes=8 * 1024 * 1024),
    )(*args, *[near(v) for v in after])


def role_of():
    return lax.axis_index("dp") & 1


def unit_rows(values):
    wide = values.astype(F32)
    length = jnp.sqrt(jnp.sum(wide * wide, axis=1, keepdims=True) + 1e-06)
    return wide / length, length


def row_ids(ref, at=0):
    tail = ref[at + BLOCK : at + SPAN, :BLOCK].astype(F32)
    return tail[0:1, :] * 128.0 + tail[1:2, :]


def down_rows(row, width):
    wide = jnp.transpose(jnp.broadcast_to(row, (128, row.shape[1])))
    return jnp.concatenate([wide] * (width // 128), axis=1)


def pre_kernel(q_hbm, d_hbm, p_hbm, keep_ref, send_ref, q_ref, d_ref, p_ref, sems):
    copies = [
        pltpu.make_async_copy(src, dst, sems.at[n])
        for n, (src, dst) in enumerate(((q_hbm, q_ref), (d_hbm, d_ref), (p_hbm, p_ref)))
    ]
    for copy in copies:
        copy.start()
    me = lax.axis_index("dp")
    role = role_of()
    for copy in copies:
        copy.wait()

    def fill(ref, values, ids):
        ref[:ROWS, :] = unit_rows(values)[0].astype(BF16)
        high = ids >> 7
        rows = lax.broadcasted_iota(jnp.int32, (PAD, ROWS), 0)
        tail = jnp.where(rows == 0, high, jnp.where(rows == 1, ids - high * 128, 0))
        ref[ROWS:, :] = jnp.zeros((PAD, WIDTH), BF16)
        ref[ROWS:, :ROWS] = tail.astype(F32).astype(BF16)

    mine = me * ROWS + lax.broadcasted_iota(jnp.int32, (1, ROWS), 1)

    @pl.when(role == 0)
    def _():
        fill(keep_ref, q_ref[...], p_ref[...])
        fill(send_ref, d_ref[...], mine)

    @pl.when(role == 1)
    def _():
        fill(keep_ref, d_ref[...], mine)
        fill(send_ref, q_ref[...], p_ref[...])


def join_kernel(keep_ref, come_ref, own_ref):
    def fill(low, high):
        own_ref[:ROWS, :] = low[:ROWS, :]
        own_ref[ROWS:BLOCK, :] = high[:ROWS, :]
        own_ref[BLOCK:, :] = jnp.zeros((PAD, WIDTH), BF16)
        own_ref[BLOCK:, :ROWS] = low[ROWS:, :ROWS]
        own_ref[BLOCK:, ROWS:BLOCK] = high[ROWS:, :ROWS]

    role = role_of()

    @pl.when(role == 0)
    def _():
        fill(keep_ref, come_ref)

    @pl.when(role == 1)
    def _():
        fill(come_ref, keep_ref)


def place_in_cube():
    me = lax.axis_index("dp")
    return ((me >> 5) & 1) * 4 + ((me >> 3) & 1) * 2 + ((me >> 1) & 1)


def pack_kernel(*refs):
    for n, ref in enumerate(refs[:-1]):
        refs[-1][n * SPAN : (n + 1) * SPAN, :] = ref[...]


def packs_of(columns):
    used = [pack for pack in PACKS if set(pack) & set(columns)]
    return used, [
        (p, pack.index(number) * SPAN) for number in columns for p, pack in enumerate(used) if number in pack
    ]


def tile_kernel(part, *refs):
    rows, columns = PARTS[part]
    last = part == len(PARTS) - 1
    used, where = packs_of(columns)
    x, refs = refs[: len(rows)], refs[len(rows) :]
    y, refs = refs[: len(used)], refs[len(used) :]
    if last:
        before, (e_ref, stats_ref, rowsum_ref, colsum_ref) = refs[: 2 * part], refs[2 * part :]
        before = [(before[2 * n], before[2 * n + 1]) for n in range(part)]
    else:
        e_ref, rowsum_ref, colsum_ref = refs
    ids_of_columns = [row_ids(y[p], at) for p, at in where]
    for i in range(len(rows)):
        ids = down_rows(row_ids(x[i]), BLOCK)
        partial = None
        for k, (p, start) in enumerate(where):
            dots = lax.dot_general(
                x[i][:BLOCK, :],
                y[p][start : start + BLOCK, :],
                (((1,), (1,)), ((), ())),
                preferred_element_type=F32,
            )
            e = jnp.exp2(dots * (20.0 * LOG2E) - 20.0 * LOG2E)
            at = slice(k * BLOCK, (k + 1) * BLOCK)
            e_ref[i * BLOCK : (i + 1) * BLOCK, at] = e
            for h in range(PER):
                piece = e[:, h * 128 : (h + 1) * 128]
                partial = piece if partial is None else partial + piece
            hit = jnp.where(ids == ids_of_columns[k], dots, 0.0)
            for n, value in enumerate((e, hit)):
                value = jnp.sum(value.reshape(BLOCK // 8, 8, BLOCK), axis=0)
                to = slice(n * 8, n * 8 + 8)
                colsum_ref[to, at] = value if i == 0 else colsum_ref[to, at] + value
        rowsum_ref[i * BLOCK : (i + 1) * BLOCK, :] = partial

    if last:
        place = place_in_cube()
        sums = before + [(rowsum_ref, colsum_ref)]

        def put(n, number, row):
            at = (place ^ number) * PER + n * HALF
            for h in range(PER):
                for g in range(CUBE):
                    stats_ref[g, pl.ds(at + h, 1), :] = row[:, h * 128 : (h + 1) * 128]

        @pl.when(role_of() == 0)
        def _():
            for number in ALL:
                total = None
                for (these, _), (ref, _) in zip(PARTS, sums):
                    if number in these:
                        at = these.index(number) * BLOCK
                        piece = ref[at : at + BLOCK, :]
                        total = piece if total is None else total + piece
                put(0, number, jnp.sum(jnp.transpose(total), axis=0, keepdims=True))
                put(1, number, jnp.zeros((1, BLOCK), F32))

        @pl.when(role_of() == 1)
        def _():
            for number in ALL:
                for n in range(2):
                    total = None
                    for (_, these), (_, ref) in zip(PARTS, sums):
                        if number in these:
                            at = these.index(number) * BLOCK
                            piece = ref[n * 8 : n * 8 + 8, at : at + BLOCK]
                            total = piece if total is None else total + piece
                    put(n, number, jnp.sum(total, axis=0, keepdims=True))


def encode(out_ref, value, digits):
    largest = None
    for h in range(WIDTH // 128):
        piece = jnp.abs(value[:, h * 128 : (h + 1) * 128])
        largest = piece if largest is None else jnp.maximum(largest, piece)
    largest = jnp.max(jnp.transpose(largest), axis=0, keepdims=True)
    power = jnp.ceil(jnp.log2(jnp.maximum(largest, 1e-35)) * 128.0)
    steps = value * down_rows(FULL * jnp.exp2(power * (-1.0 / 128.0)), WIDTH)
    out_ref[:BLOCK, :] = jnp.floor(steps + 0.5).astype(jnp.int32).astype(jnp.int16)
    at = lax.broadcasted_iota(jnp.int32, (PAD, BLOCK), 0)
    lane = lax.broadcasted_iota(jnp.int32, (PAD, BLOCK), 1)
    tail = jnp.where(at == 0, jnp.broadcast_to(power, (PAD, BLOCK)), 0.0)
    for n, digit in enumerate(digits):
        tail = jnp.where((at == 1) & (lane == n), digit, tail)
    out_ref[BLOCK:, :] = jnp.zeros((PAD, WIDTH), jnp.int16)
    out_ref[BLOCK:, :BLOCK] = tail.astype(jnp.int32).astype(jnp.int16)


def decode(ref):
    tail = ref[BLOCK:, :BLOCK].astype(jnp.int32).astype(F32)
    scale = down_rows(jnp.exp2(tail[0:1, :] * (1.0 / 128.0)) * (1.0 / FULL), WIDTH)
    return ref[:BLOCK, :].astype(jnp.int32).astype(F32) * scale


def digits_of(loss):
    high = jnp.floor(loss * (1.0 / 16.0))
    rest = (loss - high * 16.0) * 1024.0
    middle = jnp.floor(rest)
    low = jnp.floor((rest - middle) * 16384.0)
    return high, middle, low


def loss_of(ref):
    tail = ref[BLOCK:, :BLOCK].astype(jnp.int32).astype(F32)[1:2, :]
    lane = lax.broadcasted_iota(jnp.int32, (1, BLOCK), 1)
    unit = jnp.where(lane == 0, 16.0, jnp.where(lane == 1, 1.0 / 1024.0, 1.0 / (1024.0 * 16384.0)))
    return jnp.sum(jnp.where(lane < 3, tail * unit, 0.0))


def scale_kernel(stats_ref, out_ref):
    total = jnp.sum(stats_ref[:, :HALF, :], axis=0)
    out_ref[:HALF, :] = 1.0 / total
    lse = 20.0 + jnp.log(total)
    picked = 20.0 * jnp.sum(stats_ref[:, HALF:, :], axis=0)
    out_ref[HALF:, :] = jnp.full((8, 128), jnp.sum(lse - picked), F32)


def grad_kernel(number, coded, *refs):
    exps, refs = refs[: len(PARTS)], refs[len(PARTS) :]
    y, refs = refs[: len(PACKS)], refs[len(PACKS) :]
    scale_ref, x_ref, come, out_ref = refs[0], refs[1], refs[2:-1], refs[-1]
    place = place_in_cube()
    role = role_of()
    loss = scale_ref[HALF, 0]
    _, where = packs_of(ALL)

    def scale_of(block):
        at = (place ^ block) * PER
        return jnp.concatenate([scale_ref[pl.ds(at + h, 1), :] for h in range(PER)], axis=1)

    ids = down_rows(row_ids(x_ref), BLOCK)
    down = down_rows(jnp.where(role == 0, scale_of(number), 1.0), BLOCK)
    acc = None
    for column, (p, start) in zip(ALL, where):
        (e,) = [
            ref[
                rows.index(number) * BLOCK : (rows.index(number) + 1) * BLOCK,
                columns.index(column) * BLOCK : (columns.index(column) + 1) * BLOCK,
            ]
            for (rows, columns), ref in zip(PARTS, exps)
            if number in rows and column in columns
        ]
        along = jnp.where(role == 1, scale_of(column), 1.0)
        hit = jnp.where(ids == row_ids(y[p], start), 1.0, 0.0)
        weights = (e * down * along - hit).astype(BF16)
        part = jnp.dot(weights, y[p][start : start + BLOCK, :], preferred_element_type=F32)
        acc = part if acc is None else acc + part
    value = 20.0 * acc
    for ref in come:
        value = value + decode(ref)
        loss = loss + loss_of(ref)
    if coded:
        encode(out_ref, value, digits_of(loss))
    else:
        out_ref[:BLOCK, :] = value
        out_ref[BLOCK:, :] = jnp.full((LOSS, WIDTH), loss, F32)


def split_kernel(own_ref, a_ref, b_ref, c_ref, keep_ref, send_ref):
    value, loss = own_ref[:BLOCK, :], own_ref[BLOCK, 0]
    for ref in (a_ref, b_ref, c_ref):
        value = value + decode(ref)
        loss = loss + loss_of(ref)
    role = role_of()
    keep_ref[ROWS:, :] = jnp.full((LOSS, WIDTH), loss, F32)
    send_ref[ROWS:, :] = jnp.full((LOSS, WIDTH), loss, F32)

    @pl.when(role == 0)
    def _():
        keep_ref[:ROWS, :] = value[:ROWS, :]
        send_ref[:ROWS, :] = value[ROWS:, :]

    @pl.when(role == 1)
    def _():
        keep_ref[:ROWS, :] = value[ROWS:, :]
        send_ref[:ROWS, :] = value[:ROWS, :]


def post_kernel(q_ref, d_ref, keep_ref, come_ref, loss_ref, gq_ref, gd_ref):
    def project(out_ref, grad, values):
        unit, length = unit_rows(values)
        out_ref[...] = (grad - jnp.sum(grad * unit, axis=1, keepdims=True) * unit) / length

    def fill(gq, gd):
        project(gq_ref, gq[:ROWS, :], q_ref[...])
        project(gd_ref, gd[:ROWS, :], d_ref[...])
        loss_ref[...] = gd[ROWS : ROWS + 1, 0:1] * (1.0 / 16384)

    role = role_of()

    @pl.when(role == 0)
    def _():
        fill(keep_ref, come_ref)

    @pl.when(role == 1)
    def _():
        fill(come_ref, keep_ref)


def local(queries, documents, positives):
    piece = pltpu.VMEM((ROWS + PAD, WIDTH), BF16)
    raw = [queries, documents, positives.reshape(1, ROWS)]
    keep, give = pl.pallas_call(
        pre_kernel,
        name="pre",
        in_specs=[pl.BlockSpec(memory_space=pltpu.HBM)] * 3,
        out_shape=[piece, piece],
        scratch_shapes=[
            pltpu.VMEM((ROWS, WIDTH), BF16),
            pltpu.VMEM((ROWS, WIDTH), BF16),
            pltpu.VMEM((1, ROWS), jnp.int32),
            pltpu.SemaphoreType.DMA((3,)),
        ],
        compiler_params=pltpu.CompilerParams(vmem_limit_bytes=8 * 1024 * 1024),
    )(*[pltpu.with_memory_space_constraint(v, pltpu.HBM) for v in raw])
    come = swap(give)
    own = call(join_kernel, "join", pltpu.VMEM((SPAN, WIDTH), BF16), near(keep), near(come))

    def pack(blocks, name, after=()):
        shape = pltpu.VMEM((len(blocks) * SPAN, WIDTH), BF16)
        return call(pack_kernel, name, shape, *[near(x[n]) for n in blocks], after=after)

    x = {0: own}
    for bits in (4, 2, 1):
        x[bits] = send(own, bits)
    x[3] = send(x[1], 2)
    x[6] = send(x[2], 4)
    x[5] = send(x[4], 1)
    x[7] = send(x[3], 4)
    y = [swap(pack(NEAR, "pack_near"))]
    parts = []

    def tile(part, name, after=()):
        rows, columns = PARTS[part]
        used, _ = packs_of(columns)
        last = part == len(PARTS) - 1
        e = pltpu.VMEM((len(rows) * BLOCK, len(columns) * BLOCK), F32)
        sums = [pltpu.VMEM((len(rows) * BLOCK, 128), F32), pltpu.VMEM((16, len(columns) * BLOCK), F32)]
        before = [near(v) for done in parts for v in done[1:]] if last else []
        parts.append(
            call(
                functools.partial(tile_kernel, part),
                name,
                [e, pltpu.VMEM((CUBE, 2 * HALF, 128), F32)] if last else [e, *sums],
                *[near(x[n]) for n in rows],
                *[near(y[PACKS.index(pack)]) for pack in used],
                *before,
                scratch=sums if last else [],
                after=after,
            )
        )

    tile(0, "tile_0")
    y.append(swap(pack(SIDES, "pack_sides", after=[parts[0][1]])))
    tile(1, "tile_1")
    tile(2, "tile_2", [parts[1][1]])
    y.append(swap(pack(CORNER, "pack_corner", after=[parts[2][1]])))
    tile(3, "tile_3")
    tile(4, "tile_4")
    stats = lax.all_to_all(parts[-1][1], "dp", 0, 0, axis_index_groups=SUM_GROUPS, tiled=True)
    scales = call(scale_kernel, "scales", pltpu.VMEM((HALF + 8, 128), F32), near(stats))

    coded = pltpu.VMEM((SPAN, WIDTH), jnp.int16)
    plain = pltpu.VMEM((BLOCK + LOSS, WIDTH), F32)

    def grad(number, *come, after=(), shape=coded):
        return call(
            functools.partial(grad_kernel, number, shape is coded),
            f"grad_{number}",
            shape,
            *[near(v[0]) for v in parts],
            *[near(v) for v in y],
            near(scales),
            near(x[number]),
            *[near(v) for v in come],
            after=after,
        )

    g7 = grad(7)
    r7 = send(g7, 4)
    g6 = grad(6)
    r6 = send(g6, 2)
    g5 = grad(5)
    r5 = send(g5, 1)
    g3 = grad(3, r7)
    r3 = send(g3, 2)
    g4 = grad(4, r6, r5)
    r4 = send(g4, 4)
    g2 = grad(2)
    r2 = send(g2, 2)
    g1 = grad(1, r3)
    r1 = send(g1, 1)
    g0 = grad(0, shape=plain)
    part = pltpu.VMEM((ROWS + LOSS, WIDTH), F32)
    keep, give = call(split_kernel, "split", [part, part], *[near(v) for v in (g0, r1, r2, r4)])
    come = swap(give)
    loss, gq, gd = call(
        post_kernel,
        "post",
        [
            jax.ShapeDtypeStruct((1, 1), F32),
            jax.ShapeDtypeStruct((ROWS, WIDTH), F32),
            jax.ShapeDtypeStruct((ROWS, WIDTH), F32),
        ],
        queries,
        documents,
        near(keep),
        near(come),
    )
    return (loss.reshape(()), gq, gd)


def solution(mesh):
    placed = (P("dp", None), P("dp", None), P("dp"))
    return jax.shard_map(
        local,
        mesh=mesh,
        in_specs=placed,
        out_specs=(P(), P("dp", None), P("dp", None)),
        check_vma=False,
    )
```

```python
import functools

import jax
import jax.numpy as jnp
from jax import lax
from jax.experimental import pallas as pl
from jax.experimental.pallas import tpu as pltpu
from jax.sharding import PartitionSpec as P

PAIRS_A = ((0, 1), (2, 3))
PAIRS_B = ((0, 3), (1, 2))
CUBE = 8
CORES = 2
ROWS = 128
BLOCK = CORES * ROWS
SIDE = CUBE * BLOCK
WIDTH = 768
PAD = 16
LOSS = 8
PER = BLOCK // 128
HALF = CUBE * PER
LOG2E = 1.4426950408889634
FULL = 32760.0
NEAR = (0, 4, 2, 1)
FAR = (7, 3, 6, 5)
PACKS = (NEAR, FAR[:2], FAR[2:])
ALL = NEAR + FAR
PARTS = (
    (NEAR, NEAR, ()),
    (FAR, NEAR, ()),
    (ALL, FAR[:2], ()),
    (ALL, FAR[2:], ()),
)
SPAN = BLOCK + PAD
F32 = jnp.float32
BF16 = jnp.bfloat16


def device_index(x, z, y, core):
    return ((x * 4 + z) * 4 + y) * CORES + core


def partners(bits):
    moves = []
    for x in range(4):
        for z in range(4):
            for y in range(4):
                for core in range(CORES):
                    flip = (lambda v: v ^ 1) if core == 0 else (lambda v: 3 - v)
                    to = [flip(v) if bits & bit else v for v, bit in ((x, 4), (z, 2), (y, 1))]
                    moves.append((device_index(x, z, y, core), device_index(*to, core)))
    return moves


def a_cubes():
    return [
        [device_index(x, z, y, core) for x in px for z in pz for y in py]
        for core in range(CORES)
        for px in PAIRS_A
        for pz in PAIRS_A
        for py in PAIRS_A
    ]


SWAP = [(i, i ^ 1) for i in range(128)]
SUM_GROUPS = a_cubes()


def send(value, bits):
    return lax.ppermute(value, "dp", partners(bits))


def swap(value):
    return lax.ppermute(value, "dp", SWAP)


def near(value):
    return pltpu.with_memory_space_constraint(value, pltpu.VMEM)


def call(kernel, name, out_shape, *args, scratch=(), after=()):
    n = len(args)

    def body(*refs):
        kernel(*refs[:n], *refs[n + len(after) :])

    return pl.pallas_call(
        body,
        name=name,
        out_shape=out_shape,
        scratch_shapes=scratch,
        compiler_params=pltpu.CompilerParams(vmem_limit_bytes=8 * 1024 * 1024),
    )(*args, *[near(v) for v in after])


def role_of():
    return lax.axis_index("dp") & 1


def unit_rows(values):
    wide = values.astype(F32)
    length = jnp.sqrt(jnp.sum(wide * wide, axis=1, keepdims=True) + 1e-06)
    return wide / length, length


def row_ids(ref, at=0):
    tail = ref[at + BLOCK : at + SPAN, :BLOCK].astype(F32)
    return tail[0:1, :] * 128.0 + tail[1:2, :]


def down_rows(row, width):
    wide = jnp.transpose(jnp.broadcast_to(row, (128, row.shape[1])))
    return jnp.concatenate([wide] * (width // 128), axis=1)


def pre_kernel(q_hbm, d_hbm, p_hbm, keep_ref, send_ref, q_ref, d_ref, p_ref, sems):
    copies = [
        pltpu.make_async_copy(src, dst, sems.at[n])
        for n, (src, dst) in enumerate(((q_hbm, q_ref), (d_hbm, d_ref), (p_hbm, p_ref)))
    ]
    for copy in copies:
        copy.start()
    me = lax.axis_index("dp")
    role = role_of()
    for copy in copies:
        copy.wait()

    def fill(ref, values, ids):
        ref[:ROWS, :] = unit_rows(values)[0].astype(BF16)
        high = ids >> 7
        rows = lax.broadcasted_iota(jnp.int32, (PAD, ROWS), 0)
        tail = jnp.where(rows == 0, high, jnp.where(rows == 1, ids - high * 128, 0))
        ref[ROWS:, :] = jnp.zeros((PAD, WIDTH), BF16)
        ref[ROWS:, :ROWS] = tail.astype(F32).astype(BF16)

    mine = me * ROWS + lax.broadcasted_iota(jnp.int32, (1, ROWS), 1)

    @pl.when(role == 0)
    def _():
        fill(keep_ref, q_ref[...], p_ref[...])
        fill(send_ref, d_ref[...], mine)

    @pl.when(role == 1)
    def _():
        fill(keep_ref, d_ref[...], mine)
        fill(send_ref, q_ref[...], p_ref[...])


def join_kernel(keep_ref, come_ref, own_ref):
    def fill(low, high):
        own_ref[:ROWS, :] = low[:ROWS, :]
        own_ref[ROWS:BLOCK, :] = high[:ROWS, :]
        own_ref[BLOCK:, :] = jnp.zeros((PAD, WIDTH), BF16)
        own_ref[BLOCK:, :ROWS] = low[ROWS:, :ROWS]
        own_ref[BLOCK:, ROWS:BLOCK] = high[ROWS:, :ROWS]

    role = role_of()

    @pl.when(role == 0)
    def _():
        fill(keep_ref, come_ref)

    @pl.when(role == 1)
    def _():
        fill(come_ref, keep_ref)


def place_in_cube():
    me = lax.axis_index("dp")
    return ((me >> 5) & 1) * 4 + ((me >> 3) & 1) * 2 + ((me >> 1) & 1)


def pack_kernel(*refs):
    for n, ref in enumerate(refs[:-1]):
        refs[-1][n * SPAN : (n + 1) * SPAN, :] = ref[...]


def packs_of(columns):
    used = [pack for pack in PACKS if set(pack) & set(columns)]
    return used, [
        (p, pack.index(number) * SPAN) for number in columns for p, pack in enumerate(used) if number in pack
    ]


def has(part, row, column):
    rows, columns, known = PARTS[part]
    return row in rows and column in columns and not (row in known and column in known)


def tile_kernel(part, *refs):
    rows, columns, _ = PARTS[part]
    last = part == len(PARTS) - 1
    used, where = packs_of(columns)
    x, refs = refs[: len(rows)], refs[len(rows) :]
    y, refs = refs[: len(used)], refs[len(used) :]
    if last:
        before, (e_ref, stats_ref, rowsum_ref, colsum_ref) = refs[: 2 * part], refs[2 * part :]
        before = [(before[2 * n], before[2 * n + 1]) for n in range(part)]
    else:
        e_ref, rowsum_ref, colsum_ref = refs
    ids_of_columns = [row_ids(y[p], at) for p, at in where]
    begun = set()
    for i, number in enumerate(rows):
        ids = down_rows(row_ids(x[i]), BLOCK)
        partial = None
        for k, (p, start) in enumerate(where):
            if not has(part, number, columns[k]):
                continue
            dots = lax.dot_general(
                x[i][:BLOCK, :],
                y[p][start : start + BLOCK, :],
                (((1,), (1,)), ((), ())),
                preferred_element_type=F32,
            )
            e = jnp.exp2(dots * (20.0 * LOG2E) - 20.0 * LOG2E)
            at = slice(k * BLOCK, (k + 1) * BLOCK)
            e_ref[i * BLOCK : (i + 1) * BLOCK, at] = e
            for h in range(PER):
                piece = e[:, h * 128 : (h + 1) * 128]
                partial = piece if partial is None else partial + piece
            hit = jnp.where(ids == ids_of_columns[k], dots, 0.0)
            for n, value in enumerate((e, hit)):
                value = jnp.sum(value.reshape(BLOCK // 8, 8, BLOCK), axis=0)
                to = slice(n * 8, n * 8 + 8)
                colsum_ref[to, at] = colsum_ref[to, at] + value if k in begun else value
            begun.add(k)
        rowsum_ref[i * BLOCK : (i + 1) * BLOCK, :] = partial

    if last:
        place = place_in_cube()
        sums = before + [(rowsum_ref, colsum_ref)]

        def put(n, number, row):
            at = (place ^ number) * PER + n * HALF
            for h in range(PER):
                for g in range(CUBE):
                    stats_ref[g, pl.ds(at + h, 1), :] = row[:, h * 128 : (h + 1) * 128]

        @pl.when(role_of() == 0)
        def _():
            for number in ALL:
                total = None
                for (these, _, _), (ref, _) in zip(PARTS, sums):
                    if number in these:
                        at = these.index(number) * BLOCK
                        piece = ref[at : at + BLOCK, :]
                        total = piece if total is None else total + piece
                put(0, number, jnp.sum(jnp.transpose(total), axis=0, keepdims=True))
                put(1, number, jnp.zeros((1, BLOCK), F32))

        @pl.when(role_of() == 1)
        def _():
            for number in ALL:
                for n in range(2):
                    total = None
                    for (_, these, _), (_, ref) in zip(PARTS, sums):
                        if number in these:
                            at = these.index(number) * BLOCK
                            piece = ref[n * 8 : n * 8 + 8, at : at + BLOCK]
                            total = piece if total is None else total + piece
                    put(n, number, jnp.sum(total, axis=0, keepdims=True))


def encode(out_ref, value, digits):
    largest = None
    for h in range(WIDTH // 128):
        piece = jnp.abs(value[:, h * 128 : (h + 1) * 128])
        largest = piece if largest is None else jnp.maximum(largest, piece)
    largest = jnp.max(jnp.transpose(largest), axis=0, keepdims=True)
    power = jnp.ceil(jnp.log2(jnp.maximum(largest, 1e-35)) * 128.0)
    steps = value * down_rows(FULL * jnp.exp2(power * (-1.0 / 128.0)), WIDTH)
    out_ref[:BLOCK, :] = jnp.floor(steps + 0.5).astype(jnp.int32).astype(jnp.int16)
    at = lax.broadcasted_iota(jnp.int32, (PAD, BLOCK), 0)
    lane = lax.broadcasted_iota(jnp.int32, (PAD, BLOCK), 1)
    tail = jnp.where(at == 0, jnp.broadcast_to(power, (PAD, BLOCK)), 0.0)
    for n, digit in enumerate(digits):
        tail = jnp.where((at == 1) & (lane == n), digit, tail)
    out_ref[BLOCK:, :] = jnp.zeros((PAD, WIDTH), jnp.int16)
    out_ref[BLOCK:, :BLOCK] = tail.astype(jnp.int32).astype(jnp.int16)


def decode(ref):
    tail = ref[BLOCK:, :BLOCK].astype(jnp.int32).astype(F32)
    scale = down_rows(jnp.exp2(tail[0:1, :] * (1.0 / 128.0)) * (1.0 / FULL), WIDTH)
    return ref[:BLOCK, :].astype(jnp.int32).astype(F32) * scale


def digits_of(loss):
    high = jnp.floor(loss * (1.0 / 16.0))
    rest = (loss - high * 16.0) * 1024.0
    middle = jnp.floor(rest)
    low = jnp.floor((rest - middle) * 16384.0)
    return high, middle, low


def loss_of(ref):
    tail = ref[BLOCK:, :BLOCK].astype(jnp.int32).astype(F32)[1:2, :]
    lane = lax.broadcasted_iota(jnp.int32, (1, BLOCK), 1)
    unit = jnp.where(lane == 0, 16.0, jnp.where(lane == 1, 1.0 / 1024.0, 1.0 / (1024.0 * 16384.0)))
    return jnp.sum(jnp.where(lane < 3, tail * unit, 0.0))


def scale_kernel(stats_ref, out_ref):
    total = jnp.sum(stats_ref[:, :HALF, :], axis=0)
    out_ref[:HALF, :] = 1.0 / total
    lse = 20.0 + jnp.log(total)
    picked = 20.0 * jnp.sum(stats_ref[:, HALF:, :], axis=0)
    out_ref[HALF:, :] = jnp.full((8, 128), jnp.sum(lse - picked), F32)


def grad_kernel(number, coded, *refs):
    exps, refs = refs[: len(PARTS)], refs[len(PARTS) :]
    y, refs = refs[: len(PACKS)], refs[len(PACKS) :]
    scale_ref, x_ref, come, out_ref = refs[0], refs[1], refs[2:-1], refs[-1]
    place = place_in_cube()
    role = role_of()
    loss = scale_ref[HALF, 0]
    _, where = packs_of(ALL)

    def scale_of(block):
        at = (place ^ block) * PER
        return jnp.concatenate([scale_ref[pl.ds(at + h, 1), :] for h in range(PER)], axis=1)

    ids = down_rows(row_ids(x_ref), BLOCK)
    down = down_rows(jnp.where(role == 0, scale_of(number), 1.0), BLOCK)
    acc = None
    for column, (p, start) in zip(ALL, where):
        (e,) = [
            ref[
                rows.index(number) * BLOCK : (rows.index(number) + 1) * BLOCK,
                columns.index(column) * BLOCK : (columns.index(column) + 1) * BLOCK,
            ]
            for part, ((rows, columns, _), ref) in enumerate(zip(PARTS, exps))
            if has(part, number, column)
        ]
        along = jnp.where(role == 1, scale_of(column), 1.0)
        hit = jnp.where(ids == row_ids(y[p], start), 1.0, 0.0)
        weights = (e * down * along - hit).astype(BF16)
        piece = jnp.dot(weights, y[p][start : start + BLOCK, :], preferred_element_type=F32)
        acc = piece if acc is None else acc + piece
    value = 20.0 * acc
    for ref in come:
        value = value + decode(ref)
        loss = loss + loss_of(ref)
    if coded:
        encode(out_ref, value, digits_of(loss))
    else:
        out_ref[:BLOCK, :] = value
        out_ref[BLOCK:, :] = jnp.full((LOSS, WIDTH), loss, F32)


def split_kernel(own_ref, a_ref, b_ref, c_ref, d_ref, keep_ref, send_ref):
    value, loss = own_ref[:BLOCK, :], own_ref[BLOCK, 0]
    for ref in (a_ref, b_ref, c_ref, d_ref):
        value = value + decode(ref)
        loss = loss + loss_of(ref)
    role = role_of()
    keep_ref[ROWS:, :] = jnp.full((LOSS, WIDTH), loss, F32)
    send_ref[ROWS:, :] = jnp.full((LOSS, WIDTH), loss, F32)

    @pl.when(role == 0)
    def _():
        keep_ref[:ROWS, :] = value[:ROWS, :]
        send_ref[:ROWS, :] = value[ROWS:, :]

    @pl.when(role == 1)
    def _():
        keep_ref[:ROWS, :] = value[ROWS:, :]
        send_ref[:ROWS, :] = value[:ROWS, :]


def post_kernel(q_ref, d_ref, keep_ref, come_ref, loss_ref, gq_ref, gd_ref):
    def project(out_ref, grad, values):
        unit, length = unit_rows(values)
        out_ref[...] = (grad - jnp.sum(grad * unit, axis=1, keepdims=True) * unit) / length

    def fill(gq, gd):
        project(gq_ref, gq[:ROWS, :], q_ref[...])
        project(gd_ref, gd[:ROWS, :], d_ref[...])
        loss_ref[...] = gd[ROWS : ROWS + 1, 0:1] * (1.0 / 16384)

    role = role_of()

    @pl.when(role == 0)
    def _():
        fill(keep_ref, come_ref)

    @pl.when(role == 1)
    def _():
        fill(come_ref, keep_ref)


def local(queries, documents, positives):
    piece = pltpu.VMEM((ROWS + PAD, WIDTH), BF16)
    raw = [queries, documents, positives.reshape(1, ROWS)]
    keep, give = pl.pallas_call(
        pre_kernel,
        name="pre",
        in_specs=[pl.BlockSpec(memory_space=pltpu.HBM)] * 3,
        out_shape=[piece, piece],
        scratch_shapes=[
            pltpu.VMEM((ROWS, WIDTH), BF16),
            pltpu.VMEM((ROWS, WIDTH), BF16),
            pltpu.VMEM((1, ROWS), jnp.int32),
            pltpu.SemaphoreType.DMA((3,)),
        ],
        compiler_params=pltpu.CompilerParams(vmem_limit_bytes=8 * 1024 * 1024),
    )(*[pltpu.with_memory_space_constraint(v, pltpu.HBM) for v in raw])
    come = swap(give)
    own = call(join_kernel, "join", pltpu.VMEM((SPAN, WIDTH), BF16), near(keep), near(come))

    def pack(blocks, name, after=()):
        shape = pltpu.VMEM((len(blocks) * SPAN, WIDTH), BF16)
        return call(pack_kernel, name, shape, *[near(x[n]) for n in blocks], after=after)

    x = {0: own}
    x[7] = send(own, 7)
    for bits in (4, 2, 1):
        x[bits] = send(own, bits)
    x[3] = send(x[1], 2)
    x[6] = send(x[2], 4)
    x[5] = send(x[4], 1)
    y = [swap(pack(NEAR, "pack_near"))]
    parts = []

    def tile(part, name, after=()):
        rows, columns, _ = PARTS[part]
        used, _ = packs_of(columns)
        last = part == len(PARTS) - 1
        e = pltpu.VMEM((len(rows) * BLOCK, len(columns) * BLOCK), F32)
        sums = [pltpu.VMEM((len(rows) * BLOCK, 128), F32), pltpu.VMEM((16, len(columns) * BLOCK), F32)]
        before = [near(v) for done in parts for v in done[1:]] if last else []
        parts.append(
            call(
                functools.partial(tile_kernel, part),
                name,
                [e, pltpu.VMEM((CUBE, 2 * HALF, 128), F32)] if last else [e, *sums],
                *[near(x[n]) for n in rows],
                *[near(y[PACKS.index(pack)]) for pack in used],
                *before,
                scratch=sums if last else [],
                after=after,
            )
        )

    tile(0, "tile_0")
    y.append(swap(pack(FAR[:2], "pack_first", after=[parts[0][1]])))
    y.append(swap(pack(FAR[2:], "pack_second")))
    tile(1, "tile_1", [parts[0][1]])
    tile(2, "tile_2", [parts[1][1]])
    tile(3, "tile_3")
    stats = lax.all_to_all(parts[-1][1], "dp", 0, 0, axis_index_groups=SUM_GROUPS, tiled=True)
    scales = call(scale_kernel, "scales", pltpu.VMEM((HALF + 8, 128), F32), near(stats))

    coded = pltpu.VMEM((SPAN, WIDTH), jnp.int16)
    plain = pltpu.VMEM((BLOCK + LOSS, WIDTH), F32)

    def grad(number, *come, after=(), shape=coded):
        return call(
            functools.partial(grad_kernel, number, shape is coded),
            f"grad_{number}",
            shape,
            *[near(v[0]) for v in parts],
            *[near(v) for v in y],
            near(scales),
            near(x[number]),
            *[near(v) for v in come],
            after=after,
        )

    g3 = grad(3)
    r3 = send(g3, 2)
    g6 = grad(6)
    r6 = send(g6, 4)
    g5 = grad(5)
    r5 = send(g5, 1)
    g7 = grad(7)
    r7 = send(g7, 7)
    g1 = grad(1, r3)
    r1 = send(g1, 1)
    g2 = grad(2, r6)
    r2 = send(g2, 2)
    g4 = grad(4, r5)
    r4 = send(g4, 4)
    g0 = grad(0, shape=plain)
    part = pltpu.VMEM((ROWS + LOSS, WIDTH), F32)
    keep, give = call(split_kernel, "split", [part, part], *[near(v) for v in (g0, r7, r1, r2, r4)])
    come = swap(give)
    loss, gq, gd = call(
        post_kernel,
        "post",
        [
            jax.ShapeDtypeStruct((1, 1), F32),
            jax.ShapeDtypeStruct((ROWS, WIDTH), F32),
            jax.ShapeDtypeStruct((ROWS, WIDTH), F32),
        ],
        queries,
        documents,
        near(keep),
        near(come),
    )
    return (loss.reshape(()), gq, gd)


def solution(mesh):
    placed = (P("dp", None), P("dp", None), P("dp"))
    return jax.shard_map(
        local,
        mesh=mesh,
        in_specs=placed,
        out_specs=(P(), P("dp", None), P("dp", None)),
        check_vma=False,
    )
```

```python
import functools

import jax
import jax.numpy as jnp
from jax import lax
from jax.experimental import pallas as pl
from jax.experimental.pallas import tpu as pltpu
from jax.sharding import PartitionSpec as P

PAIRS_A = ((0, 1), (2, 3))
PAIRS_B = ((0, 3), (1, 2))
CUBE = 8
CORES = 2
ROWS = 128
BLOCK = CORES * ROWS
SIDE = CUBE * BLOCK
WIDTH = 768
PAD = 16
LOSS = 8
PER = BLOCK // 128
HALF = CUBE * PER
LOG2E = 1.4426950408889634
FULL = 32760.0
NEAR = (0, 4, 2, 1)
FAR = (7, 5, 3, 6)
PACKS = (NEAR, FAR[:2], FAR[2:])
ALL = NEAR + FAR
PARTS = (
    (NEAR, NEAR, ()),
    (FAR[:2], NEAR, ()),
    (NEAR + FAR[:2], FAR[:2], ()),
    (FAR[2:], NEAR + FAR[:2], ()),
    (ALL, FAR[2:], ()),
)
SPAN = BLOCK + PAD
F32 = jnp.float32
BF16 = jnp.bfloat16


def device_index(x, z, y, core):
    return ((x * 4 + z) * 4 + y) * CORES + core


def partners(bits):
    moves = []
    for x in range(4):
        for z in range(4):
            for y in range(4):
                for core in range(CORES):
                    flip = (lambda v: v ^ 1) if core == 0 else (lambda v: 3 - v)
                    to = [flip(v) if bits & bit else v for v, bit in ((x, 4), (z, 2), (y, 1))]
                    moves.append((device_index(x, z, y, core), device_index(*to, core)))
    return moves


def a_cubes():
    return [
        [device_index(x, z, y, core) for x in px for z in pz for y in py]
        for core in range(CORES)
        for px in PAIRS_A
        for pz in PAIRS_A
        for py in PAIRS_A
    ]


SWAP = [(i, i ^ 1) for i in range(128)]
SUM_GROUPS = a_cubes()


def send(value, bits):
    return lax.ppermute(value, "dp", partners(bits))


def swap(value):
    return lax.ppermute(value, "dp", SWAP)


def near(value):
    return pltpu.with_memory_space_constraint(value, pltpu.VMEM)


def call(kernel, name, out_shape, *args, scratch=(), after=()):
    n = len(args)

    def body(*refs):
        kernel(*refs[:n], *refs[n + len(after) :])

    return pl.pallas_call(
        body,
        name=name,
        out_shape=out_shape,
        scratch_shapes=scratch,
        compiler_params=pltpu.CompilerParams(vmem_limit_bytes=8 * 1024 * 1024),
    )(*args, *[near(v) for v in after])


def role_of():
    return lax.axis_index("dp") & 1


def unit_rows(values):
    wide = values.astype(F32)
    length = jnp.sqrt(jnp.sum(wide * wide, axis=1, keepdims=True) + 1e-06)
    return wide / length, length


def row_ids(ref, at=0):
    tail = ref[at + BLOCK : at + SPAN, :BLOCK].astype(F32)
    return tail[0:1, :] * 128.0 + tail[1:2, :]


def down_rows(row, width):
    wide = jnp.transpose(jnp.broadcast_to(row, (128, row.shape[1])))
    return jnp.concatenate([wide] * (width // 128), axis=1)


def pre_kernel(q_hbm, d_hbm, p_hbm, keep_ref, send_ref, q_ref, d_ref, p_ref, sems):
    copies = [
        pltpu.make_async_copy(src, dst, sems.at[n])
        for n, (src, dst) in enumerate(((q_hbm, q_ref), (d_hbm, d_ref), (p_hbm, p_ref)))
    ]
    for copy in copies:
        copy.start()
    me = lax.axis_index("dp")
    role = role_of()
    for copy in copies:
        copy.wait()

    def fill(ref, values, ids):
        ref[:ROWS, :] = unit_rows(values)[0].astype(BF16)
        high = ids >> 7
        rows = lax.broadcasted_iota(jnp.int32, (PAD, ROWS), 0)
        tail = jnp.where(rows == 0, high, jnp.where(rows == 1, ids - high * 128, 0))
        ref[ROWS:, :] = jnp.zeros((PAD, WIDTH), BF16)
        ref[ROWS:, :ROWS] = tail.astype(F32).astype(BF16)

    mine = me * ROWS + lax.broadcasted_iota(jnp.int32, (1, ROWS), 1)

    @pl.when(role == 0)
    def _():
        fill(keep_ref, q_ref[...], p_ref[...])
        fill(send_ref, d_ref[...], mine)

    @pl.when(role == 1)
    def _():
        fill(keep_ref, d_ref[...], mine)
        fill(send_ref, q_ref[...], p_ref[...])


def join_kernel(keep_ref, come_ref, own_ref):
    def fill(low, high):
        own_ref[:ROWS, :] = low[:ROWS, :]
        own_ref[ROWS:BLOCK, :] = high[:ROWS, :]
        own_ref[BLOCK:, :] = jnp.zeros((PAD, WIDTH), BF16)
        own_ref[BLOCK:, :ROWS] = low[ROWS:, :ROWS]
        own_ref[BLOCK:, ROWS:BLOCK] = high[ROWS:, :ROWS]

    role = role_of()

    @pl.when(role == 0)
    def _():
        fill(keep_ref, come_ref)

    @pl.when(role == 1)
    def _():
        fill(come_ref, keep_ref)


def place_in_cube():
    me = lax.axis_index("dp")
    return ((me >> 5) & 1) * 4 + ((me >> 3) & 1) * 2 + ((me >> 1) & 1)


def pack_kernel(*refs):
    for n, ref in enumerate(refs[:-1]):
        refs[-1][n * SPAN : (n + 1) * SPAN, :] = ref[...]


def packs_of(columns):
    used = [pack for pack in PACKS if set(pack) & set(columns)]
    return used, [
        (p, pack.index(number) * SPAN) for number in columns for p, pack in enumerate(used) if number in pack
    ]


def has(part, row, column):
    rows, columns, known = PARTS[part]
    return row in rows and column in columns and not (row in known and column in known)


def tile_kernel(part, *refs):
    rows, columns, _ = PARTS[part]
    last = part == len(PARTS) - 1
    used, where = packs_of(columns)
    x, refs = refs[: len(rows)], refs[len(rows) :]
    y, refs = refs[: len(used)], refs[len(used) :]
    if last:
        before, (e_ref, stats_ref, rowsum_ref, colsum_ref) = refs[: 2 * part], refs[2 * part :]
        before = [(before[2 * n], before[2 * n + 1]) for n in range(part)]
    else:
        e_ref, rowsum_ref, colsum_ref = refs
    ids_of_columns = [row_ids(y[p], at) for p, at in where]
    begun = set()
    for i, number in enumerate(rows):
        ids = down_rows(row_ids(x[i]), BLOCK)
        partial = None
        for k, (p, start) in enumerate(where):
            if not has(part, number, columns[k]):
                continue
            dots = lax.dot_general(
                x[i][:BLOCK, :],
                y[p][start : start + BLOCK, :],
                (((1,), (1,)), ((), ())),
                preferred_element_type=F32,
            )
            e = jnp.exp2(dots * (20.0 * LOG2E) - 20.0 * LOG2E)
            at = slice(k * BLOCK, (k + 1) * BLOCK)
            e_ref[i * BLOCK : (i + 1) * BLOCK, at] = e
            for h in range(PER):
                piece = e[:, h * 128 : (h + 1) * 128]
                partial = piece if partial is None else partial + piece
            hit = jnp.where(ids == ids_of_columns[k], dots, 0.0)
            for n, value in enumerate((e, hit)):
                value = jnp.sum(value.reshape(BLOCK // 8, 8, BLOCK), axis=0)
                to = slice(n * 8, n * 8 + 8)
                colsum_ref[to, at] = colsum_ref[to, at] + value if k in begun else value
            begun.add(k)
        rowsum_ref[i * BLOCK : (i + 1) * BLOCK, :] = partial

    if last:
        place = place_in_cube()
        sums = before + [(rowsum_ref, colsum_ref)]

        def put(n, number, row):
            at = (place ^ number) * PER + n * HALF
            for h in range(PER):
                for g in range(CUBE):
                    stats_ref[g, pl.ds(at + h, 1), :] = row[:, h * 128 : (h + 1) * 128]

        @pl.when(role_of() == 0)
        def _():
            for number in ALL:
                total = None
                for (these, _, _), (ref, _) in zip(PARTS, sums):
                    if number in these:
                        at = these.index(number) * BLOCK
                        piece = ref[at : at + BLOCK, :]
                        total = piece if total is None else total + piece
                put(0, number, jnp.sum(jnp.transpose(total), axis=0, keepdims=True))
                put(1, number, jnp.zeros((1, BLOCK), F32))

        @pl.when(role_of() == 1)
        def _():
            for number in ALL:
                for n in range(2):
                    total = None
                    for (_, these, _), (_, ref) in zip(PARTS, sums):
                        if number in these:
                            at = these.index(number) * BLOCK
                            piece = ref[n * 8 : n * 8 + 8, at : at + BLOCK]
                            total = piece if total is None else total + piece
                    put(n, number, jnp.sum(total, axis=0, keepdims=True))


def encode(out_ref, value, digits):
    largest = None
    for h in range(WIDTH // 128):
        piece = jnp.abs(value[:, h * 128 : (h + 1) * 128])
        largest = piece if largest is None else jnp.maximum(largest, piece)
    largest = jnp.max(jnp.transpose(largest), axis=0, keepdims=True)
    power = jnp.ceil(jnp.log2(jnp.maximum(largest, 1e-35)) * 128.0)
    steps = value * down_rows(FULL * jnp.exp2(power * (-1.0 / 128.0)), WIDTH)
    out_ref[:BLOCK, :] = jnp.floor(steps + 0.5).astype(jnp.int32).astype(jnp.int16)
    at = lax.broadcasted_iota(jnp.int32, (PAD, BLOCK), 0)
    lane = lax.broadcasted_iota(jnp.int32, (PAD, BLOCK), 1)
    tail = jnp.where(at == 0, jnp.broadcast_to(power, (PAD, BLOCK)), 0.0)
    for n, digit in enumerate(digits):
        tail = jnp.where((at == 1) & (lane == n), digit, tail)
    out_ref[BLOCK:, :] = jnp.zeros((PAD, WIDTH), jnp.int16)
    out_ref[BLOCK:, :BLOCK] = tail.astype(jnp.int32).astype(jnp.int16)


def decode(ref, at=slice(0, BLOCK)):
    tail = ref[BLOCK:, :BLOCK].astype(jnp.int32).astype(F32)
    scale = down_rows(jnp.exp2(tail[0:1, at] * (1.0 / 128.0)) * (1.0 / FULL), WIDTH)
    return ref[at, :].astype(jnp.int32).astype(F32) * scale


def digits_of(loss):
    high = jnp.floor(loss * (1.0 / 16.0))
    rest = (loss - high * 16.0) * 1024.0
    middle = jnp.floor(rest)
    low = jnp.floor((rest - middle) * 16384.0)
    return high, middle, low


def loss_of(ref):
    tail = ref[BLOCK:, :BLOCK].astype(jnp.int32).astype(F32)[1:2, :]
    lane = lax.broadcasted_iota(jnp.int32, (1, BLOCK), 1)
    unit = jnp.where(lane == 0, 16.0, jnp.where(lane == 1, 1.0 / 1024.0, 1.0 / (1024.0 * 16384.0)))
    return jnp.sum(jnp.where(lane < 3, tail * unit, 0.0))


def scale_kernel(stats_ref, out_ref):
    total = jnp.sum(stats_ref[:, :HALF, :], axis=0)
    out_ref[:HALF, :] = 1.0 / total
    lse = 20.0 + jnp.log(total)
    picked = 20.0 * jnp.sum(stats_ref[:, HALF:, :], axis=0)
    out_ref[HALF:, :] = jnp.full((8, 128), jnp.sum(lse - picked), F32)


def grad_kernel(number, coded, *refs):
    exps, refs = refs[: len(PARTS)], refs[len(PARTS) :]
    y, refs = refs[: len(PACKS)], refs[len(PACKS) :]
    scale_ref, x_ref, come, out_ref = refs[0], refs[1], refs[2:-1], refs[-1]
    place = place_in_cube()
    role = role_of()
    loss = scale_ref[HALF, 0]
    _, where = packs_of(ALL)

    def scale_of(block):
        at = (place ^ block) * PER
        return jnp.concatenate([scale_ref[pl.ds(at + h, 1), :] for h in range(PER)], axis=1)

    ids = down_rows(row_ids(x_ref), BLOCK)
    down = down_rows(jnp.where(role == 0, scale_of(number), 1.0), BLOCK)
    acc = None
    for column, (p, start) in zip(ALL, where):
        (e,) = [
            ref[
                rows.index(number) * BLOCK : (rows.index(number) + 1) * BLOCK,
                columns.index(column) * BLOCK : (columns.index(column) + 1) * BLOCK,
            ]
            for part, ((rows, columns, _), ref) in enumerate(zip(PARTS, exps))
            if has(part, number, column)
        ]
        along = jnp.where(role == 1, scale_of(column), 1.0)
        hit = jnp.where(ids == row_ids(y[p], start), 1.0, 0.0)
        weights = (e * down * along - hit).astype(BF16)
        piece = jnp.dot(weights, y[p][start : start + BLOCK, :], preferred_element_type=F32)
        acc = piece if acc is None else acc + piece
    value = 20.0 * acc
    for ref in come:
        value = value + decode(ref)
        loss = loss + loss_of(ref)
    if coded:
        encode(out_ref, value, digits_of(loss))
    else:
        out_ref[:BLOCK, :] = value
        out_ref[BLOCK:, :] = jnp.full((LOSS, WIDTH), loss, F32)


def split_kernel(own_ref, *refs):
    come, (keep_ref, send_ref) = refs[:-2], refs[-2:]
    value, loss = own_ref[:BLOCK, :], own_ref[BLOCK, 0]
    for ref in come:
        value = value + decode(ref)
        loss = loss + loss_of(ref)
    role = role_of()
    keep_ref[ROWS:, :] = jnp.full((LOSS, WIDTH), loss, F32)
    send_ref[ROWS:, :] = jnp.full((LOSS, WIDTH), loss, F32)

    @pl.when(role == 0)
    def _():
        keep_ref[:ROWS, :] = value[:ROWS, :]
        send_ref[:ROWS, :] = value[ROWS:, :]

    @pl.when(role == 1)
    def _():
        keep_ref[:ROWS, :] = value[ROWS:, :]
        send_ref[:ROWS, :] = value[:ROWS, :]


def post_kernel(q_ref, d_ref, keep_ref, come_ref, last_ref, other_ref, loss_ref, gq_ref, gd_ref):
    def project(out_ref, grad, values):
        unit, length = unit_rows(values)
        out_ref[...] = (grad - jnp.sum(grad * unit, axis=1, keepdims=True) * unit) / length

    def fill(gq, last_q, gd, last_d, half):
        at = slice(half * ROWS, (half + 1) * ROWS)
        project(gq_ref, gq[:ROWS, :] + decode(last_q, at), q_ref[...])
        project(gd_ref, gd[:ROWS, :] + decode(last_d, at), d_ref[...])
        loss_ref[...] = (gd[ROWS : ROWS + 1, 0:1] + loss_of(last_d)) * (1.0 / 16384)

    role = role_of()

    @pl.when(role == 0)
    def _():
        fill(keep_ref, last_ref, come_ref, other_ref, 0)

    @pl.when(role == 1)
    def _():
        fill(come_ref, other_ref, keep_ref, last_ref, 1)


def local(queries, documents, positives):
    piece = pltpu.VMEM((ROWS + PAD, WIDTH), BF16)
    raw = [queries, documents, positives.reshape(1, ROWS)]
    keep, give = pl.pallas_call(
        pre_kernel,
        name="pre",
        in_specs=[pl.BlockSpec(memory_space=pltpu.HBM)] * 3,
        out_shape=[piece, piece],
        scratch_shapes=[
            pltpu.VMEM((ROWS, WIDTH), BF16),
            pltpu.VMEM((ROWS, WIDTH), BF16),
            pltpu.VMEM((1, ROWS), jnp.int32),
            pltpu.SemaphoreType.DMA((3,)),
        ],
        compiler_params=pltpu.CompilerParams(vmem_limit_bytes=8 * 1024 * 1024),
    )(*[pltpu.with_memory_space_constraint(v, pltpu.HBM) for v in raw])
    come = swap(give)
    own = call(join_kernel, "join", pltpu.VMEM((SPAN, WIDTH), BF16), near(keep), near(come))

    def pack(blocks, name, after=()):
        shape = pltpu.VMEM((len(blocks) * SPAN, WIDTH), BF16)
        return call(pack_kernel, name, shape, *[near(x[n]) for n in blocks], after=after)

    x = {0: own}
    for bits in (4, 2, 1):
        x[bits] = send(own, bits)
    x[5] = send(x[4], 1)
    x[6] = send(x[2], 4)
    x[3] = send(x[1], 2)
    x[7] = send(x[1], 6)
    y = [swap(pack(NEAR, "pack_near"))]
    parts = []

    def tile(part, name, after=()):
        rows, columns, _ = PARTS[part]
        used, _ = packs_of(columns)
        last = part == len(PARTS) - 1
        e = pltpu.VMEM((len(rows) * BLOCK, len(columns) * BLOCK), F32)
        sums = [pltpu.VMEM((len(rows) * BLOCK, 128), F32), pltpu.VMEM((16, len(columns) * BLOCK), F32)]
        before = [near(v) for done in parts for v in done[1:]] if last else []
        parts.append(
            call(
                functools.partial(tile_kernel, part),
                name,
                [e, pltpu.VMEM((CUBE, 2 * HALF, 128), F32)] if last else [e, *sums],
                *[near(x[n]) for n in rows],
                *[near(y[PACKS.index(pack)]) for pack in used],
                *before,
                scratch=sums if last else [],
                after=after,
            )
        )

    tile(0, "tile_0", [])
    y.append(swap(pack(FAR[:2], "pack_first", after=[parts[0][1]])))
    tile(1, "tile_1", [parts[0][1]])
    tile(2, "tile_2", [parts[1][1]])
    y.append(swap(pack(FAR[2:], "pack_second", after=[parts[1][1]])))
    tile(3, "tile_3", [parts[2][1]])
    tile(4, "tile_4")
    stats = lax.all_to_all(parts[-1][1], "dp", 0, 0, axis_index_groups=SUM_GROUPS, tiled=True)
    scales = call(scale_kernel, "scales", pltpu.VMEM((HALF + 8, 128), F32), near(stats))

    coded = pltpu.VMEM((SPAN, WIDTH), jnp.int16)
    plain = pltpu.VMEM((BLOCK + LOSS, WIDTH), F32)

    def grad(number, *come, after=(), shape=coded):
        return call(
            functools.partial(grad_kernel, number, shape is coded),
            f"grad_{number}",
            shape,
            *[near(v[0]) for v in parts],
            *[near(v) for v in y],
            near(scales),
            near(x[number]),
            *[near(v) for v in come],
            after=after,
        )

    g3 = grad(3)
    r3 = send(g3, 2)
    g6 = grad(6)
    r6 = send(g6, 4)
    g5 = grad(5)
    r5 = send(g5, 1)
    g7 = grad(7)
    r7 = send(g7, 7)
    g1 = grad(1, r3)
    r1 = send(g1, 1)
    g2 = grad(2, r6)
    r2 = send(g2, 2)
    g4 = grad(4, r5)
    r4 = send(g4, 4)
    g0 = grad(0, shape=plain)
    part = pltpu.VMEM((ROWS + LOSS, WIDTH), F32)
    keep, give = call(split_kernel, "split", [part, part], *[near(v) for v in (g0, r7, r1, r2)])
    come = swap(give)
    other = swap(r4)
    loss, gq, gd = call(
        post_kernel,
        "post",
        [
            jax.ShapeDtypeStruct((1, 1), F32),
            jax.ShapeDtypeStruct((ROWS, WIDTH), F32),
            jax.ShapeDtypeStruct((ROWS, WIDTH), F32),
        ],
        queries,
        documents,
        *[near(v) for v in (keep, come, r4, other)],
    )
    return (loss.reshape(()), gq, gd)


def solution(mesh):
    placed = (P("dp", None), P("dp", None), P("dp"))
    return jax.shard_map(
        local,
        mesh=mesh,
        in_specs=placed,
        out_specs=(P(), P("dp", None), P("dp", None)),
        check_vma=False,
    )
```

```python
import functools

import jax
import jax.numpy as jnp
from jax import lax
from jax.experimental import pallas as pl
from jax.experimental.pallas import tpu as pltpu
from jax.sharding import PartitionSpec as P

PAIRS_A = ((0, 1), (2, 3))
PAIRS_B = ((0, 3), (1, 2))
CUBE = 8
CORES = 2
ROWS = 128
BLOCK = CORES * ROWS
SIDE = CUBE * BLOCK
WIDTH = 768
PAD = 16
LOSS = 8
PER = BLOCK // 128
HALF = CUBE * PER
LOG2E = 1.4426950408889634
FULL = 32760.0
NEAR = (0, 4, 2, 1)
FAR = (7, 5, 3, 6)
PACKS = (NEAR, FAR[:2], FAR[2:])
ALL = NEAR + FAR
PARTS = (
    (NEAR, NEAR, ()),
    (FAR[:2], NEAR, ()),
    (NEAR + FAR[:2], FAR[:2], ()),
    (FAR[2:], NEAR + FAR[:2], ()),
    (ALL, FAR[2:], ()),
)
SPAN = BLOCK + PAD
F32 = jnp.float32
BF16 = jnp.bfloat16


def device_index(x, z, y, core):
    return ((x * 4 + z) * 4 + y) * CORES + core


def partners(bits):
    moves = []
    for x in range(4):
        for z in range(4):
            for y in range(4):
                for core in range(CORES):
                    flip = (lambda v: v ^ 1) if core == 0 else (lambda v: 3 - v)
                    to = [flip(v) if bits & bit else v for v, bit in ((x, 4), (z, 2), (y, 1))]
                    moves.append((device_index(x, z, y, core), device_index(*to, core)))
    return moves


def a_cubes():
    return [
        [device_index(x, z, y, core) for x in px for z in pz for y in py]
        for core in range(CORES)
        for px in PAIRS_A
        for pz in PAIRS_A
        for py in PAIRS_A
    ]


SWAP = [(i, i ^ 1) for i in range(128)]
SUM_GROUPS = a_cubes()


def send(value, bits):
    return lax.ppermute(value, "dp", partners(bits))


def swap(value):
    return lax.ppermute(value, "dp", SWAP)


def near(value):
    return pltpu.with_memory_space_constraint(value, pltpu.VMEM)


def call(kernel, name, out_shape, *args, scratch=(), after=()):
    n = len(args)

    def body(*refs):
        kernel(*refs[:n], *refs[n + len(after) :])

    return pl.pallas_call(
        body,
        name=name,
        out_shape=out_shape,
        scratch_shapes=scratch,
        compiler_params=pltpu.CompilerParams(vmem_limit_bytes=8 * 1024 * 1024),
    )(*args, *[near(v) for v in after])


def role_of():
    return lax.axis_index("dp") & 1


def unit_rows(values):
    wide = values.astype(F32)
    length = jnp.sqrt(jnp.sum(wide * wide, axis=1, keepdims=True) + 1e-06)
    return wide / length, length


def row_ids(ref, at=0):
    tail = ref[at + BLOCK : at + SPAN, :BLOCK].astype(F32)
    return tail[0:1, :] * 128.0 + tail[1:2, :]


def down_rows(row, width):
    wide = jnp.transpose(jnp.broadcast_to(row, (128, row.shape[1])))
    return jnp.concatenate([wide] * (width // 128), axis=1)


def pre_kernel(q_hbm, d_hbm, p_hbm, keep_ref, send_ref, q_ref, d_ref, p_ref, sems):
    copies = [
        pltpu.make_async_copy(src, dst, sems.at[n])
        for n, (src, dst) in enumerate(((q_hbm, q_ref), (d_hbm, d_ref), (p_hbm, p_ref)))
    ]
    for copy in copies:
        copy.start()
    me = lax.axis_index("dp")
    role = role_of()
    for copy in copies:
        copy.wait()

    def fill(ref, values, ids):
        ref[:ROWS, :] = unit_rows(values)[0].astype(BF16)
        high = ids >> 7
        rows = lax.broadcasted_iota(jnp.int32, (PAD, ROWS), 0)
        tail = jnp.where(rows == 0, high, jnp.where(rows == 1, ids - high * 128, 0))
        ref[ROWS:, :] = jnp.zeros((PAD, WIDTH), BF16)
        ref[ROWS:, :ROWS] = tail.astype(F32).astype(BF16)

    mine = me * ROWS + lax.broadcasted_iota(jnp.int32, (1, ROWS), 1)

    @pl.when(role == 0)
    def _():
        fill(keep_ref, q_ref[...], p_ref[...])
        fill(send_ref, d_ref[...], mine)

    @pl.when(role == 1)
    def _():
        fill(keep_ref, d_ref[...], mine)
        fill(send_ref, q_ref[...], p_ref[...])


def join_kernel(keep_ref, come_ref, own_ref):
    def fill(low, high):
        own_ref[:ROWS, :] = low[:ROWS, :]
        own_ref[ROWS:BLOCK, :] = high[:ROWS, :]
        own_ref[BLOCK:, :] = jnp.zeros((PAD, WIDTH), BF16)
        own_ref[BLOCK:, :ROWS] = low[ROWS:, :ROWS]
        own_ref[BLOCK:, ROWS:BLOCK] = high[ROWS:, :ROWS]

    role = role_of()

    @pl.when(role == 0)
    def _():
        fill(keep_ref, come_ref)

    @pl.when(role == 1)
    def _():
        fill(come_ref, keep_ref)


def place_in_cube():
    me = lax.axis_index("dp")
    return ((me >> 5) & 1) * 4 + ((me >> 3) & 1) * 2 + ((me >> 1) & 1)


def pack_kernel(*refs):
    for n, ref in enumerate(refs[:-1]):
        refs[-1][n * SPAN : (n + 1) * SPAN, :] = ref[...]


def packs_of(columns):
    used = [pack for pack in PACKS if set(pack) & set(columns)]
    return used, [
        (p, pack.index(number) * SPAN) for number in columns for p, pack in enumerate(used) if number in pack
    ]


def has(part, row, column):
    rows, columns, known = PARTS[part]
    return row in rows and column in columns and not (row in known and column in known)


def tile_kernel(part, *refs):
    rows, columns, _ = PARTS[part]
    last = part == len(PARTS) - 1
    used, where = packs_of(columns)
    x, refs = refs[: len(rows)], refs[len(rows) :]
    y, refs = refs[: len(used)], refs[len(used) :]
    if last:
        before, (e_ref, stats_ref, rowsum_ref, colsum_ref) = refs[: 2 * part], refs[2 * part :]
        before = [(before[2 * n], before[2 * n + 1]) for n in range(part)]
    else:
        e_ref, rowsum_ref, colsum_ref = refs
    ids_of_columns = [row_ids(y[p], at) for p, at in where]
    begun = set()
    for i, number in enumerate(rows):
        ids = down_rows(row_ids(x[i]), BLOCK)
        partial = None
        for k, (p, start) in enumerate(where):
            if not has(part, number, columns[k]):
                continue
            dots = lax.dot_general(
                x[i][:BLOCK, :],
                y[p][start : start + BLOCK, :],
                (((1,), (1,)), ((), ())),
                preferred_element_type=F32,
            )
            e = jnp.exp2(dots * (20.0 * LOG2E) - 20.0 * LOG2E)
            at = slice(k * BLOCK, (k + 1) * BLOCK)
            e_ref[i * BLOCK : (i + 1) * BLOCK, at] = e
            for h in range(PER):
                piece = e[:, h * 128 : (h + 1) * 128]
                partial = piece if partial is None else partial + piece
            hit = jnp.where(ids == ids_of_columns[k], dots, 0.0)
            for n, value in enumerate((e, hit)):
                value = jnp.sum(value.reshape(BLOCK // 8, 8, BLOCK), axis=0)
                to = slice(n * 8, n * 8 + 8)
                colsum_ref[to, at] = colsum_ref[to, at] + value if k in begun else value
            begun.add(k)
        rowsum_ref[i * BLOCK : (i + 1) * BLOCK, :] = partial

    if last:
        place = place_in_cube()
        sums = before + [(rowsum_ref, colsum_ref)]

        def put(n, number, row):
            at = (place ^ number) * PER + n * HALF
            for h in range(PER):
                for g in range(CUBE):
                    stats_ref[g, pl.ds(at + h, 1), :] = row[:, h * 128 : (h + 1) * 128]

        @pl.when(role_of() == 0)
        def _():
            for number in ALL:
                total = None
                for (these, _, _), (ref, _) in zip(PARTS, sums):
                    if number in these:
                        at = these.index(number) * BLOCK
                        piece = ref[at : at + BLOCK, :]
                        total = piece if total is None else total + piece
                put(0, number, jnp.sum(jnp.transpose(total), axis=0, keepdims=True))
                put(1, number, jnp.zeros((1, BLOCK), F32))

        @pl.when(role_of() == 1)
        def _():
            for number in ALL:
                for n in range(2):
                    total = None
                    for (_, these, _), (_, ref) in zip(PARTS, sums):
                        if number in these:
                            at = these.index(number) * BLOCK
                            piece = ref[n * 8 : n * 8 + 8, at : at + BLOCK]
                            total = piece if total is None else total + piece
                    put(n, number, jnp.sum(total, axis=0, keepdims=True))


def encode(out_ref, value, digits):
    largest = None
    for h in range(WIDTH // 128):
        piece = jnp.abs(value[:, h * 128 : (h + 1) * 128])
        largest = piece if largest is None else jnp.maximum(largest, piece)
    largest = jnp.max(largest, axis=1, keepdims=True)
    power = jnp.ceil(jnp.log2(jnp.maximum(largest, 1e-35)) * 128.0)
    steps = value * (FULL * jnp.exp2(power * (-1.0 / 128.0)))
    out_ref[:BLOCK, :] = jnp.floor(steps + 0.5).astype(jnp.int32).astype(jnp.int16)
    at = lax.broadcasted_iota(jnp.int32, (PAD, BLOCK), 0)
    lane = lax.broadcasted_iota(jnp.int32, (PAD, BLOCK), 1)
    power = jnp.transpose(jnp.broadcast_to(power, (BLOCK, 128)))[:PAD, :]
    tail = jnp.where(at == 0, power, 0.0)
    for n, digit in enumerate(digits):
        tail = jnp.where((at == 1) & (lane == n), digit, tail)
    out_ref[BLOCK:, :] = jnp.zeros((PAD, WIDTH), jnp.int16)
    out_ref[BLOCK:, :BLOCK] = tail.astype(jnp.int32).astype(jnp.int16)


def decode(ref, at=slice(0, BLOCK)):
    tail = ref[BLOCK:, :BLOCK].astype(jnp.int32).astype(F32)
    scale = down_rows(jnp.exp2(tail[0:1, at] * (1.0 / 128.0)) * (1.0 / FULL), WIDTH)
    return ref[at, :].astype(jnp.int32).astype(F32) * scale


def digits_of(loss):
    high = jnp.floor(loss * (1.0 / 16.0))
    rest = (loss - high * 16.0) * 1024.0
    middle = jnp.floor(rest)
    low = jnp.floor((rest - middle) * 16384.0)
    return high, middle, low


def loss_of(ref):
    tail = ref[BLOCK:, :BLOCK].astype(jnp.int32).astype(F32)[1:2, :]
    lane = lax.broadcasted_iota(jnp.int32, (1, BLOCK), 1)
    unit = jnp.where(lane == 0, 16.0, jnp.where(lane == 1, 1.0 / 1024.0, 1.0 / (1024.0 * 16384.0)))
    return jnp.sum(jnp.where(lane < 3, tail * unit, 0.0))


def scale_kernel(stats_ref, out_ref):
    total = jnp.sum(stats_ref[:, :HALF, :], axis=0)
    out_ref[:HALF, :] = 1.0 / total
    lse = 20.0 + jnp.log(total)
    picked = 20.0 * jnp.sum(stats_ref[:, HALF:, :], axis=0)
    out_ref[HALF:, :] = jnp.full((8, 128), jnp.sum(lse - picked), F32)


def grad_kernel(number, coded, *refs):
    exps, refs = refs[: len(PARTS)], refs[len(PARTS) :]
    y, refs = refs[: len(PACKS)], refs[len(PACKS) :]
    scale_ref, x_ref, come, out_ref = refs[0], refs[1], refs[2:-1], refs[-1]
    place = place_in_cube()
    role = role_of()
    loss = scale_ref[HALF, 0]
    _, where = packs_of(ALL)

    def scale_of(block):
        at = (place ^ block) * PER
        return jnp.concatenate([scale_ref[pl.ds(at + h, 1), :] for h in range(PER)], axis=1)

    ids = down_rows(row_ids(x_ref), BLOCK)
    down = down_rows(jnp.where(role == 0, scale_of(number), 1.0), BLOCK)
    acc = None
    for column, (p, start) in zip(ALL, where):
        (e,) = [
            ref[
                rows.index(number) * BLOCK : (rows.index(number) + 1) * BLOCK,
                columns.index(column) * BLOCK : (columns.index(column) + 1) * BLOCK,
            ]
            for part, ((rows, columns, _), ref) in enumerate(zip(PARTS, exps))
            if has(part, number, column)
        ]
        along = jnp.where(role == 1, scale_of(column), 1.0)
        hit = jnp.where(ids == row_ids(y[p], start), 1.0, 0.0)
        weights = (e * down * along - hit).astype(BF16)
        piece = jnp.dot(weights, y[p][start : start + BLOCK, :], preferred_element_type=F32)
        acc = piece if acc is None else acc + piece
    value = 20.0 * acc
    for ref in come:
        value = value + decode(ref)
        loss = loss + loss_of(ref)
    if coded:
        encode(out_ref, value, digits_of(loss))
    else:
        out_ref[:BLOCK, :] = value
        out_ref[BLOCK:, :] = jnp.full((LOSS, WIDTH), loss, F32)


def split_kernel(own_ref, *refs):
    come, (keep_ref, send_ref) = refs[:-2], refs[-2:]
    value, loss = own_ref[:BLOCK, :], own_ref[BLOCK, 0]
    for ref in come:
        value = value + decode(ref)
        loss = loss + loss_of(ref)
    role = role_of()
    keep_ref[ROWS:, :] = jnp.full((LOSS, WIDTH), loss, F32)
    send_ref[ROWS:, :] = jnp.full((LOSS, WIDTH), loss, F32)

    @pl.when(role == 0)
    def _():
        keep_ref[:ROWS, :] = value[:ROWS, :]
        send_ref[:ROWS, :] = value[ROWS:, :]

    @pl.when(role == 1)
    def _():
        keep_ref[:ROWS, :] = value[ROWS:, :]
        send_ref[:ROWS, :] = value[:ROWS, :]


def post_kernel(q_ref, d_ref, keep_ref, come_ref, last_ref, other_ref, loss_ref, gq_ref, gd_ref):
    def project(out_ref, grad, values):
        unit, length = unit_rows(values)
        out_ref[...] = (grad - jnp.sum(grad * unit, axis=1, keepdims=True) * unit) / length

    def fill(gq, last_q, gd, last_d, half):
        at = slice(half * ROWS, (half + 1) * ROWS)
        project(gq_ref, gq[:ROWS, :] + decode(last_q, at), q_ref[...])
        project(gd_ref, gd[:ROWS, :] + decode(last_d, at), d_ref[...])
        loss_ref[...] = (gd[ROWS : ROWS + 1, 0:1] + loss_of(last_d)) * (1.0 / 16384)

    role = role_of()

    @pl.when(role == 0)
    def _():
        fill(keep_ref, last_ref, come_ref, other_ref, 0)

    @pl.when(role == 1)
    def _():
        fill(come_ref, other_ref, keep_ref, last_ref, 1)


def local(queries, documents, positives):
    piece = pltpu.VMEM((ROWS + PAD, WIDTH), BF16)
    raw = [queries, documents, positives.reshape(1, ROWS)]
    keep, give = pl.pallas_call(
        pre_kernel,
        name="pre",
        in_specs=[pl.BlockSpec(memory_space=pltpu.HBM)] * 3,
        out_shape=[piece, piece],
        scratch_shapes=[
            pltpu.VMEM((ROWS, WIDTH), BF16),
            pltpu.VMEM((ROWS, WIDTH), BF16),
            pltpu.VMEM((1, ROWS), jnp.int32),
            pltpu.SemaphoreType.DMA((3,)),
        ],
        compiler_params=pltpu.CompilerParams(vmem_limit_bytes=8 * 1024 * 1024),
    )(*[pltpu.with_memory_space_constraint(v, pltpu.HBM) for v in raw])
    come = swap(give)
    own = call(join_kernel, "join", pltpu.VMEM((SPAN, WIDTH), BF16), near(keep), near(come))

    def pack(blocks, name, after=()):
        shape = pltpu.VMEM((len(blocks) * SPAN, WIDTH), BF16)
        return call(pack_kernel, name, shape, *[near(x[n]) for n in blocks], after=after)

    x = {0: own}
    for bits in (4, 2, 1):
        x[bits] = send(own, bits)
    x[5] = send(x[4], 1)
    x[6] = send(x[2], 4)
    x[3] = send(x[1], 2)
    x[7] = send(x[1], 6)
    y = [swap(pack(NEAR, "pack_near"))]
    parts = []

    def tile(part, name, after=()):
        rows, columns, _ = PARTS[part]
        used, _ = packs_of(columns)
        last = part == len(PARTS) - 1
        e = pltpu.VMEM((len(rows) * BLOCK, len(columns) * BLOCK), F32)
        sums = [pltpu.VMEM((len(rows) * BLOCK, 128), F32), pltpu.VMEM((16, len(columns) * BLOCK), F32)]
        before = [near(v) for done in parts for v in done[1:]] if last else []
        parts.append(
            call(
                functools.partial(tile_kernel, part),
                name,
                [e, pltpu.VMEM((CUBE, 2 * HALF, 128), F32)] if last else [e, *sums],
                *[near(x[n]) for n in rows],
                *[near(y[PACKS.index(pack)]) for pack in used],
                *before,
                scratch=sums if last else [],
                after=after,
            )
        )

    tile(0, "tile_0", [])
    y.append(swap(pack(FAR[:2], "pack_first", after=[parts[0][1]])))
    tile(1, "tile_1", [parts[0][1]])
    tile(2, "tile_2", [parts[1][1]])
    y.append(swap(pack(FAR[2:], "pack_second", after=[parts[1][1]])))
    tile(3, "tile_3", [parts[2][1]])
    tile(4, "tile_4")
    stats = lax.all_to_all(parts[-1][1], "dp", 0, 0, axis_index_groups=SUM_GROUPS, tiled=True)
    scales = call(scale_kernel, "scales", pltpu.VMEM((HALF + 8, 128), F32), near(stats))

    coded = pltpu.VMEM((SPAN, WIDTH), jnp.int16)
    plain = pltpu.VMEM((BLOCK + LOSS, WIDTH), F32)

    def grad(number, *come, after=(), shape=coded):
        return call(
            functools.partial(grad_kernel, number, shape is coded),
            f"grad_{number}",
            shape,
            *[near(v[0]) for v in parts],
            *[near(v) for v in y],
            near(scales),
            near(x[number]),
            *[near(v) for v in come],
            after=after,
        )

    g3 = grad(3)
    r3 = send(g3, 2)
    g6 = grad(6)
    r6 = send(g6, 4)
    g5 = grad(5)
    r5 = send(g5, 1)
    g7 = grad(7)
    r7 = send(g7, 7)
    g1 = grad(1, r3)
    r1 = send(g1, 1)
    g2 = grad(2, r6)
    r2 = send(g2, 2)
    g4 = grad(4, r5)
    r4 = send(g4, 4)
    g0 = grad(0, shape=plain)
    part = pltpu.VMEM((ROWS + LOSS, WIDTH), F32)
    keep, give = call(split_kernel, "split", [part, part], *[near(v) for v in (g0, r7, r1, r2)])
    come = swap(give)
    other = swap(r4)
    loss, gq, gd = call(
        post_kernel,
        "post",
        [
            jax.ShapeDtypeStruct((1, 1), F32),
            jax.ShapeDtypeStruct((ROWS, WIDTH), F32),
            jax.ShapeDtypeStruct((ROWS, WIDTH), F32),
        ],
        queries,
        documents,
        *[near(v) for v in (keep, come, r4, other)],
    )
    return (loss.reshape(()), gq, gd)


def solution(mesh):
    placed = (P("dp", None), P("dp", None), P("dp"))
    return jax.shard_map(
        local,
        mesh=mesh,
        in_specs=placed,
        out_specs=(P(), P("dp", None), P("dp", None)),
        check_vma=False,
    )
```

```python
import functools

import jax
import jax.numpy as jnp
from jax import lax
from jax.experimental import pallas as pl
from jax.experimental.pallas import tpu as pltpu
from jax.sharding import PartitionSpec as P

PAIRS_A = ((0, 1), (2, 3))
PAIRS_B = ((0, 3), (1, 2))
CUBE = 8
CORES = 2
ROWS = 128
BLOCK = CORES * ROWS
SIDE = CUBE * BLOCK
WIDTH = 768
PAD = 16
PIECES = (48, 48, 40)
LOSS = 8
PER = BLOCK // 128
HALF = CUBE * PER
LOG2E = 1.4426950408889634
FULL = 32760.0
NEAR = (0, 4, 2, 1)
FAR = (7, 5, 3, 6)
PACKS = (NEAR, FAR[:2], FAR[2:])
ALL = NEAR + FAR
PARTS = (
    (NEAR, NEAR, ()),
    (FAR[:2], NEAR, ()),
    (NEAR + FAR[:2], FAR[:2], ()),
    (FAR[2:], NEAR + FAR[:2], ()),
    (ALL, FAR[2:], ()),
)
SPAN = BLOCK + PAD
F32 = jnp.float32
BF16 = jnp.bfloat16


def device_index(x, z, y, core):
    return ((x * 4 + z) * 4 + y) * CORES + core


def partners(bits):
    moves = []
    for x in range(4):
        for z in range(4):
            for y in range(4):
                for core in range(CORES):
                    flip = (lambda v: v ^ 1) if core == 0 else (lambda v: 3 - v)
                    to = [flip(v) if bits & bit else v for v, bit in ((x, 4), (z, 2), (y, 1))]
                    moves.append((device_index(x, z, y, core), device_index(*to, core)))
    return moves


def crossing(bits):
    return [(source, target ^ 1) for source, target in partners(bits)]


def a_cubes():
    return [
        [device_index(x, z, y, core) for x in px for z in pz for y in py]
        for core in range(CORES)
        for px in PAIRS_A
        for pz in PAIRS_A
        for py in PAIRS_A
    ]


SWAP = [(i, i ^ 1) for i in range(128)]
SUM_GROUPS = a_cubes()


def send(value, bits):
    return lax.ppermute(value, "dp", partners(bits))


def swap(value):
    return lax.ppermute(value, "dp", SWAP)


def near(value):
    return pltpu.with_memory_space_constraint(value, pltpu.VMEM)


def call(kernel, name, out_shape, *args, scratch=(), after=()):
    n = len(args)

    def body(*refs):
        kernel(*refs[:n], *refs[n + len(after) :])

    return pl.pallas_call(
        body,
        name=name,
        out_shape=out_shape,
        scratch_shapes=scratch,
        compiler_params=pltpu.CompilerParams(vmem_limit_bytes=8 * 1024 * 1024),
    )(*args, *[near(v) for v in after])


def role_of():
    return lax.axis_index("dp") & 1


def unit_rows(values):
    wide = values.astype(F32)
    length = jnp.sqrt(jnp.sum(wide * wide, axis=1, keepdims=True) + 1e-06)
    return wide / length, length


def row_ids(ref, at=0):
    tail = ref[at + BLOCK : at + SPAN, :BLOCK].astype(F32)
    return tail[0:1, :] * 128.0 + tail[1:2, :]


def down_rows(row, width):
    wide = jnp.transpose(jnp.broadcast_to(row, (128, row.shape[1])))
    return jnp.concatenate([wide] * (width // 128), axis=1)


def pre_kernel(q_hbm, d_hbm, p_hbm, keep_ref, send_ref, q_ref, d_ref, p_ref, sems):
    copies = [
        pltpu.make_async_copy(src, dst, sems.at[n])
        for n, (src, dst) in enumerate(((q_hbm, q_ref), (d_hbm, d_ref), (p_hbm, p_ref)))
    ]
    for copy in copies:
        copy.start()
    me = lax.axis_index("dp")
    role = role_of()
    for copy in copies:
        copy.wait()

    def fill(ref, values, ids):
        ref[:ROWS, :] = unit_rows(values)[0].astype(BF16)
        high = ids >> 7
        rows = lax.broadcasted_iota(jnp.int32, (PAD, ROWS), 0)
        tail = jnp.where(rows == 0, high, jnp.where(rows == 1, ids - high * 128, 0))
        ref[ROWS:, :] = jnp.zeros((PAD, WIDTH), BF16)
        ref[ROWS:, :ROWS] = tail.astype(F32).astype(BF16)

    mine = me * ROWS + lax.broadcasted_iota(jnp.int32, (1, ROWS), 1)

    @pl.when(role == 0)
    def _():
        fill(keep_ref, q_ref[...], p_ref[...])
        fill(send_ref, d_ref[...], mine)

    @pl.when(role == 1)
    def _():
        fill(keep_ref, d_ref[...], mine)
        fill(send_ref, q_ref[...], p_ref[...])


def join_kernel(keep_ref, come_ref, own_ref):
    def fill(low, high):
        own_ref[:ROWS, :] = low[:ROWS, :]
        own_ref[ROWS:BLOCK, :] = high[:ROWS, :]
        own_ref[BLOCK:, :] = jnp.zeros((PAD, WIDTH), BF16)
        own_ref[BLOCK:, :ROWS] = low[ROWS:, :ROWS]
        own_ref[BLOCK:, ROWS:BLOCK] = high[ROWS:, :ROWS]

    role = role_of()

    @pl.when(role == 0)
    def _():
        fill(keep_ref, come_ref)

    @pl.when(role == 1)
    def _():
        fill(come_ref, keep_ref)


def place_in_cube():
    me = lax.axis_index("dp")
    return ((me >> 5) & 1) * 4 + ((me >> 3) & 1) * 2 + ((me >> 1) & 1)


def pack_kernel(*refs):
    for n, ref in enumerate(refs[:-1]):
        refs[-1][n * SPAN : (n + 1) * SPAN, :] = ref[...]


def packs_of(columns):
    used = [pack for pack in PACKS if set(pack) & set(columns)]
    return used, [
        (p, pack.index(number) * SPAN) for number in columns for p, pack in enumerate(used) if number in pack
    ]


def has(part, row, column):
    rows, columns, known = PARTS[part]
    return row in rows and column in columns and not (row in known and column in known)


def tile_kernel(part, *refs):
    rows, columns, _ = PARTS[part]
    last = part == len(PARTS) - 1
    used, where = packs_of(columns)
    x, refs = refs[: len(rows)], refs[len(rows) :]
    y, refs = refs[: len(used)], refs[len(used) :]
    if last:
        before, (e_ref, stats_ref, rowsum_ref, colsum_ref) = refs[: 2 * part], refs[2 * part :]
        before = [(before[2 * n], before[2 * n + 1]) for n in range(part)]
    else:
        e_ref, rowsum_ref, colsum_ref = refs
    ids_of_columns = [row_ids(y[p], at) for p, at in where]
    begun = set()
    for i, number in enumerate(rows):
        ids = down_rows(row_ids(x[i]), BLOCK)
        partial = None
        for k, (p, start) in enumerate(where):
            if not has(part, number, columns[k]):
                continue
            dots = lax.dot_general(
                x[i][:BLOCK, :],
                y[p][start : start + BLOCK, :],
                (((1,), (1,)), ((), ())),
                preferred_element_type=F32,
            )
            e = jnp.exp2(dots * (20.0 * LOG2E) - 20.0 * LOG2E)
            at = slice(k * BLOCK, (k + 1) * BLOCK)
            e_ref[i * BLOCK : (i + 1) * BLOCK, at] = e
            for h in range(PER):
                piece = e[:, h * 128 : (h + 1) * 128]
                partial = piece if partial is None else partial + piece
            hit = jnp.where(ids == ids_of_columns[k], dots, 0.0)
            for n, value in enumerate((e, hit)):
                value = jnp.sum(value.reshape(BLOCK // 8, 8, BLOCK), axis=0)
                to = slice(n * 8, n * 8 + 8)
                colsum_ref[to, at] = colsum_ref[to, at] + value if k in begun else value
            begun.add(k)
        rowsum_ref[i * BLOCK : (i + 1) * BLOCK, :] = partial

    if last:
        place = place_in_cube()
        sums = before + [(rowsum_ref, colsum_ref)]

        def put(n, number, row):
            at = (place ^ number) * PER + n * HALF
            for h in range(PER):
                for g in range(CUBE):
                    stats_ref[g, pl.ds(at + h, 1), :] = row[:, h * 128 : (h + 1) * 128]

        @pl.when(role_of() == 0)
        def _():
            for number in ALL:
                total = None
                for (these, _, _), (ref, _) in zip(PARTS, sums):
                    if number in these:
                        at = these.index(number) * BLOCK
                        piece = ref[at : at + BLOCK, :]
                        total = piece if total is None else total + piece
                put(0, number, jnp.sum(jnp.transpose(total), axis=0, keepdims=True))
                put(1, number, jnp.zeros((1, BLOCK), F32))

        @pl.when(role_of() == 1)
        def _():
            for number in ALL:
                for n in range(2):
                    total = None
                    for (_, these, _), (_, ref) in zip(PARTS, sums):
                        if number in these:
                            at = these.index(number) * BLOCK
                            piece = ref[n * 8 : n * 8 + 8, at : at + BLOCK]
                            total = piece if total is None else total + piece
                    put(n, number, jnp.sum(total, axis=0, keepdims=True))


def encode(out_ref, value, digits):
    largest = None
    for h in range(WIDTH // 128):
        piece = jnp.abs(value[:, h * 128 : (h + 1) * 128])
        largest = piece if largest is None else jnp.maximum(largest, piece)
    largest = jnp.max(largest, axis=1, keepdims=True)
    power = jnp.ceil(jnp.log2(jnp.maximum(largest, 1e-35)) * 128.0)
    steps = value * (FULL * jnp.exp2(power * (-1.0 / 128.0)))
    out_ref[:BLOCK, :] = jnp.floor(steps + 0.5).astype(jnp.int32).astype(jnp.int16)
    at = lax.broadcasted_iota(jnp.int32, (PAD, BLOCK), 0)
    lane = lax.broadcasted_iota(jnp.int32, (PAD, BLOCK), 1)
    power = jnp.transpose(jnp.broadcast_to(power, (BLOCK, 128)))[:PAD, :]
    tail = jnp.where(at == 0, power, 0.0)
    for n, digit in enumerate(digits):
        tail = jnp.where((at == 1) & (lane == n), digit, tail)
    out_ref[BLOCK:, :] = jnp.zeros((PAD, WIDTH), jnp.int16)
    out_ref[BLOCK:, :BLOCK] = tail.astype(jnp.int32).astype(jnp.int16)


def decode(ref):
    tail = ref[BLOCK:, :BLOCK].astype(jnp.int32).astype(F32)
    scale = down_rows(jnp.exp2(tail[0:1, :] * (1.0 / 128.0)) * (1.0 / FULL), WIDTH)
    return ref[:BLOCK, :].astype(jnp.int32).astype(F32) * scale


def decode_half(ref, half):
    tail = ref[ROWS:, half * ROWS : (half + 1) * ROWS].astype(jnp.int32).astype(F32)
    scale = down_rows(jnp.exp2(tail[0:1, :] * (1.0 / 128.0)) * (1.0 / FULL), WIDTH)
    return ref[:ROWS, :].astype(jnp.int32).astype(F32) * scale


def digits_of(loss):
    high = jnp.floor(loss * (1.0 / 16.0))
    rest = (loss - high * 16.0) * 1024.0
    middle = jnp.floor(rest)
    low = jnp.floor((rest - middle) * 16384.0)
    return high, middle, low


def loss_of(ref, rows=BLOCK):
    tail = ref[rows:, :BLOCK].astype(jnp.int32).astype(F32)[1:2, :]
    lane = lax.broadcasted_iota(jnp.int32, (1, BLOCK), 1)
    unit = jnp.where(lane == 0, 16.0, jnp.where(lane == 1, 1.0 / 1024.0, 1.0 / (1024.0 * 16384.0)))
    return jnp.sum(jnp.where(lane < 3, tail * unit, 0.0))


def scale_kernel(stats_ref, out_ref):
    total = jnp.sum(stats_ref[:, :HALF, :], axis=0)
    out_ref[:HALF, :] = 1.0 / total
    lse = 20.0 + jnp.log(total)
    picked = 20.0 * jnp.sum(stats_ref[:, HALF:, :], axis=0)
    out_ref[HALF:, :] = jnp.full((8, 128), jnp.sum(lse - picked), F32)


def grad_kernel(number, coded, *refs):
    exps, refs = refs[: len(PARTS)], refs[len(PARTS) :]
    y, refs = refs[: len(PACKS)], refs[len(PACKS) :]
    scale_ref, x_ref, come, out_ref = refs[0], refs[1], refs[2:-1], refs[-1]
    place = place_in_cube()
    role = role_of()
    loss = scale_ref[HALF, 0]
    _, where = packs_of(ALL)

    def scale_of(block):
        at = (place ^ block) * PER
        return jnp.concatenate([scale_ref[pl.ds(at + h, 1), :] for h in range(PER)], axis=1)

    ids = down_rows(row_ids(x_ref), BLOCK)
    down = down_rows(jnp.where(role == 0, scale_of(number), 1.0), BLOCK)
    acc = None
    for column, (p, start) in zip(ALL, where):
        (e,) = [
            ref[
                rows.index(number) * BLOCK : (rows.index(number) + 1) * BLOCK,
                columns.index(column) * BLOCK : (columns.index(column) + 1) * BLOCK,
            ]
            for part, ((rows, columns, _), ref) in enumerate(zip(PARTS, exps))
            if has(part, number, column)
        ]
        along = jnp.where(role == 1, scale_of(column), 1.0)
        hit = jnp.where(ids == row_ids(y[p], start), 1.0, 0.0)
        weights = (e * down * along - hit).astype(BF16)
        piece = jnp.dot(weights, y[p][start : start + BLOCK, :], preferred_element_type=F32)
        acc = piece if acc is None else acc + piece
    value = 20.0 * acc
    for ref in come:
        value = value + decode(ref)
        loss = loss + loss_of(ref)
    if coded:
        encode(out_ref, value, digits_of(loss))
    else:
        out_ref[:BLOCK, :] = value
        out_ref[BLOCK:, :] = jnp.full((LOSS, WIDTH), loss, F32)


def halves_kernel(number, *refs):
    *given, same_ref, cross_ref, full_ref = refs
    grad_kernel(number, True, *given, full_ref)
    low, high, tail = slice(0, ROWS), slice(ROWS, BLOCK), slice(BLOCK, SPAN)
    same_ref[ROWS:, :] = full_ref[tail, :]
    cross_ref[ROWS:, :] = full_ref[tail, :]
    role = role_of()

    @pl.when(role == 0)
    def _():
        same_ref[:ROWS, :] = full_ref[low, :]
        cross_ref[:ROWS, :] = full_ref[high, :]

    @pl.when(role == 1)
    def _():
        same_ref[:ROWS, :] = full_ref[high, :]
        cross_ref[:ROWS, :] = full_ref[low, :]


def split_kernel(own_ref, *refs):
    count = len(PIECES) + 1
    come, keep_ref, send_refs = refs[:-count], refs[-count], refs[1 - count :]
    value, loss = own_ref[:BLOCK, :], own_ref[BLOCK, 0]
    for ref in come:
        value = value + decode(ref)
        loss = loss + loss_of(ref)
    role = role_of()
    keep_ref[ROWS:, :] = jnp.full((LOSS, WIDTH), loss, F32)
    send_refs[-1][PIECES[-1] - LOSS :, :] = jnp.full((LOSS, WIDTH), loss, F32)

    def give(half):
        start = 0
        for rows, ref in zip(PIECES, send_refs):
            stop = min(start + rows, ROWS)
            ref[: stop - start, :] = half[start:stop, :]
            start = stop

    @pl.when(role == 0)
    def _():
        keep_ref[:ROWS, :] = value[:ROWS, :]
        give(value[ROWS:, :])

    @pl.when(role == 1)
    def _():
        keep_ref[:ROWS, :] = value[ROWS:, :]
        give(value[:ROWS, :])


def post_kernel(q_ref, d_ref, keep_ref, same_ref, cross_ref, *refs):
    *come, loss_ref, gq_ref, gd_ref = refs
    come_ref = jnp.concatenate([ref[...] for ref in come], axis=0)

    def project(out_ref, grad, values):
        unit, length = unit_rows(values)
        out_ref[...] = (grad - jnp.sum(grad * unit, axis=1, keepdims=True) * unit) / length

    def fill(gq, last_q, gd, last_d, half):
        project(gq_ref, gq[:ROWS, :] + decode_half(last_q, half), q_ref[...])
        project(gd_ref, gd[:ROWS, :] + decode_half(last_d, half), d_ref[...])
        loss_ref[...] = (gd[ROWS : ROWS + 1, 0:1] + loss_of(last_d, ROWS)) * (1.0 / 16384)

    role = role_of()

    @pl.when(role == 0)
    def _():
        fill(keep_ref, same_ref, come_ref, cross_ref, 0)

    @pl.when(role == 1)
    def _():
        fill(come_ref, cross_ref, keep_ref, same_ref, 1)


def local(queries, documents, positives):
    piece = pltpu.VMEM((ROWS + PAD, WIDTH), BF16)
    raw = [queries, documents, positives.reshape(1, ROWS)]
    keep, give = pl.pallas_call(
        pre_kernel,
        name="pre",
        in_specs=[pl.BlockSpec(memory_space=pltpu.HBM)] * 3,
        out_shape=[piece, piece],
        scratch_shapes=[
            pltpu.VMEM((ROWS, WIDTH), BF16),
            pltpu.VMEM((ROWS, WIDTH), BF16),
            pltpu.VMEM((1, ROWS), jnp.int32),
            pltpu.SemaphoreType.DMA((3,)),
        ],
        compiler_params=pltpu.CompilerParams(vmem_limit_bytes=8 * 1024 * 1024),
    )(*[pltpu.with_memory_space_constraint(v, pltpu.HBM) for v in raw])
    come = swap(give)
    own = call(join_kernel, "join", pltpu.VMEM((SPAN, WIDTH), BF16), near(keep), near(come))

    def pack(blocks, name, after=()):
        shape = pltpu.VMEM((len(blocks) * SPAN, WIDTH), BF16)
        return call(pack_kernel, name, shape, *[near(x[n]) for n in blocks], after=after)

    x = {0: own}
    for bits in (4, 2, 1):
        x[bits] = send(own, bits)
    x[5] = send(x[4], 1)
    x[6] = send(x[2], 4)
    x[3] = send(x[1], 2)
    x[7] = send(x[1], 6)
    y = [swap(pack(NEAR, "pack_near"))]
    parts = []

    def tile(part, name, after=()):
        rows, columns, _ = PARTS[part]
        used, _ = packs_of(columns)
        last = part == len(PARTS) - 1
        e = pltpu.VMEM((len(rows) * BLOCK, len(columns) * BLOCK), F32)
        sums = [pltpu.VMEM((len(rows) * BLOCK, 128), F32), pltpu.VMEM((16, len(columns) * BLOCK), F32)]
        before = [near(v) for done in parts for v in done[1:]] if last else []
        parts.append(
            call(
                functools.partial(tile_kernel, part),
                name,
                [e, pltpu.VMEM((CUBE, 2 * HALF, 128), F32)] if last else [e, *sums],
                *[near(x[n]) for n in rows],
                *[near(y[PACKS.index(pack)]) for pack in used],
                *before,
                scratch=sums if last else [],
                after=after,
            )
        )

    tile(0, "tile_0", [])
    y.append(swap(pack(FAR[:2], "pack_first", after=[parts[0][1]])))
    tile(1, "tile_1", [parts[0][1]])
    tile(2, "tile_2", [parts[1][1]])
    y.append(swap(pack(FAR[2:], "pack_second", after=[parts[1][1]])))
    tile(3, "tile_3", [parts[2][1]])
    tile(4, "tile_4")
    stats = lax.all_to_all(parts[-1][1], "dp", 0, 0, axis_index_groups=SUM_GROUPS, tiled=True)
    scales = call(scale_kernel, "scales", pltpu.VMEM((HALF + 8, 128), F32), near(stats))

    coded = pltpu.VMEM((SPAN, WIDTH), jnp.int16)
    half = pltpu.VMEM((ROWS + PAD, WIDTH), jnp.int16)
    plain = pltpu.VMEM((BLOCK + LOSS, WIDTH), F32)

    def grad(number, *come, after=(), shape=coded):
        halves = shape is half
        return call(
            functools.partial(halves_kernel, number)
            if halves
            else functools.partial(grad_kernel, number, shape is coded),
            f"grad_{number}",
            [half, half] if halves else shape,
            *[near(v[0]) for v in parts],
            *[near(v) for v in y],
            near(scales),
            near(x[number]),
            *[near(v) for v in come],
            scratch=[coded] if halves else [],
            after=after,
        )

    g3 = grad(3)
    r3 = send(g3, 2)
    g6 = grad(6)
    r6 = send(g6, 4)
    g5 = grad(5)
    r5 = send(g5, 1)
    g7 = grad(7, after=[g5])
    r7 = send(g7, 7)
    g1 = grad(1, r3)
    r1 = send(g1, 1)
    g2 = grad(2, r6)
    r2 = send(g2, 2)
    halves = grad(4, r5, shape=half)
    cross = lax.ppermute(halves[1], "dp", crossing(4))
    same = send(halves[0], 4)
    g0 = grad(0, after=[halves[0]], shape=plain)
    part = pltpu.VMEM((ROWS + LOSS, WIDTH), F32)
    pieces = [pltpu.VMEM((rows, WIDTH), F32) for rows in PIECES]
    keep, *give = call(split_kernel, "split", [part, *pieces], *[near(v) for v in (g0, r7, r1, r2)])
    come = [swap(v) for v in give]
    loss, gq, gd = call(
        post_kernel,
        "post",
        [
            jax.ShapeDtypeStruct((1, 1), F32),
            jax.ShapeDtypeStruct((ROWS, WIDTH), F32),
            jax.ShapeDtypeStruct((ROWS, WIDTH), F32),
        ],
        queries,
        documents,
        *[near(v) for v in (keep, same, cross, *come)],
    )
    return (loss.reshape(()), gq, gd)


def solution(mesh):
    placed = (P("dp", None), P("dp", None), P("dp"))
    return jax.shard_map(
        local,
        mesh=mesh,
        in_specs=placed,
        out_specs=(P(), P("dp", None), P("dp", None)),
        check_vma=False,
    )
```

```python
import functools

import jax
import jax.numpy as jnp
from jax import lax
from jax.experimental import pallas as pl
from jax.experimental.pallas import tpu as pltpu
from jax.sharding import PartitionSpec as P

PAIRS_A = ((0, 1), (2, 3))
PAIRS_B = ((0, 3), (1, 2))
CUBE = 8
CORES = 2
ROWS = 128
BLOCK = CORES * ROWS
SIDE = CUBE * BLOCK
WIDTH = 768
PAD = 16
PIECES = (48, 48, 40)
LOSS = 8
PER = BLOCK // 128
HALF = CUBE * PER
LOG2E = 1.4426950408889634
FULL = 32760.0
NEAR = (0, 4, 2, 1)
FAR = (7, 5, 3, 6)
PACKS = (NEAR, FAR[:2], FAR[2:])
ALL = NEAR + FAR
PARTS = (
    (NEAR, NEAR, ()),
    (FAR[:2], NEAR, ()),
    (NEAR + FAR[:2], FAR[:2], ()),
    (FAR[2:], NEAR + FAR[:2], ()),
    (ALL, FAR[2:], ()),
)
SPAN = BLOCK + PAD
F32 = jnp.float32
BF16 = jnp.bfloat16


def device_index(x, z, y, core):
    return ((x * 4 + z) * 4 + y) * CORES + core


def partners(bits):
    moves = []
    for x in range(4):
        for z in range(4):
            for y in range(4):
                for core in range(CORES):
                    flip = (lambda v: v ^ 1) if core == 0 else (lambda v: 3 - v)
                    to = [flip(v) if bits & bit else v for v, bit in ((x, 4), (z, 2), (y, 1))]
                    moves.append((device_index(x, z, y, core), device_index(*to, core)))
    return moves


def crossing(bits):
    return [(source, target ^ 1) for source, target in partners(bits)]


def a_cubes():
    return [
        [device_index(x, z, y, core) for x in px for z in pz for y in py]
        for core in range(CORES)
        for px in PAIRS_A
        for pz in PAIRS_A
        for py in PAIRS_A
    ]


SWAP = [(i, i ^ 1) for i in range(128)]
SUM_GROUPS = a_cubes()


def send(value, bits):
    return lax.ppermute(value, "dp", partners(bits))


def swap(value):
    return lax.ppermute(value, "dp", SWAP)


def near(value):
    return pltpu.with_memory_space_constraint(value, pltpu.VMEM)


def call(kernel, name, out_shape, *args, scratch=(), after=()):
    n = len(args)

    def body(*refs):
        kernel(*refs[:n], *refs[n + len(after) :])

    return pl.pallas_call(
        body,
        name=name,
        out_shape=out_shape,
        scratch_shapes=scratch,
        compiler_params=pltpu.CompilerParams(vmem_limit_bytes=8 * 1024 * 1024),
    )(*args, *[near(v) for v in after])


def role_of():
    return lax.axis_index("dp") & 1


def unit_rows(values):
    wide = values.astype(F32)
    length = jnp.sqrt(jnp.sum(wide * wide, axis=1, keepdims=True) + 1e-06)
    return wide / length, length


def row_ids(ref, at=0):
    tail = ref[at + BLOCK : at + SPAN, :BLOCK].astype(F32)
    return tail[0:1, :] * 128.0 + tail[1:2, :]


def down_rows(row, width):
    wide = jnp.transpose(jnp.broadcast_to(row, (128, row.shape[1])))
    return jnp.concatenate([wide] * (width // 128), axis=1)


def pre_kernel(q_hbm, d_hbm, p_hbm, keep_ref, send_ref, q_ref, d_ref, p_ref, sems):
    copies = [
        pltpu.make_async_copy(src, dst, sems.at[n])
        for n, (src, dst) in enumerate(((q_hbm, q_ref), (d_hbm, d_ref), (p_hbm, p_ref)))
    ]
    for copy in copies:
        copy.start()
    me = lax.axis_index("dp")
    role = role_of()
    for copy in copies:
        copy.wait()

    def fill(ref, values, ids):
        ref[:ROWS, :] = unit_rows(values)[0].astype(BF16)
        high = ids >> 7
        rows = lax.broadcasted_iota(jnp.int32, (PAD, ROWS), 0)
        tail = jnp.where(rows == 0, high, jnp.where(rows == 1, ids - high * 128, 0))
        ref[ROWS:, :] = jnp.zeros((PAD, WIDTH), BF16)
        ref[ROWS:, :ROWS] = tail.astype(F32).astype(BF16)

    mine = me * ROWS + lax.broadcasted_iota(jnp.int32, (1, ROWS), 1)

    @pl.when(role == 0)
    def _():
        fill(keep_ref, q_ref[...], p_ref[...])
        fill(send_ref, d_ref[...], mine)

    @pl.when(role == 1)
    def _():
        fill(keep_ref, d_ref[...], mine)
        fill(send_ref, q_ref[...], p_ref[...])


def join_kernel(keep_ref, come_ref, own_ref):
    def fill(low, high):
        own_ref[:ROWS, :] = low[:ROWS, :]
        own_ref[ROWS:BLOCK, :] = high[:ROWS, :]
        own_ref[BLOCK:, :] = jnp.zeros((PAD, WIDTH), BF16)
        own_ref[BLOCK:, :ROWS] = low[ROWS:, :ROWS]
        own_ref[BLOCK:, ROWS:BLOCK] = high[ROWS:, :ROWS]

    role = role_of()

    @pl.when(role == 0)
    def _():
        fill(keep_ref, come_ref)

    @pl.when(role == 1)
    def _():
        fill(come_ref, keep_ref)


def place_in_cube():
    me = lax.axis_index("dp")
    return ((me >> 5) & 1) * 4 + ((me >> 3) & 1) * 2 + ((me >> 1) & 1)


def pack_kernel(*refs):
    for n, ref in enumerate(refs[:-1]):
        refs[-1][n * SPAN : (n + 1) * SPAN, :] = ref[...]


def packs_of(columns):
    used = [pack for pack in PACKS if set(pack) & set(columns)]
    return used, [
        (p, pack.index(number) * SPAN) for number in columns for p, pack in enumerate(used) if number in pack
    ]


def has(part, row, column):
    rows, columns, known = PARTS[part]
    return row in rows and column in columns and not (row in known and column in known)


def tile_kernel(part, *refs):
    rows, columns, _ = PARTS[part]
    last = part == len(PARTS) - 1
    used, where = packs_of(columns)
    x, refs = refs[: len(rows)], refs[len(rows) :]
    y, refs = refs[: len(used)], refs[len(used) :]
    if last:
        before, (e_ref, stats_ref, rowsum_ref, colsum_ref) = refs[: 2 * part], refs[2 * part :]
        before = [(before[2 * n], before[2 * n + 1]) for n in range(part)]
    else:
        e_ref, rowsum_ref, colsum_ref = refs
    ids_of_columns = [row_ids(y[p], at) for p, at in where]
    begun = set()
    for i, number in enumerate(rows):
        ids = down_rows(row_ids(x[i]), BLOCK)
        partial = None
        for k, (p, start) in enumerate(where):
            if not has(part, number, columns[k]):
                continue
            dots = lax.dot_general(
                x[i][:BLOCK, :],
                y[p][start : start + BLOCK, :],
                (((1,), (1,)), ((), ())),
                preferred_element_type=F32,
            )
            e = jnp.exp2(dots * (20.0 * LOG2E) - 20.0 * LOG2E)
            at = slice(k * BLOCK, (k + 1) * BLOCK)
            e_ref[i * BLOCK : (i + 1) * BLOCK, at] = e
            for h in range(PER):
                piece = e[:, h * 128 : (h + 1) * 128]
                partial = piece if partial is None else partial + piece
            hit = jnp.where(ids == ids_of_columns[k], dots, 0.0)
            for n, value in enumerate((e, hit)):
                value = jnp.sum(value.reshape(BLOCK // 8, 8, BLOCK), axis=0)
                to = slice(n * 8, n * 8 + 8)
                colsum_ref[to, at] = colsum_ref[to, at] + value if k in begun else value
            begun.add(k)
        rowsum_ref[i * BLOCK : (i + 1) * BLOCK, :] = partial

    if last:
        place = place_in_cube()
        sums = before + [(rowsum_ref, colsum_ref)]

        def put(n, number, row):
            at = (place ^ number) * PER + n * HALF
            for h in range(PER):
                for g in range(CUBE):
                    stats_ref[g, pl.ds(at + h, 1), :] = row[:, h * 128 : (h + 1) * 128]

        @pl.when(role_of() == 0)
        def _():
            for number in ALL:
                total = None
                for (these, _, _), (ref, _) in zip(PARTS, sums):
                    if number in these:
                        at = these.index(number) * BLOCK
                        piece = ref[at : at + BLOCK, :]
                        total = piece if total is None else total + piece
                put(0, number, jnp.sum(jnp.transpose(total), axis=0, keepdims=True))
                put(1, number, jnp.zeros((1, BLOCK), F32))

        @pl.when(role_of() == 1)
        def _():
            for number in ALL:
                for n in range(2):
                    total = None
                    for (_, these, _), (_, ref) in zip(PARTS, sums):
                        if number in these:
                            at = these.index(number) * BLOCK
                            piece = ref[n * 8 : n * 8 + 8, at : at + BLOCK]
                            total = piece if total is None else total + piece
                    put(n, number, jnp.sum(total, axis=0, keepdims=True))


def encode(out_ref, value, digits):
    largest = None
    for h in range(WIDTH // 128):
        piece = jnp.abs(value[:, h * 128 : (h + 1) * 128])
        largest = piece if largest is None else jnp.maximum(largest, piece)
    largest = jnp.max(largest, axis=1, keepdims=True)
    power = jnp.ceil(jnp.log2(jnp.maximum(largest, 1e-30)) * 128.0)
    steps = value * (FULL * jnp.exp2(power * (-1.0 / 128.0)))
    out_ref[:BLOCK, :] = jnp.floor(steps + 0.5).astype(jnp.int32).astype(jnp.int16)
    at = lax.broadcasted_iota(jnp.int32, (PAD, BLOCK), 0)
    lane = lax.broadcasted_iota(jnp.int32, (PAD, BLOCK), 1)
    power = jnp.transpose(jnp.broadcast_to(power, (BLOCK, 128)))[:PAD, :]
    tail = jnp.where(at == 0, power, 0.0)
    for n, digit in enumerate(digits):
        tail = jnp.where((at == 1) & (lane == n), digit, tail)
    out_ref[BLOCK:, :] = jnp.zeros((PAD, WIDTH), jnp.int16)
    out_ref[BLOCK:, :BLOCK] = tail.astype(jnp.int32).astype(jnp.int16)


def decode(ref):
    tail = ref[BLOCK:, :BLOCK].astype(jnp.int32).astype(F32)
    scale = down_rows(jnp.exp2(tail[0:1, :] * (1.0 / 128.0)) * (1.0 / FULL), WIDTH)
    return ref[:BLOCK, :].astype(jnp.int32).astype(F32) * scale


def decode_half(ref, half):
    tail = ref[ROWS:, half * ROWS : (half + 1) * ROWS].astype(jnp.int32).astype(F32)
    scale = down_rows(jnp.exp2(tail[0:1, :] * (1.0 / 128.0)) * (1.0 / FULL), WIDTH)
    return ref[:ROWS, :].astype(jnp.int32).astype(F32) * scale


def digits_of(loss):
    high = jnp.floor(loss * (1.0 / 16.0))
    rest = (loss - high * 16.0) * 1024.0
    middle = jnp.floor(rest)
    low = jnp.floor((rest - middle) * 16384.0)
    return high, middle, low


def loss_of(ref, rows=BLOCK):
    tail = ref[rows:, :BLOCK].astype(jnp.int32).astype(F32)[1:2, :]
    lane = lax.broadcasted_iota(jnp.int32, (1, BLOCK), 1)
    unit = jnp.where(lane == 0, 16.0, jnp.where(lane == 1, 1.0 / 1024.0, 1.0 / (1024.0 * 16384.0)))
    return jnp.sum(jnp.where(lane < 3, tail * unit, 0.0))


def scale_kernel(stats_ref, out_ref):
    total = jnp.sum(stats_ref[:, :HALF, :], axis=0)
    out_ref[:HALF, :] = 1.0 / total
    lse = 20.0 + jnp.log(total)
    picked = 20.0 * jnp.sum(stats_ref[:, HALF:, :], axis=0)
    out_ref[HALF:, :] = jnp.full((8, 128), jnp.sum(lse - picked), F32)


def grad_kernel(number, coded, *refs):
    exps, refs = refs[: len(PARTS)], refs[len(PARTS) :]
    y, refs = refs[: len(PACKS)], refs[len(PACKS) :]
    scale_ref, x_ref, come, out_ref = refs[0], refs[1], refs[2:-1], refs[-1]
    place = place_in_cube()
    role = role_of()
    loss = scale_ref[HALF, 0]
    _, where = packs_of(ALL)

    def scale_of(block):
        at = (place ^ block) * PER
        return jnp.concatenate([scale_ref[pl.ds(at + h, 1), :] for h in range(PER)], axis=1)

    ids = down_rows(row_ids(x_ref), BLOCK)
    down = down_rows(jnp.where(role == 0, scale_of(number), 1.0), BLOCK)
    acc = None
    for column, (p, start) in zip(ALL, where):
        (e,) = [
            ref[
                rows.index(number) * BLOCK : (rows.index(number) + 1) * BLOCK,
                columns.index(column) * BLOCK : (columns.index(column) + 1) * BLOCK,
            ]
            for part, ((rows, columns, _), ref) in enumerate(zip(PARTS, exps))
            if has(part, number, column)
        ]
        along = jnp.where(role == 1, scale_of(column), 1.0)
        hit = jnp.where(ids == row_ids(y[p], start), 1.0, 0.0)
        weights = (e * down * along - hit).astype(BF16)
        piece = jnp.dot(weights, y[p][start : start + BLOCK, :], preferred_element_type=F32)
        acc = piece if acc is None else acc + piece
    value = 20.0 * acc
    for ref in come:
        value = value + decode(ref)
        loss = loss + loss_of(ref)
    if coded:
        encode(out_ref, value, digits_of(loss))
    else:
        out_ref[:BLOCK, :] = value
        out_ref[BLOCK:, :] = jnp.full((LOSS, WIDTH), loss, F32)


def halves_kernel(number, *refs):
    *given, same_ref, cross_ref, full_ref = refs
    grad_kernel(number, True, *given, full_ref)
    low, high, tail = slice(0, ROWS), slice(ROWS, BLOCK), slice(BLOCK, SPAN)
    same_ref[ROWS:, :] = full_ref[tail, :]
    cross_ref[ROWS:, :] = full_ref[tail, :]
    role = role_of()

    @pl.when(role == 0)
    def _():
        same_ref[:ROWS, :] = full_ref[low, :]
        cross_ref[:ROWS, :] = full_ref[high, :]

    @pl.when(role == 1)
    def _():
        same_ref[:ROWS, :] = full_ref[high, :]
        cross_ref[:ROWS, :] = full_ref[low, :]


def split_kernel(own_ref, *refs):
    count = len(PIECES) + 1
    come, keep_ref, send_refs = refs[:-count], refs[-count], refs[1 - count :]
    value, loss = own_ref[:BLOCK, :], own_ref[BLOCK, 0]
    for ref in come:
        value = value + decode(ref)
        loss = loss + loss_of(ref)
    role = role_of()
    keep_ref[ROWS:, :] = jnp.full((LOSS, WIDTH), loss, F32)
    send_refs[-1][PIECES[-1] - LOSS :, :] = jnp.full((LOSS, WIDTH), loss, F32)

    def give(half):
        start = 0
        for rows, ref in zip(PIECES, send_refs):
            stop = min(start + rows, ROWS)
            ref[: stop - start, :] = half[start:stop, :]
            start = stop

    @pl.when(role == 0)
    def _():
        keep_ref[:ROWS, :] = value[:ROWS, :]
        give(value[ROWS:, :])

    @pl.when(role == 1)
    def _():
        keep_ref[:ROWS, :] = value[ROWS:, :]
        give(value[:ROWS, :])


def post_kernel(q_ref, d_ref, keep_ref, same_ref, cross_ref, *refs):
    *come, loss_ref, gq_ref, gd_ref = refs
    come_ref = jnp.concatenate([ref[...] for ref in come], axis=0)

    def project(out_ref, grad, values):
        unit, length = unit_rows(values)
        out_ref[...] = (grad - jnp.sum(grad * unit, axis=1, keepdims=True) * unit) / length

    def fill(gq, last_q, gd, last_d, half):
        project(gq_ref, gq[:ROWS, :] + decode_half(last_q, half), q_ref[...])
        project(gd_ref, gd[:ROWS, :] + decode_half(last_d, half), d_ref[...])
        loss_ref[...] = (gd[ROWS : ROWS + 1, 0:1] + loss_of(last_d, ROWS)) * (1.0 / 16384)

    role = role_of()

    @pl.when(role == 0)
    def _():
        fill(keep_ref, same_ref, come_ref, cross_ref, 0)

    @pl.when(role == 1)
    def _():
        fill(come_ref, cross_ref, keep_ref, same_ref, 1)


def local(queries, documents, positives):
    piece = pltpu.VMEM((ROWS + PAD, WIDTH), BF16)
    raw = [queries, documents, positives.reshape(1, ROWS)]
    keep, give = pl.pallas_call(
        pre_kernel,
        name="pre",
        in_specs=[pl.BlockSpec(memory_space=pltpu.HBM)] * 3,
        out_shape=[piece, piece],
        scratch_shapes=[
            pltpu.VMEM((ROWS, WIDTH), BF16),
            pltpu.VMEM((ROWS, WIDTH), BF16),
            pltpu.VMEM((1, ROWS), jnp.int32),
            pltpu.SemaphoreType.DMA((3,)),
        ],
        compiler_params=pltpu.CompilerParams(vmem_limit_bytes=8 * 1024 * 1024),
    )(*[pltpu.with_memory_space_constraint(v, pltpu.HBM) for v in raw])
    come = swap(give)
    own = call(join_kernel, "join", pltpu.VMEM((SPAN, WIDTH), BF16), near(keep), near(come))

    def pack(blocks, name, after=()):
        shape = pltpu.VMEM((len(blocks) * SPAN, WIDTH), BF16)
        return call(pack_kernel, name, shape, *[near(x[n]) for n in blocks], after=after)

    x = {0: own}
    for bits in (4, 2, 1):
        x[bits] = send(own, bits)
    x[5] = send(x[4], 1)
    x[6] = send(x[2], 4)
    x[3] = send(x[1], 2)
    x[7] = send(x[1], 6)
    y = [swap(pack(NEAR, "pack_near"))]
    parts = []

    def tile(part, name, after=()):
        rows, columns, _ = PARTS[part]
        used, _ = packs_of(columns)
        last = part == len(PARTS) - 1
        e = pltpu.VMEM((len(rows) * BLOCK, len(columns) * BLOCK), F32)
        sums = [pltpu.VMEM((len(rows) * BLOCK, 128), F32), pltpu.VMEM((16, len(columns) * BLOCK), F32)]
        before = [near(v) for done in parts for v in done[1:]] if last else []
        parts.append(
            call(
                functools.partial(tile_kernel, part),
                name,
                [e, pltpu.VMEM((CUBE, 2 * HALF, 128), F32)] if last else [e, *sums],
                *[near(x[n]) for n in rows],
                *[near(y[PACKS.index(pack)]) for pack in used],
                *before,
                scratch=sums if last else [],
                after=after,
            )
        )

    tile(0, "tile_0", [])
    y.append(swap(pack(FAR[:2], "pack_first", after=[parts[0][1]])))
    tile(1, "tile_1", [parts[0][1]])
    tile(2, "tile_2", [parts[1][1]])
    y.append(swap(pack(FAR[2:], "pack_second", after=[parts[1][1]])))
    tile(3, "tile_3", [parts[2][1]])
    tile(4, "tile_4")
    stats = lax.all_to_all(parts[-1][1], "dp", 0, 0, axis_index_groups=SUM_GROUPS, tiled=True)
    scales = call(scale_kernel, "scales", pltpu.VMEM((HALF + 8, 128), F32), near(stats))

    coded = pltpu.VMEM((SPAN, WIDTH), jnp.int16)
    half = pltpu.VMEM((ROWS + PAD, WIDTH), jnp.int16)
    plain = pltpu.VMEM((BLOCK + LOSS, WIDTH), F32)

    def grad(number, *come, after=(), shape=coded):
        halves = shape is half
        return call(
            functools.partial(halves_kernel, number)
            if halves
            else functools.partial(grad_kernel, number, shape is coded),
            f"grad_{number}",
            [half, half] if halves else shape,
            *[near(v[0]) for v in parts],
            *[near(v) for v in y],
            near(scales),
            near(x[number]),
            *[near(v) for v in come],
            scratch=[coded] if halves else [],
            after=after,
        )

    g3 = grad(3)
    r3 = send(g3, 2)
    g6 = grad(6)
    r6 = send(g6, 4)
    g5 = grad(5)
    r5 = send(g5, 1)
    g7 = grad(7, after=[g5])
    r7 = send(g7, 7)
    g1 = grad(1, r3)
    r1 = send(g1, 1)
    g2 = grad(2, r6)
    r2 = send(g2, 2)
    halves = grad(4, r5, shape=half)
    cross = lax.ppermute(halves[1], "dp", crossing(4))
    same = send(halves[0], 4)
    g0 = grad(0, after=[halves[0]], shape=plain)
    part = pltpu.VMEM((ROWS + LOSS, WIDTH), F32)
    pieces = [pltpu.VMEM((rows, WIDTH), F32) for rows in PIECES]
    keep, *give = call(split_kernel, "split", [part, *pieces], *[near(v) for v in (g0, r7, r1, r2)])
    come = [swap(v) for v in give]
    loss, gq, gd = call(
        post_kernel,
        "post",
        [
            jax.ShapeDtypeStruct((1, 1), F32),
            jax.ShapeDtypeStruct((ROWS, WIDTH), F32),
            jax.ShapeDtypeStruct((ROWS, WIDTH), F32),
        ],
        queries,
        documents,
        *[near(v) for v in (keep, same, cross, *come)],
    )
    return (loss.reshape(()), gq, gd)


def solution(mesh):
    placed = (P("dp", None), P("dp", None), P("dp"))
    return jax.shard_map(
        local,
        mesh=mesh,
        in_specs=placed,
        out_specs=(P(), P("dp", None), P("dp", None)),
        check_vma=False,
    )
```

```python
import functools

import jax
import jax.numpy as jnp
from jax import lax
from jax.experimental import pallas as pl
from jax.experimental.pallas import tpu as pltpu
from jax.sharding import PartitionSpec as P

PAIRS_A = ((0, 1), (2, 3))
PAIRS_B = ((0, 3), (1, 2))
CUBE = 8
CORES = 2
ROWS = 128
BLOCK = CORES * ROWS
SIDE = CUBE * BLOCK
WIDTH = 768
PAD = 16
PIECES = (48, 48, 40)
LOSS = 8
PER = BLOCK // 128
HALF = CUBE * PER
LOG2E = 1.4426950408889634
FULL = 32760.0
NEAR = (0, 4, 2, 1)
FAR = (7, 5, 3, 6)
PACKS = (NEAR, FAR[:2], FAR[2:])
ALL = NEAR + FAR
PARTS = (
    (NEAR, NEAR, ()),
    (FAR[:2], NEAR, ()),
    (NEAR + FAR[:2], FAR[:2], ()),
    (FAR[2:], NEAR + FAR[:2], ()),
    (ALL, FAR[2:], ()),
)
SPAN = BLOCK + PAD
F32 = jnp.float32
BF16 = jnp.bfloat16


def device_index(x, z, y, core):
    return ((x * 4 + z) * 4 + y) * CORES + core


def partners(bits):
    moves = []
    for x in range(4):
        for z in range(4):
            for y in range(4):
                for core in range(CORES):
                    flip = (lambda v: v ^ 1) if core == 0 else (lambda v: 3 - v)
                    to = [flip(v) if bits & bit else v for v, bit in ((x, 4), (z, 2), (y, 1))]
                    moves.append((device_index(x, z, y, core), device_index(*to, core)))
    return moves


def crossing(bits):
    return [(source, target ^ 1) for source, target in partners(bits)]


def a_cubes():
    return [
        [device_index(x, z, y, core) for x in px for z in pz for y in py]
        for core in range(CORES)
        for px in PAIRS_A
        for pz in PAIRS_A
        for py in PAIRS_A
    ]


SWAP = [(i, i ^ 1) for i in range(128)]
SUM_GROUPS = a_cubes()


def send(value, bits):
    return lax.ppermute(value, "dp", partners(bits))


def swap(value):
    return lax.ppermute(value, "dp", SWAP)


def near(value):
    return pltpu.with_memory_space_constraint(value, pltpu.VMEM)


def call(kernel, name, out_shape, *args, scratch=(), after=()):
    n = len(args)

    def body(*refs):
        kernel(*refs[:n], *refs[n + len(after) :])

    return pl.pallas_call(
        body,
        name=name,
        out_shape=out_shape,
        scratch_shapes=scratch,
        compiler_params=pltpu.CompilerParams(vmem_limit_bytes=8 * 1024 * 1024),
    )(*args, *[near(v) for v in after])


def role_of():
    return lax.axis_index("dp") & 1


def unit_rows(values):
    wide = values.astype(F32)
    length = jnp.sqrt(jnp.sum(wide * wide, axis=1, keepdims=True) + 1e-06)
    return wide / length, length


def row_ids(ref, at=0):
    tail = ref[at + BLOCK : at + SPAN, :BLOCK].astype(F32)
    return tail[0:1, :] * 128.0 + tail[1:2, :]


def down_rows(row, width):
    wide = jnp.transpose(jnp.broadcast_to(row, (128, row.shape[1])))
    return jnp.concatenate([wide] * (width // 128), axis=1)


def pre_kernel(q_hbm, d_hbm, p_hbm, keep_ref, send_ref, q_ref, d_ref, p_ref, sems):
    copies = [
        pltpu.make_async_copy(src, dst, sems.at[n])
        for n, (src, dst) in enumerate(((q_hbm, q_ref), (d_hbm, d_ref), (p_hbm, p_ref)))
    ]
    for copy in copies:
        copy.start()
    me = lax.axis_index("dp")
    role = role_of()
    for copy in copies:
        copy.wait()

    def fill(ref, values, ids):
        ref[:ROWS, :] = unit_rows(values)[0].astype(BF16)
        high = ids >> 7
        rows = lax.broadcasted_iota(jnp.int32, (PAD, ROWS), 0)
        tail = jnp.where(rows == 0, high, jnp.where(rows == 1, ids - high * 128, 0))
        ref[ROWS:, :] = jnp.zeros((PAD, WIDTH), BF16)
        ref[ROWS:, :ROWS] = tail.astype(F32).astype(BF16)

    mine = me * ROWS + lax.broadcasted_iota(jnp.int32, (1, ROWS), 1)

    @pl.when(role == 0)
    def _():
        fill(keep_ref, q_ref[...], p_ref[...])
        fill(send_ref, d_ref[...], mine)

    @pl.when(role == 1)
    def _():
        fill(keep_ref, d_ref[...], mine)
        fill(send_ref, q_ref[...], p_ref[...])


def join_kernel(keep_ref, come_ref, own_ref):
    def fill(low, high):
        own_ref[:ROWS, :] = low[:ROWS, :]
        own_ref[ROWS:BLOCK, :] = high[:ROWS, :]
        own_ref[BLOCK:, :] = jnp.zeros((PAD, WIDTH), BF16)
        own_ref[BLOCK:, :ROWS] = low[ROWS:, :ROWS]
        own_ref[BLOCK:, ROWS:BLOCK] = high[ROWS:, :ROWS]

    role = role_of()

    @pl.when(role == 0)
    def _():
        fill(keep_ref, come_ref)

    @pl.when(role == 1)
    def _():
        fill(come_ref, keep_ref)


def place_in_cube():
    me = lax.axis_index("dp")
    return ((me >> 5) & 1) * 4 + ((me >> 3) & 1) * 2 + ((me >> 1) & 1)


def pack_kernel(*refs):
    for n, ref in enumerate(refs[:-1]):
        refs[-1][n * SPAN : (n + 1) * SPAN, :] = ref[...]


def packs_of(columns):
    used = [pack for pack in PACKS if set(pack) & set(columns)]
    return used, [
        (p, pack.index(number) * SPAN) for number in columns for p, pack in enumerate(used) if number in pack
    ]


def has(part, row, column):
    rows, columns, known = PARTS[part]
    return row in rows and column in columns and not (row in known and column in known)


def tile_kernel(part, *refs):
    rows, columns, _ = PARTS[part]
    last = part == len(PARTS) - 1
    used, where = packs_of(columns)
    x, refs = refs[: len(rows)], refs[len(rows) :]
    y, refs = refs[: len(used)], refs[len(used) :]
    if last:
        before, (e_ref, stats_ref, rowsum_ref, colsum_ref) = refs[: 2 * part], refs[2 * part :]
        before = [(before[2 * n], before[2 * n + 1]) for n in range(part)]
    else:
        e_ref, rowsum_ref, colsum_ref = refs
    ids_of_columns = [row_ids(y[p], at) for p, at in where]
    begun = set()
    for i, number in enumerate(rows):
        ids = down_rows(row_ids(x[i]), BLOCK)
        partial = None
        for k, (p, start) in enumerate(where):
            if not has(part, number, columns[k]):
                continue
            dots = lax.dot_general(
                x[i][:BLOCK, :],
                y[p][start : start + BLOCK, :],
                (((1,), (1,)), ((), ())),
                preferred_element_type=F32,
            )
            e = jnp.exp2(dots * (20.0 * LOG2E) - 20.0 * LOG2E)
            at = slice(k * BLOCK, (k + 1) * BLOCK)
            e_ref[i * BLOCK : (i + 1) * BLOCK, at] = e
            for h in range(PER):
                piece = e[:, h * 128 : (h + 1) * 128]
                partial = piece if partial is None else partial + piece
            hit = jnp.where(ids == ids_of_columns[k], dots, 0.0)
            for n, value in enumerate((e, hit)):
                value = jnp.sum(value.reshape(BLOCK // 8, 8, BLOCK), axis=0)
                to = slice(n * 8, n * 8 + 8)
                colsum_ref[to, at] = colsum_ref[to, at] + value if k in begun else value
            begun.add(k)
        rowsum_ref[i * BLOCK : (i + 1) * BLOCK, :] = partial

    if last:
        place = place_in_cube()
        sums = before + [(rowsum_ref, colsum_ref)]

        def put(n, number, row):
            at = (place ^ number) * PER + n * HALF
            for h in range(PER):
                for g in range(CUBE):
                    stats_ref[g, pl.ds(at + h, 1), :] = row[:, h * 128 : (h + 1) * 128]

        @pl.when(role_of() == 0)
        def _():
            for number in ALL:
                total = None
                for (these, _, _), (ref, _) in zip(PARTS, sums):
                    if number in these:
                        at = these.index(number) * BLOCK
                        piece = ref[at : at + BLOCK, :]
                        total = piece if total is None else total + piece
                put(0, number, jnp.sum(jnp.transpose(total), axis=0, keepdims=True))
                put(1, number, jnp.zeros((1, BLOCK), F32))

        @pl.when(role_of() == 1)
        def _():
            for number in ALL:
                for n in range(2):
                    total = None
                    for (_, these, _), (_, ref) in zip(PARTS, sums):
                        if number in these:
                            at = these.index(number) * BLOCK
                            piece = ref[n * 8 : n * 8 + 8, at : at + BLOCK]
                            total = piece if total is None else total + piece
                    put(n, number, jnp.sum(total, axis=0, keepdims=True))


def encode(out_ref, value, digits):
    largest = None
    for h in range(WIDTH // 128):
        piece = jnp.abs(value[:, h * 128 : (h + 1) * 128])
        largest = piece if largest is None else jnp.maximum(largest, piece)
    largest = jnp.max(largest, axis=1, keepdims=True)
    power = jnp.ceil(jnp.log2(jnp.maximum(largest, 1e-30)) * 128.0)
    steps = value * (FULL * jnp.exp2(power * (-1.0 / 128.0)))
    out_ref[:BLOCK, :] = jnp.floor(steps + 0.5).astype(jnp.int32).astype(jnp.int16)
    at = lax.broadcasted_iota(jnp.int32, (PAD, BLOCK), 0)
    lane = lax.broadcasted_iota(jnp.int32, (PAD, BLOCK), 1)
    power = jnp.transpose(jnp.broadcast_to(power, (BLOCK, 128)))[:PAD, :]
    tail = jnp.where(at == 0, power, 0.0)
    for n, digit in enumerate(digits):
        tail = jnp.where((at == 1) & (lane == n), digit, tail)
    out_ref[BLOCK:, :] = jnp.zeros((PAD, WIDTH), jnp.int16)
    out_ref[BLOCK:, :BLOCK] = tail.astype(jnp.int32).astype(jnp.int16)


def decode(ref):
    tail = ref[BLOCK:, :BLOCK].astype(jnp.int32).astype(F32)
    scale = down_rows(jnp.exp2(tail[0:1, :] * (1.0 / 128.0)) * (1.0 / FULL), WIDTH)
    return ref[:BLOCK, :].astype(jnp.int32).astype(F32) * scale


def decode_half(ref, half):
    tail = ref[ROWS:, half * ROWS : (half + 1) * ROWS].astype(jnp.int32).astype(F32)
    scale = down_rows(jnp.exp2(tail[0:1, :] * (1.0 / 128.0)) * (1.0 / FULL), WIDTH)
    return ref[:ROWS, :].astype(jnp.int32).astype(F32) * scale


def digits_of(loss):
    high = jnp.floor(loss * (1.0 / 16.0))
    rest = (loss - high * 16.0) * 1024.0
    middle = jnp.floor(rest)
    low = jnp.floor((rest - middle) * 16384.0)
    return high, middle, low


def loss_of(ref, rows=BLOCK):
    tail = ref[rows:, :BLOCK].astype(jnp.int32).astype(F32)[1:2, :]
    lane = lax.broadcasted_iota(jnp.int32, (1, BLOCK), 1)
    unit = jnp.where(lane == 0, 16.0, jnp.where(lane == 1, 1.0 / 1024.0, 1.0 / (1024.0 * 16384.0)))
    return jnp.sum(jnp.where(lane < 3, tail * unit, 0.0))


def scale_kernel(stats_ref, out_ref):
    total = jnp.sum(stats_ref[:, :HALF, :], axis=0)
    out_ref[:HALF, :] = 1.0 / total
    lse = 20.0 + jnp.log(total)
    picked = 20.0 * jnp.sum(stats_ref[:, HALF:, :], axis=0)
    out_ref[HALF:, :] = jnp.full((8, 128), jnp.sum(lse - picked), F32)


def grad_kernel(number, coded, *refs):
    exps, refs = refs[: len(PARTS)], refs[len(PARTS) :]
    y, refs = refs[: len(PACKS)], refs[len(PACKS) :]
    scale_ref, x_ref, come, out_ref = refs[0], refs[1], refs[2:-1], refs[-1]
    place = place_in_cube()
    role = role_of()
    loss = scale_ref[HALF, 0]
    _, where = packs_of(ALL)

    def scale_of(block):
        at = (place ^ block) * PER
        return jnp.concatenate([scale_ref[pl.ds(at + h, 1), :] for h in range(PER)], axis=1)

    ids = down_rows(row_ids(x_ref), BLOCK)
    down = down_rows(jnp.where(role == 0, scale_of(number), 1.0), BLOCK)
    acc = None
    for column, (p, start) in zip(ALL, where):
        (e,) = [
            ref[
                rows.index(number) * BLOCK : (rows.index(number) + 1) * BLOCK,
                columns.index(column) * BLOCK : (columns.index(column) + 1) * BLOCK,
            ]
            for part, ((rows, columns, _), ref) in enumerate(zip(PARTS, exps))
            if has(part, number, column)
        ]
        along = jnp.where(role == 1, scale_of(column), 1.0)
        hit = jnp.where(ids == row_ids(y[p], start), 1.0, 0.0)
        weights = (e * down * along - hit).astype(BF16)
        piece = jnp.dot(weights, y[p][start : start + BLOCK, :], preferred_element_type=F32)
        acc = piece if acc is None else acc + piece
    value = 20.0 * acc
    for ref in come:
        value = value + decode(ref)
        loss = loss + loss_of(ref)
    if coded:
        encode(out_ref, value, digits_of(loss))
    else:
        out_ref[:BLOCK, :] = value
        out_ref[BLOCK:, :] = jnp.full((LOSS, WIDTH), loss, F32)


def halves_kernel(number, *refs):
    *given, same_ref, cross_ref, full_ref = refs
    grad_kernel(number, True, *given, full_ref)
    low, high, tail = slice(0, ROWS), slice(ROWS, BLOCK), slice(BLOCK, SPAN)
    same_ref[ROWS:, :] = full_ref[tail, :]
    cross_ref[ROWS:, :] = full_ref[tail, :]
    role = role_of()

    @pl.when(role == 0)
    def _():
        same_ref[:ROWS, :] = full_ref[low, :]
        cross_ref[:ROWS, :] = full_ref[high, :]

    @pl.when(role == 1)
    def _():
        same_ref[:ROWS, :] = full_ref[high, :]
        cross_ref[:ROWS, :] = full_ref[low, :]


def split_kernel(q_ref, d_ref, own_ref, *refs):
    *refs, qn_ref, qr_ref, dn_ref, dr_ref = refs
    for raw, unit_ref, over_ref in ((q_ref, qn_ref, qr_ref), (d_ref, dn_ref, dr_ref)):
        unit, length = unit_rows(raw[...])
        unit_ref[...] = unit
        over_ref[...] = jnp.broadcast_to(1.0 / length, (ROWS, 128))
    count = len(PIECES) + 1
    come, keep_ref, send_refs = refs[:-count], refs[-count], refs[1 - count :]
    value, loss = own_ref[:BLOCK, :], own_ref[BLOCK, 0]
    for ref in come:
        value = value + decode(ref)
        loss = loss + loss_of(ref)
    role = role_of()
    keep_ref[ROWS:, :] = jnp.full((LOSS, WIDTH), loss, F32)
    send_refs[-1][PIECES[-1] - LOSS :, :] = jnp.full((LOSS, WIDTH), loss, F32)

    def give(half):
        start = 0
        for rows, ref in zip(PIECES, send_refs):
            stop = min(start + rows, ROWS)
            ref[: stop - start, :] = half[start:stop, :]
            start = stop

    @pl.when(role == 0)
    def _():
        keep_ref[:ROWS, :] = value[:ROWS, :]
        give(value[ROWS:, :])

    @pl.when(role == 1)
    def _():
        keep_ref[:ROWS, :] = value[ROWS:, :]
        give(value[:ROWS, :])


def post_kernel(qn_ref, qr_ref, dn_ref, dr_ref, keep_ref, same_ref, cross_ref, *refs):
    *come, loss_ref, gq_ref, gd_ref = refs
    come_ref = jnp.concatenate([ref[...] for ref in come], axis=0)

    def project(out_ref, grad, unit_ref, over_ref):
        unit = unit_ref[...]
        over = jnp.concatenate([over_ref[...]] * (WIDTH // 128), axis=1)
        out_ref[...] = (grad - jnp.sum(grad * unit, axis=1, keepdims=True) * unit) * over

    def fill(gq, last_q, gd, last_d, half):
        project(gq_ref, gq[:ROWS, :] + decode_half(last_q, half), qn_ref, qr_ref)
        project(gd_ref, gd[:ROWS, :] + decode_half(last_d, half), dn_ref, dr_ref)
        loss_ref[...] = (gd[ROWS : ROWS + 1, 0:1] + loss_of(last_d, ROWS)) * (1.0 / 16384)

    role = role_of()

    @pl.when(role == 0)
    def _():
        fill(keep_ref, same_ref, come_ref, cross_ref, 0)

    @pl.when(role == 1)
    def _():
        fill(come_ref, cross_ref, keep_ref, same_ref, 1)


def local(queries, documents, positives):
    piece = pltpu.VMEM((ROWS + PAD, WIDTH), BF16)
    raw = [queries, documents, positives.reshape(1, ROWS)]
    keep, give = pl.pallas_call(
        pre_kernel,
        name="pre",
        in_specs=[pl.BlockSpec(memory_space=pltpu.HBM)] * 3,
        out_shape=[piece, piece],
        scratch_shapes=[
            pltpu.VMEM((ROWS, WIDTH), BF16),
            pltpu.VMEM((ROWS, WIDTH), BF16),
            pltpu.VMEM((1, ROWS), jnp.int32),
            pltpu.SemaphoreType.DMA((3,)),
        ],
        compiler_params=pltpu.CompilerParams(vmem_limit_bytes=8 * 1024 * 1024),
    )(*[pltpu.with_memory_space_constraint(v, pltpu.HBM) for v in raw])
    come = swap(give)
    own = call(join_kernel, "join", pltpu.VMEM((SPAN, WIDTH), BF16), near(keep), near(come))

    def pack(blocks, name, after=()):
        shape = pltpu.VMEM((len(blocks) * SPAN, WIDTH), BF16)
        return call(pack_kernel, name, shape, *[near(x[n]) for n in blocks], after=after)

    x = {0: own}
    for bits in (4, 2, 1):
        x[bits] = send(own, bits)
    x[5] = send(x[4], 1)
    x[6] = send(x[2], 4)
    x[3] = send(x[1], 2)
    x[7] = send(x[1], 6)
    y = [swap(pack(NEAR, "pack_near"))]
    parts = []

    def tile(part, name, after=()):
        rows, columns, _ = PARTS[part]
        used, _ = packs_of(columns)
        last = part == len(PARTS) - 1
        e = pltpu.VMEM((len(rows) * BLOCK, len(columns) * BLOCK), F32)
        sums = [pltpu.VMEM((len(rows) * BLOCK, 128), F32), pltpu.VMEM((16, len(columns) * BLOCK), F32)]
        before = [near(v) for done in parts for v in done[1:]] if last else []
        parts.append(
            call(
                functools.partial(tile_kernel, part),
                name,
                [e, pltpu.VMEM((CUBE, 2 * HALF, 128), F32)] if last else [e, *sums],
                *[near(x[n]) for n in rows],
                *[near(y[PACKS.index(pack)]) for pack in used],
                *before,
                scratch=sums if last else [],
                after=after,
            )
        )

    tile(0, "tile_0", [])
    y.append(swap(pack(FAR[:2], "pack_first", after=[parts[0][1]])))
    tile(1, "tile_1", [parts[0][1]])
    tile(2, "tile_2", [parts[1][1]])
    y.append(swap(pack(FAR[2:], "pack_second", after=[parts[1][1]])))
    tile(3, "tile_3", [parts[2][1]])
    tile(4, "tile_4")
    stats = lax.all_to_all(parts[-1][1], "dp", 0, 0, axis_index_groups=SUM_GROUPS, tiled=True)
    scales = call(scale_kernel, "scales", pltpu.VMEM((HALF + 8, 128), F32), near(stats))

    coded = pltpu.VMEM((SPAN, WIDTH), jnp.int16)
    half = pltpu.VMEM((ROWS + PAD, WIDTH), jnp.int16)
    plain = pltpu.VMEM((BLOCK + LOSS, WIDTH), F32)

    def grad(number, *come, after=(), shape=coded):
        halves = shape is half
        return call(
            functools.partial(halves_kernel, number)
            if halves
            else functools.partial(grad_kernel, number, shape is coded),
            f"grad_{number}",
            [half, half] if halves else shape,
            *[near(v[0]) for v in parts],
            *[near(v) for v in y],
            near(scales),
            near(x[number]),
            *[near(v) for v in come],
            scratch=[coded] if halves else [],
            after=after,
        )

    g3 = grad(3)
    r3 = send(g3, 2)
    g6 = grad(6)
    r6 = send(g6, 4)
    g5 = grad(5)
    r5 = send(g5, 1)
    g7 = grad(7, after=[g5])
    r7 = send(g7, 7)
    g1 = grad(1, r3)
    r1 = send(g1, 1)
    g2 = grad(2, r6)
    r2 = send(g2, 2)
    halves = grad(4, r5, shape=half)
    cross = lax.ppermute(halves[1], "dp", crossing(4))
    same = send(halves[0], 4)
    g0 = grad(0, after=[halves[0]], shape=plain)
    part = pltpu.VMEM((ROWS + LOSS, WIDTH), F32)
    pieces = [pltpu.VMEM((rows, WIDTH), F32) for rows in PIECES]
    unit, over = pltpu.VMEM((ROWS, WIDTH), F32), pltpu.VMEM((ROWS, 128), F32)
    keep, *give, qn, qr, dn, dr = call(
        split_kernel,
        "split",
        [part, *pieces, unit, over, unit, over],
        *[near(v) for v in (queries, documents, g0, r7, r1, r2)],
    )
    come = [swap(v) for v in give]
    loss, gq, gd = call(
        post_kernel,
        "post",
        [
            jax.ShapeDtypeStruct((1, 1), F32),
            jax.ShapeDtypeStruct((ROWS, WIDTH), F32),
            jax.ShapeDtypeStruct((ROWS, WIDTH), F32),
        ],
        *[near(v) for v in (qn, qr, dn, dr, keep, same, cross, *come)],
    )
    return (loss.reshape(()), gq, gd)


def solution(mesh):
    placed = (P("dp", None), P("dp", None), P("dp"))
    return jax.shard_map(
        local,
        mesh=mesh,
        in_specs=placed,
        out_specs=(P(), P("dp", None), P("dp", None)),
        check_vma=False,
    )
```

```python
import functools

import jax
import jax.numpy as jnp
from jax import lax
from jax.experimental import pallas as pl
from jax.experimental.pallas import tpu as pltpu
from jax.sharding import PartitionSpec as P

PAIRS_A = ((0, 1), (2, 3))
PAIRS_B = ((0, 3), (1, 2))
CUBE = 8
CORES = 2
ROWS = 128
BLOCK = CORES * ROWS
SIDE = CUBE * BLOCK
WIDTH = 768
PAD = 16
PIECES = (48, 48, 40)
LOSS = 8
PER = BLOCK // 128
HALF = CUBE * PER
LOG2E = 1.4426950408889634
FULL = 32760.0
NEAR = (0, 4, 2, 1)
FAR = (7, 5, 3, 6)
PACKS = (NEAR, FAR[:2], FAR[2:])
ALL = NEAR + FAR
PARTS = (
    (NEAR, NEAR, ()),
    (FAR[:2], NEAR, ()),
    (NEAR + FAR[:2], FAR[:2], ()),
    (FAR[2:], NEAR + FAR[:2], ()),
    (ALL, FAR[2:], ()),
)
SPAN = BLOCK + PAD
F32 = jnp.float32
BF16 = jnp.bfloat16


def device_index(x, z, y, core):
    return ((x * 4 + z) * 4 + y) * CORES + core


def partners(bits):
    moves = []
    for x in range(4):
        for z in range(4):
            for y in range(4):
                for core in range(CORES):
                    flip = (lambda v: v ^ 1) if core == 0 else (lambda v: 3 - v)
                    to = [flip(v) if bits & bit else v for v, bit in ((x, 4), (z, 2), (y, 1))]
                    moves.append((device_index(x, z, y, core), device_index(*to, core)))
    return moves


def crossing(bits):
    return [(source, target ^ 1) for source, target in partners(bits)]


def a_cubes():
    return [
        [device_index(x, z, y, core) for x in px for z in pz for y in py]
        for core in range(CORES)
        for px in PAIRS_A
        for pz in PAIRS_A
        for py in PAIRS_A
    ]


SWAP = [(i, i ^ 1) for i in range(128)]
SUM_GROUPS = a_cubes()


def send(value, bits):
    return lax.ppermute(value, "dp", partners(bits))


def swap(value):
    return lax.ppermute(value, "dp", SWAP)


def near(value):
    return pltpu.with_memory_space_constraint(value, pltpu.VMEM)


def call(kernel, name, out_shape, *args, scratch=(), after=()):
    n = len(args)

    def body(*refs):
        kernel(*refs[:n], *refs[n + len(after) :])

    return pl.pallas_call(
        body,
        name=name,
        out_shape=out_shape,
        scratch_shapes=scratch,
        compiler_params=pltpu.CompilerParams(vmem_limit_bytes=8 * 1024 * 1024),
    )(*args, *[near(v) for v in after])


def role_of():
    return lax.axis_index("dp") & 1


def unit_rows(values):
    wide = values.astype(F32)
    length = jnp.sqrt(jnp.sum(wide * wide, axis=1, keepdims=True) + 1e-06)
    return wide / length, length


def row_ids(ref, at=0):
    tail = ref[at + BLOCK : at + SPAN, :BLOCK].astype(F32)
    return tail[0:1, :] * 128.0 + tail[1:2, :]


def down_rows(row, width):
    wide = jnp.transpose(jnp.broadcast_to(row, (128, row.shape[1])))
    return jnp.concatenate([wide] * (width // 128), axis=1)


def pre_kernel(q_hbm, d_hbm, p_hbm, keep_ref, send_ref, q_ref, d_ref, p_ref, sems):
    copies = [
        pltpu.make_async_copy(src, dst, sems.at[n])
        for n, (src, dst) in enumerate(((q_hbm, q_ref), (d_hbm, d_ref), (p_hbm, p_ref)))
    ]
    for copy in copies:
        copy.start()
    me = lax.axis_index("dp")
    role = role_of()
    for copy in copies:
        copy.wait()

    def fill(ref, values, ids):
        ref[:ROWS, :] = unit_rows(values)[0].astype(BF16)
        high = ids >> 7
        rows = lax.broadcasted_iota(jnp.int32, (PAD, ROWS), 0)
        tail = jnp.where(rows == 0, high, jnp.where(rows == 1, ids - high * 128, 0))
        ref[ROWS:, :] = jnp.zeros((PAD, WIDTH), BF16)
        ref[ROWS:, :ROWS] = tail.astype(F32).astype(BF16)

    mine = me * ROWS + lax.broadcasted_iota(jnp.int32, (1, ROWS), 1)

    @pl.when(role == 0)
    def _():
        fill(keep_ref, q_ref[...], p_ref[...])
        fill(send_ref, d_ref[...], mine)

    @pl.when(role == 1)
    def _():
        fill(keep_ref, d_ref[...], mine)
        fill(send_ref, q_ref[...], p_ref[...])


def join_kernel(keep_ref, come_ref, own_ref):
    def fill(low, high):
        own_ref[:ROWS, :] = low[:ROWS, :]
        own_ref[ROWS:BLOCK, :] = high[:ROWS, :]
        own_ref[BLOCK:, :] = jnp.zeros((PAD, WIDTH), BF16)
        own_ref[BLOCK:, :ROWS] = low[ROWS:, :ROWS]
        own_ref[BLOCK:, ROWS:BLOCK] = high[ROWS:, :ROWS]

    role = role_of()

    @pl.when(role == 0)
    def _():
        fill(keep_ref, come_ref)

    @pl.when(role == 1)
    def _():
        fill(come_ref, keep_ref)


def place_in_cube():
    me = lax.axis_index("dp")
    return ((me >> 5) & 1) * 4 + ((me >> 3) & 1) * 2 + ((me >> 1) & 1)


def pack_kernel(*refs):
    for n, ref in enumerate(refs[:-1]):
        refs[-1][n * SPAN : (n + 1) * SPAN, :] = ref[...]


def packs_of(columns):
    used = [pack for pack in PACKS if set(pack) & set(columns)]
    return used, [
        (p, pack.index(number) * SPAN) for number in columns for p, pack in enumerate(used) if number in pack
    ]


def has(part, row, column):
    rows, columns, known = PARTS[part]
    return row in rows and column in columns and not (row in known and column in known)


def tile_kernel(part, *refs):
    rows, columns, _ = PARTS[part]
    last = part == len(PARTS) - 1
    used, where = packs_of(columns)
    x, refs = refs[: len(rows)], refs[len(rows) :]
    y, refs = refs[: len(used)], refs[len(used) :]
    if last:
        before, (e_ref, stats_ref, rowsum_ref, colsum_ref) = refs[: 2 * part], refs[2 * part :]
        before = [(before[2 * n], before[2 * n + 1]) for n in range(part)]
    else:
        e_ref, rowsum_ref, colsum_ref = refs
    ids_of_columns = [row_ids(y[p], at) for p, at in where]
    begun = set()
    for i, number in enumerate(rows):
        ids = down_rows(row_ids(x[i]), BLOCK)
        partial = None
        for k, (p, start) in enumerate(where):
            if not has(part, number, columns[k]):
                continue
            dots = lax.dot_general(
                x[i][:BLOCK, :],
                y[p][start : start + BLOCK, :],
                (((1,), (1,)), ((), ())),
                preferred_element_type=F32,
            )
            e = jnp.exp2(dots * (20.0 * LOG2E) - 20.0 * LOG2E)
            at = slice(k * BLOCK, (k + 1) * BLOCK)
            e_ref[i * BLOCK : (i + 1) * BLOCK, at] = e
            for h in range(PER):
                piece = e[:, h * 128 : (h + 1) * 128]
                partial = piece if partial is None else partial + piece
            hit = jnp.where(ids == ids_of_columns[k], dots, 0.0)
            for n, value in enumerate((e, hit)):
                value = jnp.sum(value.reshape(BLOCK // 8, 8, BLOCK), axis=0)
                to = slice(n * 8, n * 8 + 8)
                colsum_ref[to, at] = colsum_ref[to, at] + value if k in begun else value
            begun.add(k)
        rowsum_ref[i * BLOCK : (i + 1) * BLOCK, :] = partial

    if last:
        place = place_in_cube()
        sums = before + [(rowsum_ref, colsum_ref)]

        def put(n, number, row):
            at = (place ^ number) * PER + n * HALF
            for h in range(PER):
                for g in range(CUBE):
                    stats_ref[g, pl.ds(at + h, 1), :] = row[:, h * 128 : (h + 1) * 128]

        @pl.when(role_of() == 0)
        def _():
            for number in ALL:
                total = None
                for (these, _, _), (ref, _) in zip(PARTS, sums):
                    if number in these:
                        at = these.index(number) * BLOCK
                        piece = ref[at : at + BLOCK, :]
                        total = piece if total is None else total + piece
                put(0, number, jnp.sum(jnp.transpose(total), axis=0, keepdims=True))
                put(1, number, jnp.zeros((1, BLOCK), F32))

        @pl.when(role_of() == 1)
        def _():
            for number in ALL:
                for n in range(2):
                    total = None
                    for (_, these, _), (_, ref) in zip(PARTS, sums):
                        if number in these:
                            at = these.index(number) * BLOCK
                            piece = ref[n * 8 : n * 8 + 8, at : at + BLOCK]
                            total = piece if total is None else total + piece
                    put(n, number, jnp.sum(total, axis=0, keepdims=True))


def encode(out_ref, value, digits):
    largest = None
    for h in range(WIDTH // 128):
        piece = jnp.abs(value[:, h * 128 : (h + 1) * 128])
        largest = piece if largest is None else jnp.maximum(largest, piece)
    largest = jnp.max(largest, axis=1, keepdims=True)
    power = jnp.ceil(jnp.log2(jnp.maximum(largest, 1e-30)) * 128.0)
    steps = value * (FULL * jnp.exp2(power * (-1.0 / 128.0)))
    out_ref[:BLOCK, :] = jnp.floor(steps + 0.5).astype(jnp.int32).astype(jnp.int16)
    at = lax.broadcasted_iota(jnp.int32, (PAD, BLOCK), 0)
    lane = lax.broadcasted_iota(jnp.int32, (PAD, BLOCK), 1)
    power = jnp.transpose(jnp.broadcast_to(power, (BLOCK, 128)))[:PAD, :]
    tail = jnp.where(at == 0, power, 0.0)
    for n, digit in enumerate(digits):
        tail = jnp.where((at == 1) & (lane == n), digit, tail)
    out_ref[BLOCK:, :] = jnp.zeros((PAD, WIDTH), jnp.int16)
    out_ref[BLOCK:, :BLOCK] = tail.astype(jnp.int32).astype(jnp.int16)


def decode(ref):
    tail = ref[BLOCK:, :BLOCK].astype(jnp.int32).astype(F32)
    scale = down_rows(jnp.exp2(tail[0:1, :] * (1.0 / 128.0)) * (1.0 / FULL), WIDTH)
    return ref[:BLOCK, :].astype(jnp.int32).astype(F32) * scale


def decode_half(ref, half):
    tail = ref[ROWS:, half * ROWS : (half + 1) * ROWS].astype(jnp.int32).astype(F32)
    scale = down_rows(jnp.exp2(tail[0:1, :] * (1.0 / 128.0)) * (1.0 / FULL), WIDTH)
    return ref[:ROWS, :].astype(jnp.int32).astype(F32) * scale


def digits_of(loss):
    high = jnp.floor(loss * (1.0 / 16.0))
    rest = (loss - high * 16.0) * 1024.0
    middle = jnp.floor(rest)
    low = jnp.floor((rest - middle) * 16384.0)
    return high, middle, low


def loss_of(ref, rows=BLOCK):
    tail = ref[rows:, :BLOCK].astype(jnp.int32).astype(F32)[1:2, :]
    lane = lax.broadcasted_iota(jnp.int32, (1, BLOCK), 1)
    unit = jnp.where(lane == 0, 16.0, jnp.where(lane == 1, 1.0 / 1024.0, 1.0 / (1024.0 * 16384.0)))
    return jnp.sum(jnp.where(lane < 3, tail * unit, 0.0))


def scale_kernel(stats_ref, out_ref):
    total = jnp.sum(stats_ref[:, :HALF, :], axis=0)
    out_ref[:HALF, :] = 1.0 / total
    lse = 20.0 + jnp.log(total)
    picked = 20.0 * jnp.sum(stats_ref[:, HALF:, :], axis=0)
    out_ref[HALF:, :] = jnp.full((8, 128), jnp.sum(lse - picked), F32)


def grad_kernel(number, coded, *refs):
    exps, refs = refs[: len(PARTS)], refs[len(PARTS) :]
    y, refs = refs[: len(PACKS)], refs[len(PACKS) :]
    scale_ref, x_ref, come, out_ref = refs[0], refs[1], refs[2:-1], refs[-1]
    place = place_in_cube()
    role = role_of()
    loss = scale_ref[HALF, 0]
    _, where = packs_of(ALL)

    def scale_of(block):
        at = (place ^ block) * PER
        return jnp.concatenate([scale_ref[pl.ds(at + h, 1), :] for h in range(PER)], axis=1)

    ids = down_rows(row_ids(x_ref), BLOCK)
    down = down_rows(jnp.where(role == 0, scale_of(number), 1.0), BLOCK)
    acc = None
    for column, (p, start) in zip(ALL, where):
        (e,) = [
            ref[
                rows.index(number) * BLOCK : (rows.index(number) + 1) * BLOCK,
                columns.index(column) * BLOCK : (columns.index(column) + 1) * BLOCK,
            ]
            for part, ((rows, columns, _), ref) in enumerate(zip(PARTS, exps))
            if has(part, number, column)
        ]
        along = jnp.where(role == 1, scale_of(column), 1.0)
        hit = jnp.where(ids == row_ids(y[p], start), 1.0, 0.0)
        weights = (e * down * along - hit).astype(BF16)
        piece = jnp.dot(weights, y[p][start : start + BLOCK, :], preferred_element_type=F32)
        acc = piece if acc is None else acc + piece
    value = 20.0 * acc
    for ref in come:
        value = value + decode(ref)
        loss = loss + loss_of(ref)
    if coded:
        encode(out_ref, value, digits_of(loss))
    else:
        out_ref[:BLOCK, :] = value
        out_ref[BLOCK:, :] = jnp.full((LOSS, WIDTH), loss, F32)


def halves_kernel(number, *refs):
    *given, same_ref, cross_ref, full_ref = refs
    grad_kernel(number, True, *given, full_ref)
    low, high, tail = slice(0, ROWS), slice(ROWS, BLOCK), slice(BLOCK, SPAN)
    same_ref[ROWS:, :] = full_ref[tail, :]
    cross_ref[ROWS:, :] = full_ref[tail, :]
    role = role_of()

    @pl.when(role == 0)
    def _():
        same_ref[:ROWS, :] = full_ref[low, :]
        cross_ref[:ROWS, :] = full_ref[high, :]

    @pl.when(role == 1)
    def _():
        same_ref[:ROWS, :] = full_ref[high, :]
        cross_ref[:ROWS, :] = full_ref[low, :]


def split_kernel(q_ref, d_ref, own_ref, *refs):
    *refs, qn_ref, qr_ref, dn_ref, dr_ref = refs
    for raw, unit_ref, over_ref in ((q_ref, qn_ref, qr_ref), (d_ref, dn_ref, dr_ref)):
        unit, length = unit_rows(raw[...])
        unit_ref[...] = unit
        over_ref[...] = jnp.broadcast_to(1.0 / length, (ROWS, 128))
    count = len(PIECES) + 1
    come, keep_ref, send_refs = refs[:-count], refs[-count], refs[1 - count :]
    value, loss = own_ref[:BLOCK, :], own_ref[BLOCK, 0]
    for ref in come:
        value = value + decode(ref)
        loss = loss + loss_of(ref)
    role = role_of()
    keep_ref[ROWS:, :] = jnp.full((LOSS, WIDTH), loss, F32)
    send_refs[-1][PIECES[-1] - LOSS :, :] = jnp.full((LOSS, WIDTH), loss, F32)

    def give(half):
        start = 0
        for rows, ref in zip(PIECES, send_refs):
            stop = min(start + rows, ROWS)
            ref[: stop - start, :] = half[start:stop, :]
            start = stop

    @pl.when(role == 0)
    def _():
        keep_ref[:ROWS, :] = value[:ROWS, :]
        give(value[ROWS:, :])

    @pl.when(role == 1)
    def _():
        keep_ref[:ROWS, :] = value[ROWS:, :]
        give(value[:ROWS, :])


def post_kernel(qn_ref, qr_ref, dn_ref, dr_ref, keep_ref, same_ref, cross_ref, *refs):
    *come, loss_ref, gq_hbm, gd_hbm, gq_ref, gd_ref, sems = refs
    out_q = pltpu.make_async_copy(gq_ref, gq_hbm, sems.at[0])
    out_d = pltpu.make_async_copy(gd_ref, gd_hbm, sems.at[1])
    come_ref = jnp.concatenate([ref[...] for ref in come], axis=0)

    def project(out_ref, grad, unit_ref, over_ref):
        unit = unit_ref[...]
        over = jnp.concatenate([over_ref[...]] * (WIDTH // 128), axis=1)
        out_ref[...] = (grad - jnp.sum(grad * unit, axis=1, keepdims=True) * unit) * over

    def fill(gq, last_q, gd, last_d, half):
        project(gq_ref, gq[:ROWS, :] + decode_half(last_q, half), qn_ref, qr_ref)
        out_q.start()
        project(gd_ref, gd[:ROWS, :] + decode_half(last_d, half), dn_ref, dr_ref)
        out_d.start()
        loss_ref[...] = (gd[ROWS : ROWS + 1, 0:1] + loss_of(last_d, ROWS)) * (1.0 / 16384)

    role = role_of()

    @pl.when(role == 0)
    def _():
        fill(keep_ref, same_ref, come_ref, cross_ref, 0)

    @pl.when(role == 1)
    def _():
        fill(come_ref, cross_ref, keep_ref, same_ref, 1)

    out_q.wait()
    out_d.wait()


def local(queries, documents, positives):
    piece = pltpu.VMEM((ROWS + PAD, WIDTH), BF16)
    raw = [queries, documents, positives.reshape(1, ROWS)]
    keep, give = pl.pallas_call(
        pre_kernel,
        name="pre",
        in_specs=[pl.BlockSpec(memory_space=pltpu.HBM)] * 3,
        out_shape=[piece, piece],
        scratch_shapes=[
            pltpu.VMEM((ROWS, WIDTH), BF16),
            pltpu.VMEM((ROWS, WIDTH), BF16),
            pltpu.VMEM((1, ROWS), jnp.int32),
            pltpu.SemaphoreType.DMA((3,)),
        ],
        compiler_params=pltpu.CompilerParams(vmem_limit_bytes=8 * 1024 * 1024),
    )(*[pltpu.with_memory_space_constraint(v, pltpu.HBM) for v in raw])
    come = swap(give)
    own = call(join_kernel, "join", pltpu.VMEM((SPAN, WIDTH), BF16), near(keep), near(come))

    def pack(blocks, name, after=()):
        shape = pltpu.VMEM((len(blocks) * SPAN, WIDTH), BF16)
        return call(pack_kernel, name, shape, *[near(x[n]) for n in blocks], after=after)

    x = {0: own}
    for bits in (4, 2, 1):
        x[bits] = send(own, bits)
    x[5] = send(x[4], 1)
    x[6] = send(x[2], 4)
    x[3] = send(x[1], 2)
    x[7] = send(x[1], 6)
    y = [swap(pack(NEAR, "pack_near"))]
    parts = []

    def tile(part, name, after=()):
        rows, columns, _ = PARTS[part]
        used, _ = packs_of(columns)
        last = part == len(PARTS) - 1
        e = pltpu.VMEM((len(rows) * BLOCK, len(columns) * BLOCK), F32)
        sums = [pltpu.VMEM((len(rows) * BLOCK, 128), F32), pltpu.VMEM((16, len(columns) * BLOCK), F32)]
        before = [near(v) for done in parts for v in done[1:]] if last else []
        parts.append(
            call(
                functools.partial(tile_kernel, part),
                name,
                [e, pltpu.VMEM((CUBE, 2 * HALF, 128), F32)] if last else [e, *sums],
                *[near(x[n]) for n in rows],
                *[near(y[PACKS.index(pack)]) for pack in used],
                *before,
                scratch=sums if last else [],
                after=after,
            )
        )

    tile(0, "tile_0", [])
    y.append(swap(pack(FAR[:2], "pack_first", after=[parts[0][1]])))
    tile(1, "tile_1", [parts[0][1]])
    tile(2, "tile_2", [parts[1][1]])
    y.append(swap(pack(FAR[2:], "pack_second", after=[parts[1][1]])))
    tile(3, "tile_3", [parts[2][1]])
    tile(4, "tile_4")
    stats = lax.all_to_all(parts[-1][1], "dp", 0, 0, axis_index_groups=SUM_GROUPS, tiled=True)
    scales = call(scale_kernel, "scales", pltpu.VMEM((HALF + 8, 128), F32), near(stats))

    coded = pltpu.VMEM((SPAN, WIDTH), jnp.int16)
    half = pltpu.VMEM((ROWS + PAD, WIDTH), jnp.int16)
    plain = pltpu.VMEM((BLOCK + LOSS, WIDTH), F32)

    def grad(number, *come, after=(), shape=coded):
        halves = shape is half
        return call(
            functools.partial(halves_kernel, number)
            if halves
            else functools.partial(grad_kernel, number, shape is coded),
            f"grad_{number}",
            [half, half] if halves else shape,
            *[near(v[0]) for v in parts],
            *[near(v) for v in y],
            near(scales),
            near(x[number]),
            *[near(v) for v in come],
            scratch=[coded] if halves else [],
            after=after,
        )

    g3 = grad(3)
    r3 = send(g3, 2)
    g6 = grad(6)
    r6 = send(g6, 4)
    g5 = grad(5)
    r5 = send(g5, 1)
    g7 = grad(7, after=[g5])
    r7 = send(g7, 7)
    g1 = grad(1, r3)
    r1 = send(g1, 1)
    g2 = grad(2, r6)
    r2 = send(g2, 2)
    halves = grad(4, r5, shape=half)
    cross = lax.ppermute(halves[1], "dp", crossing(4))
    same = send(halves[0], 4)
    g0 = grad(0, after=[halves[0]], shape=plain)
    part = pltpu.VMEM((ROWS + LOSS, WIDTH), F32)
    pieces = [pltpu.VMEM((rows, WIDTH), F32) for rows in PIECES]
    unit, over = pltpu.VMEM((ROWS, WIDTH), F32), pltpu.VMEM((ROWS, 128), F32)
    keep, *give, qn, qr, dn, dr = call(
        split_kernel,
        "split",
        [part, *pieces, unit, over, unit, over],
        *[near(v) for v in (queries, documents, g0, r7, r1, r2)],
    )
    come = [swap(v) for v in give]
    grad_shape = jax.ShapeDtypeStruct((ROWS, WIDTH), F32)
    loss, gq, gd = pl.pallas_call(
        post_kernel,
        name="post",
        out_specs=[pl.BlockSpec(), pl.BlockSpec(memory_space=pltpu.HBM), pl.BlockSpec(memory_space=pltpu.HBM)],
        out_shape=[jax.ShapeDtypeStruct((1, 1), F32), grad_shape, grad_shape],
        scratch_shapes=[
            pltpu.VMEM((ROWS, WIDTH), F32),
            pltpu.VMEM((ROWS, WIDTH), F32),
            pltpu.SemaphoreType.DMA((2,)),
        ],
        compiler_params=pltpu.CompilerParams(vmem_limit_bytes=8 * 1024 * 1024),
    )(*[near(v) for v in (qn, qr, dn, dr, keep, same, cross, *come)])
    return (loss.reshape(()), gq, gd)


def solution(mesh):
    placed = (P("dp", None), P("dp", None), P("dp"))
    return jax.shard_map(
        local,
        mesh=mesh,
        in_specs=placed,
        out_specs=(P(), P("dp", None), P("dp", None)),
        check_vma=False,
    )
```

```python
import functools

import jax
import jax.numpy as jnp
from jax import lax
from jax.experimental import pallas as pl
from jax.experimental.pallas import tpu as pltpu
from jax.sharding import PartitionSpec as P

PAIRS_A = ((0, 1), (2, 3))
PAIRS_B = ((0, 3), (1, 2))
CUBE = 8
CORES = 2
ROWS = 128
BLOCK = CORES * ROWS
SIDE = CUBE * BLOCK
WIDTH = 768
PAD = 16
PIECES = (48, 48, 40)
LOSS = 8
PER = BLOCK // 128
HALF = CUBE * PER
LOG2E = 1.4426950408889634
FULL = 32760.0
NEAR = (0, 4, 2, 1)
FAR = (7, 5, 6, 3)
PACKS = (NEAR, FAR[:2], FAR[2:])
ALL = NEAR + FAR
PARTS = (
    (NEAR, NEAR, ()),
    (FAR[:2], NEAR, ()),
    (NEAR + FAR[:2], FAR[:2], ()),
    (FAR[2:], NEAR + FAR[:2], ()),
    (ALL, FAR[2:], ()),
)
SPAN = BLOCK + PAD
F32 = jnp.float32
BF16 = jnp.bfloat16


def device_index(x, z, y, core):
    return ((x * 4 + z) * 4 + y) * CORES + core


def partners(bits):
    moves = []
    for x in range(4):
        for z in range(4):
            for y in range(4):
                for core in range(CORES):
                    flip = (lambda v: v ^ 1) if core == 0 else (lambda v: 3 - v)
                    to = [flip(v) if bits & bit else v for v, bit in ((x, 4), (z, 2), (y, 1))]
                    moves.append((device_index(x, z, y, core), device_index(*to, core)))
    return moves


def crossing(bits):
    return [(source, target ^ 1) for source, target in partners(bits)]


def a_cubes():
    return [
        [device_index(x, z, y, core) for x in px for z in pz for y in py]
        for core in range(CORES)
        for px in PAIRS_A
        for pz in PAIRS_A
        for py in PAIRS_A
    ]


SWAP = [(i, i ^ 1) for i in range(128)]
SUM_GROUPS = a_cubes()


def send(value, bits):
    return lax.ppermute(value, "dp", partners(bits))


def swap(value):
    return lax.ppermute(value, "dp", SWAP)


def near(value):
    return pltpu.with_memory_space_constraint(value, pltpu.VMEM)


def call(kernel, name, out_shape, *args, scratch=(), after=()):
    n = len(args)

    def body(*refs):
        kernel(*refs[:n], *refs[n + len(after) :])

    return pl.pallas_call(
        body,
        name=name,
        out_shape=out_shape,
        scratch_shapes=scratch,
        compiler_params=pltpu.CompilerParams(vmem_limit_bytes=8 * 1024 * 1024),
    )(*args, *[near(v) for v in after])


def role_of():
    return lax.axis_index("dp") & 1


def unit_rows(values):
    wide = values.astype(F32)
    length = jnp.sqrt(jnp.sum(wide * wide, axis=1, keepdims=True) + 1e-06)
    return wide / length, length


def row_ids(ref, at=0):
    tail = ref[at + BLOCK : at + SPAN, :BLOCK].astype(F32)
    return tail[0:1, :] * 128.0 + tail[1:2, :]


def down_rows(row, width):
    wide = jnp.transpose(jnp.broadcast_to(row, (128, row.shape[1])))
    return jnp.concatenate([wide] * (width // 128), axis=1)


def pre_kernel(q_hbm, d_hbm, p_hbm, keep_ref, send_ref, q_ref, d_ref, p_ref, sems):
    copies = [
        pltpu.make_async_copy(src, dst, sems.at[n])
        for n, (src, dst) in enumerate(((q_hbm, q_ref), (d_hbm, d_ref), (p_hbm, p_ref)))
    ]
    for copy in copies:
        copy.start()
    me = lax.axis_index("dp")
    role = role_of()
    for copy in copies:
        copy.wait()

    def fill(ref, values, ids):
        ref[:ROWS, :] = unit_rows(values)[0].astype(BF16)
        high = ids >> 7
        rows = lax.broadcasted_iota(jnp.int32, (PAD, ROWS), 0)
        tail = jnp.where(rows == 0, high, jnp.where(rows == 1, ids - high * 128, 0))
        ref[ROWS:, :] = jnp.zeros((PAD, WIDTH), BF16)
        ref[ROWS:, :ROWS] = tail.astype(F32).astype(BF16)

    mine = me * ROWS + lax.broadcasted_iota(jnp.int32, (1, ROWS), 1)

    @pl.when(role == 0)
    def _():
        fill(keep_ref, q_ref[...], p_ref[...])
        fill(send_ref, d_ref[...], mine)

    @pl.when(role == 1)
    def _():
        fill(keep_ref, d_ref[...], mine)
        fill(send_ref, q_ref[...], p_ref[...])


def join_kernel(keep_ref, come_ref, own_ref):
    def fill(low, high):
        own_ref[:ROWS, :] = low[:ROWS, :]
        own_ref[ROWS:BLOCK, :] = high[:ROWS, :]
        own_ref[BLOCK:, :] = jnp.zeros((PAD, WIDTH), BF16)
        own_ref[BLOCK:, :ROWS] = low[ROWS:, :ROWS]
        own_ref[BLOCK:, ROWS:BLOCK] = high[ROWS:, :ROWS]

    role = role_of()

    @pl.when(role == 0)
    def _():
        fill(keep_ref, come_ref)

    @pl.when(role == 1)
    def _():
        fill(come_ref, keep_ref)


def place_in_cube():
    me = lax.axis_index("dp")
    return ((me >> 5) & 1) * 4 + ((me >> 3) & 1) * 2 + ((me >> 1) & 1)


def pack_kernel(*refs):
    for n, ref in enumerate(refs[:-1]):
        refs[-1][n * SPAN : (n + 1) * SPAN, :] = ref[...]


def packs_of(columns):
    used = [pack for pack in PACKS if set(pack) & set(columns)]
    return used, [
        (p, pack.index(number) * SPAN) for number in columns for p, pack in enumerate(used) if number in pack
    ]


def has(part, row, column):
    rows, columns, known = PARTS[part]
    return row in rows and column in columns and not (row in known and column in known)


def tile_kernel(part, *refs):
    rows, columns, _ = PARTS[part]
    last = part == len(PARTS) - 1
    used, where = packs_of(columns)
    x, refs = refs[: len(rows)], refs[len(rows) :]
    y, refs = refs[: len(used)], refs[len(used) :]
    if last:
        before, (e_ref, stats_ref, rowsum_ref, colsum_ref) = refs[: 2 * part], refs[2 * part :]
        before = [(before[2 * n], before[2 * n + 1]) for n in range(part)]
    else:
        e_ref, rowsum_ref, colsum_ref = refs
    ids_of_columns = [row_ids(y[p], at) for p, at in where]
    begun = set()
    for i, number in enumerate(rows):
        ids = down_rows(row_ids(x[i]), BLOCK)
        partial = None
        for k, (p, start) in enumerate(where):
            if not has(part, number, columns[k]):
                continue
            dots = lax.dot_general(
                x[i][:BLOCK, :],
                y[p][start : start + BLOCK, :],
                (((1,), (1,)), ((), ())),
                preferred_element_type=F32,
            )
            e = jnp.exp2(dots * (20.0 * LOG2E) - 20.0 * LOG2E)
            at = slice(k * BLOCK, (k + 1) * BLOCK)
            e_ref[i * BLOCK : (i + 1) * BLOCK, at] = e
            for h in range(PER):
                piece = e[:, h * 128 : (h + 1) * 128]
                partial = piece if partial is None else partial + piece
            hit = jnp.where(ids == ids_of_columns[k], dots, 0.0)
            for n, value in enumerate((e, hit)):
                value = jnp.sum(value.reshape(BLOCK // 8, 8, BLOCK), axis=0)
                to = slice(n * 8, n * 8 + 8)
                colsum_ref[to, at] = colsum_ref[to, at] + value if k in begun else value
            begun.add(k)
        rowsum_ref[i * BLOCK : (i + 1) * BLOCK, :] = partial

    if last:
        place = place_in_cube()
        sums = before + [(rowsum_ref, colsum_ref)]

        def put(n, number, row):
            at = (place ^ number) * PER + n * HALF
            for h in range(PER):
                for g in range(CUBE):
                    stats_ref[g, pl.ds(at + h, 1), :] = row[:, h * 128 : (h + 1) * 128]

        @pl.when(role_of() == 0)
        def _():
            for number in ALL:
                total = None
                for (these, _, _), (ref, _) in zip(PARTS, sums):
                    if number in these:
                        at = these.index(number) * BLOCK
                        piece = ref[at : at + BLOCK, :]
                        total = piece if total is None else total + piece
                put(0, number, jnp.sum(jnp.transpose(total), axis=0, keepdims=True))
                put(1, number, jnp.zeros((1, BLOCK), F32))

        @pl.when(role_of() == 1)
        def _():
            for number in ALL:
                for n in range(2):
                    total = None
                    for (_, these, _), (_, ref) in zip(PARTS, sums):
                        if number in these:
                            at = these.index(number) * BLOCK
                            piece = ref[n * 8 : n * 8 + 8, at : at + BLOCK]
                            total = piece if total is None else total + piece
                    put(n, number, jnp.sum(total, axis=0, keepdims=True))


def encode(out_ref, value, digits):
    largest = None
    for h in range(WIDTH // 128):
        piece = jnp.abs(value[:, h * 128 : (h + 1) * 128])
        largest = piece if largest is None else jnp.maximum(largest, piece)
    largest = jnp.max(largest, axis=1, keepdims=True)
    power = jnp.ceil(jnp.log2(jnp.maximum(largest, 1e-30)) * 128.0)
    steps = value * (FULL * jnp.exp2(power * (-1.0 / 128.0)))
    out_ref[:BLOCK, :] = jnp.floor(steps + 0.5).astype(jnp.int32).astype(jnp.int16)
    at = lax.broadcasted_iota(jnp.int32, (PAD, BLOCK), 0)
    lane = lax.broadcasted_iota(jnp.int32, (PAD, BLOCK), 1)
    power = jnp.transpose(jnp.broadcast_to(power, (BLOCK, 128)))[:PAD, :]
    tail = jnp.where(at == 0, power, 0.0)
    for n, digit in enumerate(digits):
        tail = jnp.where((at == 1) & (lane == n), digit, tail)
    out_ref[BLOCK:, :] = jnp.zeros((PAD, WIDTH), jnp.int16)
    out_ref[BLOCK:, :BLOCK] = tail.astype(jnp.int32).astype(jnp.int16)


def decode(ref):
    tail = ref[BLOCK:, :BLOCK].astype(jnp.int32).astype(F32)
    scale = down_rows(jnp.exp2(tail[0:1, :] * (1.0 / 128.0)) * (1.0 / FULL), WIDTH)
    return ref[:BLOCK, :].astype(jnp.int32).astype(F32) * scale


def decode_half(ref, half):
    tail = ref[ROWS:, half * ROWS : (half + 1) * ROWS].astype(jnp.int32).astype(F32)
    scale = down_rows(jnp.exp2(tail[0:1, :] * (1.0 / 128.0)) * (1.0 / FULL), WIDTH)
    return ref[:ROWS, :].astype(jnp.int32).astype(F32) * scale


def digits_of(loss):
    high = jnp.floor(loss * (1.0 / 16.0))
    rest = (loss - high * 16.0) * 1024.0
    middle = jnp.floor(rest)
    low = jnp.floor((rest - middle) * 16384.0)
    return high, middle, low


def loss_of(ref, rows=BLOCK):
    tail = ref[rows:, :BLOCK].astype(jnp.int32).astype(F32)[1:2, :]
    lane = lax.broadcasted_iota(jnp.int32, (1, BLOCK), 1)
    unit = jnp.where(lane == 0, 16.0, jnp.where(lane == 1, 1.0 / 1024.0, 1.0 / (1024.0 * 16384.0)))
    return jnp.sum(jnp.where(lane < 3, tail * unit, 0.0))


def scale_kernel(stats_ref, out_ref):
    total = jnp.sum(stats_ref[:, :HALF, :], axis=0)
    out_ref[:HALF, :] = 1.0 / total
    lse = 20.0 + jnp.log(total)
    picked = 20.0 * jnp.sum(stats_ref[:, HALF:, :], axis=0)
    out_ref[HALF:, :] = jnp.full((8, 128), jnp.sum(lse - picked), F32)


def grad_kernel(number, coded, *refs):
    exps, refs = refs[: len(PARTS)], refs[len(PARTS) :]
    y, refs = refs[: len(PACKS)], refs[len(PACKS) :]
    scale_ref, x_ref, come, out_ref = refs[0], refs[1], refs[2:-1], refs[-1]
    place = place_in_cube()
    role = role_of()
    loss = scale_ref[HALF, 0]
    _, where = packs_of(ALL)

    def scale_of(block):
        at = (place ^ block) * PER
        return jnp.concatenate([scale_ref[pl.ds(at + h, 1), :] for h in range(PER)], axis=1)

    ids = down_rows(row_ids(x_ref), BLOCK)
    down = down_rows(jnp.where(role == 0, scale_of(number), 1.0), BLOCK)
    acc = None
    for column, (p, start) in zip(ALL, where):
        (e,) = [
            ref[
                rows.index(number) * BLOCK : (rows.index(number) + 1) * BLOCK,
                columns.index(column) * BLOCK : (columns.index(column) + 1) * BLOCK,
            ]
            for part, ((rows, columns, _), ref) in enumerate(zip(PARTS, exps))
            if has(part, number, column)
        ]
        along = jnp.where(role == 1, scale_of(column), 1.0)
        hit = jnp.where(ids == row_ids(y[p], start), 1.0, 0.0)
        weights = (e * down * along - hit).astype(BF16)
        piece = jnp.dot(weights, y[p][start : start + BLOCK, :], preferred_element_type=F32)
        acc = piece if acc is None else acc + piece
    value = 20.0 * acc
    for ref in come:
        value = value + decode(ref)
        loss = loss + loss_of(ref)
    if coded:
        encode(out_ref, value, digits_of(loss))
    else:
        out_ref[:BLOCK, :] = value
        out_ref[BLOCK:, :] = jnp.full((LOSS, WIDTH), loss, F32)


def halves_kernel(number, *refs):
    *given, same_ref, cross_ref, full_ref = refs
    grad_kernel(number, True, *given, full_ref)
    low, high, tail = slice(0, ROWS), slice(ROWS, BLOCK), slice(BLOCK, SPAN)
    same_ref[ROWS:, :] = full_ref[tail, :]
    cross_ref[ROWS:, :] = full_ref[tail, :]
    role = role_of()

    @pl.when(role == 0)
    def _():
        same_ref[:ROWS, :] = full_ref[low, :]
        cross_ref[:ROWS, :] = full_ref[high, :]

    @pl.when(role == 1)
    def _():
        same_ref[:ROWS, :] = full_ref[high, :]
        cross_ref[:ROWS, :] = full_ref[low, :]


def split_kernel(q_ref, d_ref, own_ref, *refs):
    *refs, qn_ref, qr_ref, dn_ref, dr_ref = refs
    for raw, unit_ref, over_ref in ((q_ref, qn_ref, qr_ref), (d_ref, dn_ref, dr_ref)):
        unit, length = unit_rows(raw[...])
        unit_ref[...] = unit
        over_ref[...] = jnp.broadcast_to(1.0 / length, (ROWS, 128))
    count = len(PIECES) + 1
    come, keep_ref, send_refs = refs[:-count], refs[-count], refs[1 - count :]
    value, loss = own_ref[:BLOCK, :], own_ref[BLOCK, 0]
    for ref in come:
        value = value + decode(ref)
        loss = loss + loss_of(ref)
    role = role_of()
    keep_ref[ROWS:, :] = jnp.full((LOSS, WIDTH), loss, F32)
    send_refs[-1][PIECES[-1] - LOSS :, :] = jnp.full((LOSS, WIDTH), loss, F32)

    def give(half):
        start = 0
        for rows, ref in zip(PIECES, send_refs):
            stop = min(start + rows, ROWS)
            ref[: stop - start, :] = half[start:stop, :]
            start = stop

    @pl.when(role == 0)
    def _():
        keep_ref[:ROWS, :] = value[:ROWS, :]
        give(value[ROWS:, :])

    @pl.when(role == 1)
    def _():
        keep_ref[:ROWS, :] = value[ROWS:, :]
        give(value[:ROWS, :])


def post_kernel(qn_ref, qr_ref, dn_ref, dr_ref, keep_ref, same_ref, cross_ref, *refs):
    *come, loss_ref, gq_ref, gd_ref = refs
    come_ref = jnp.concatenate([ref[...] for ref in come], axis=0)

    def project(out_ref, grad, unit_ref, over_ref):
        unit = unit_ref[...]
        over = jnp.concatenate([over_ref[...]] * (WIDTH // 128), axis=1)
        out_ref[...] = (grad - jnp.sum(grad * unit, axis=1, keepdims=True) * unit) * over

    def fill(gq, last_q, gd, last_d, half):
        project(gq_ref, gq[:ROWS, :] + decode_half(last_q, half), qn_ref, qr_ref)
        project(gd_ref, gd[:ROWS, :] + decode_half(last_d, half), dn_ref, dr_ref)
        loss_ref[...] = (gd[ROWS : ROWS + 1, 0:1] + loss_of(last_d, ROWS)) * (1.0 / 16384)

    role = role_of()

    @pl.when(role == 0)
    def _():
        fill(keep_ref, same_ref, come_ref, cross_ref, 0)

    @pl.when(role == 1)
    def _():
        fill(come_ref, cross_ref, keep_ref, same_ref, 1)


def local(queries, documents, positives):
    piece = pltpu.VMEM((ROWS + PAD, WIDTH), BF16)
    raw = [queries, documents, positives.reshape(1, ROWS)]
    keep, give = pl.pallas_call(
        pre_kernel,
        name="pre",
        in_specs=[pl.BlockSpec(memory_space=pltpu.HBM)] * 3,
        out_shape=[piece, piece],
        scratch_shapes=[
            pltpu.VMEM((ROWS, WIDTH), BF16),
            pltpu.VMEM((ROWS, WIDTH), BF16),
            pltpu.VMEM((1, ROWS), jnp.int32),
            pltpu.SemaphoreType.DMA((3,)),
        ],
        compiler_params=pltpu.CompilerParams(vmem_limit_bytes=8 * 1024 * 1024),
    )(*[pltpu.with_memory_space_constraint(v, pltpu.HBM) for v in raw])
    come = swap(give)
    own = call(join_kernel, "join", pltpu.VMEM((SPAN, WIDTH), BF16), near(keep), near(come))

    def pack(blocks, name, after=()):
        shape = pltpu.VMEM((len(blocks) * SPAN, WIDTH), BF16)
        return call(pack_kernel, name, shape, *[near(x[n]) for n in blocks], after=after)

    x = {0: own}
    for bits in (4, 2, 1):
        x[bits] = send(own, bits)
    x[5] = send(x[4], 1)
    x[6] = send(x[2], 4)
    x[3] = send(x[1], 2)
    x[7] = send(x[1], 6)
    y = [swap(pack(NEAR, "pack_near"))]
    parts = []

    def tile(part, name, after=()):
        rows, columns, _ = PARTS[part]
        used, _ = packs_of(columns)
        last = part == len(PARTS) - 1
        e = pltpu.VMEM((len(rows) * BLOCK, len(columns) * BLOCK), F32)
        sums = [pltpu.VMEM((len(rows) * BLOCK, 128), F32), pltpu.VMEM((16, len(columns) * BLOCK), F32)]
        before = [near(v) for done in parts for v in done[1:]] if last else []
        parts.append(
            call(
                functools.partial(tile_kernel, part),
                name,
                [e, pltpu.VMEM((CUBE, 2 * HALF, 128), F32)] if last else [e, *sums],
                *[near(x[n]) for n in rows],
                *[near(y[PACKS.index(pack)]) for pack in used],
                *before,
                scratch=sums if last else [],
                after=after,
            )
        )

    tile(0, "tile_0", [])
    y.append(swap(pack(FAR[:2], "pack_first", after=[parts[0][1]])))
    tile(1, "tile_1", [parts[0][1]])
    tile(2, "tile_2", [parts[1][1]])
    y.append(swap(pack(FAR[2:], "pack_second", after=[parts[1][1]])))
    tile(3, "tile_3", [parts[2][1]])
    tile(4, "tile_4")
    stats = lax.all_to_all(parts[-1][1], "dp", 0, 0, axis_index_groups=SUM_GROUPS, tiled=True)
    scales = call(scale_kernel, "scales", pltpu.VMEM((HALF + 8, 128), F32), near(stats))

    coded = pltpu.VMEM((SPAN, WIDTH), jnp.int16)
    half = pltpu.VMEM((ROWS + PAD, WIDTH), jnp.int16)
    plain = pltpu.VMEM((BLOCK + LOSS, WIDTH), F32)

    def grad(number, *come, after=(), shape=coded):
        halves = shape is half
        return call(
            functools.partial(halves_kernel, number)
            if halves
            else functools.partial(grad_kernel, number, shape is coded),
            f"grad_{number}",
            [half, half] if halves else shape,
            *[near(v[0]) for v in parts],
            *[near(v) for v in y],
            near(scales),
            near(x[number]),
            *[near(v) for v in come],
            scratch=[coded] if halves else [],
            after=after,
        )

    g3 = grad(3)
    r3 = send(g3, 2)
    g6 = grad(6)
    r6 = send(g6, 4)
    g5 = grad(5)
    r5 = send(g5, 1)
    g7 = grad(7, after=[g5])
    r7 = send(g7, 7)
    g1 = grad(1, r3)
    r1 = send(g1, 1)
    g2 = grad(2, r6)
    r2 = send(g2, 2)
    halves = grad(4, r5, shape=half)
    cross = lax.ppermute(halves[1], "dp", crossing(4))
    same = send(halves[0], 4)
    g0 = grad(0, after=[halves[0]], shape=plain)
    part = pltpu.VMEM((ROWS + LOSS, WIDTH), F32)
    pieces = [pltpu.VMEM((rows, WIDTH), F32) for rows in PIECES]
    unit, over = pltpu.VMEM((ROWS, WIDTH), F32), pltpu.VMEM((ROWS, 128), F32)
    keep, *give, qn, qr, dn, dr = call(
        split_kernel,
        "split",
        [part, *pieces, unit, over, unit, over],
        *[near(v) for v in (queries, documents, g0, r7, r1, r2)],
    )
    come = [swap(v) for v in give]
    loss, gq, gd = call(
        post_kernel,
        "post",
        [
            jax.ShapeDtypeStruct((1, 1), F32),
            jax.ShapeDtypeStruct((ROWS, WIDTH), F32),
            jax.ShapeDtypeStruct((ROWS, WIDTH), F32),
        ],
        *[near(v) for v in (qn, qr, dn, dr, keep, same, cross, *come)],
    )
    return (loss.reshape(()), gq, gd)


def solution(mesh):
    placed = (P("dp", None), P("dp", None), P("dp"))
    return jax.shard_map(
        local,
        mesh=mesh,
        in_specs=placed,
        out_specs=(P(), P("dp", None), P("dp", None)),
        check_vma=False,
    )
```
